32 devices in a mesh: dp: 8 (over z, y), mp: 4 (over x, core).
Axes of the slice: x: 2, y: 2, z: 4, core: 2. Of those that a mesh axis runs over, the one named last changes fastest.
Arguments:
- inputs: float32 [25088, 512], P(('dp', 'mp')), may hold values from -6 to 6
- w_qkv: float32 [3, 512, 512], P(None, 'dp', 'mp'), may hold values from -0.25 to 0.25
- qv_bias: float32 [2, 512], replicated, may hold values from -3 to 3
- w_proj: float32 [512, 512], P('mp', 'dp'), may hold values from -2 to 2
- w_fc1: float32 [512, 2048], P('dp', 'mp'), may hold values from -0.25 to 0.25
- fc1_bias: float32 [2048], replicated, may hold values from -3 to 3
- w_fc2: float32 [2048, 512], P('mp', 'dp'), may hold values from -0.125 to 0.125
- norm_gains: float32 [2, 512], replicated, may hold values from 0.1 to 1.9
- token_biases: float32 [4, 512], replicated, may hold values from -3 to 3
- table: float32 [2535, 16], replicated, may hold values from -6 to 6
- shifts: int32 [8, 3], P('dp'), may hold values from 1 to 7, as said below
- rel_index: int32 [392, 392], replicated, may hold values from 0 to 2534, as said below
- cotangent: float32 [25088, 512], P(('dp', 'mp')), may hold values from -6 to 6
Outputs:
- out: float32 [25088, 512], P(('dp', 'mp'))
- grad_x: float32 [25088, 512], P(('dp', 'mp'))
- grad_qkv: float32 [3, 512, 512], P(None, 'dp', 'mp')
- grad_qv_bias: float32 [2, 512], replicated
- grad_proj: float32 [512, 512], P('mp', 'dp')
- grad_fc1: float32 [512, 2048], P('dp', 'mp')
- grad_fc1_bias: float32 [2048], replicated
- grad_fc2: float32 [2048, 512], P('mp', 'dp')
- grad_gains: float32 [2, 512], replicated
- grad_biases: float32 [4, 512], replicated
- grad_table: float32 [2535, 16], replicated
The draws below stay inside these ranges and needn't reach their ends.
Inputs may be any that keep to these rules, and one draw needn't show every extreme that they name: `shifts`: row c holds clip c's cyclic shift along time, height and width, the time shift from 1 to 7, the height shift from 1 to 6, the width shift from 1 to 6. `rel_index`: entry (i, j) is the table row of the offset between places i and j of a window, places taken in time, height, width order; pairs with equal offsets share a row and distinct offsets have distinct rows.
All inputs are finite; a program needn't handle non-finite values.
Results may differ from the reference program's by a relative error of at most 0.015.
Values may be sent and summed in bfloat16 or wider, within the bound.
No kernel may reach another device: no remote copies, remote signals or barrier semaphores. Data moves between devices by JAX's collectives and lax.ppermute only.
A program may use at most 192 MiB of HBM per device.

```python
import jax
import jax.numpy as jnp
from jax import lax

D = 512
HEADS = 16
HD = 32
FF = 2048
WT = 8
WH = 7
WW = 7
GT = 16
GH = 14
GW = 14
WIN = 392
WINS = 8
CLIP_TOK = 3136
REL = 2535
CLIPS = 8
TOKENS = 25088


def draw_shifts(key, part):
    keys = jax.random.split(jax.random.fold_in(key, 11), 3)
    along_t = jax.random.randint(keys[0], (CLIPS, 1), 1, WT)
    along_h = jax.random.randint(keys[1], (CLIPS, 1), 1, WH)
    along_w = jax.random.randint(keys[2], (CLIPS, 1), 1, WW)
    drawn = jnp.concatenate([along_t, along_h, along_w], axis=1).astype(jnp.int32)
    highest = jnp.array([[WT - 1, WH - 1, WW - 1]], jnp.int32)
    row_ids = jnp.arange(CLIPS, dtype=jnp.int32)[:, None]
    drawn = jnp.where(row_ids == CLIPS - 1, jnp.ones_like(drawn), drawn)
    return jnp.where(row_ids == 0, highest, drawn).astype(jnp.int32)


def draw_rel_index(key, part):
    places = jnp.arange(WIN, dtype=jnp.int32)
    along_t = places // (WH * WW)
    along_h = places // WW % WH
    along_w = places % WW
    delta_t = along_t[:, None] - along_t[None, :] + WT - 1
    delta_h = along_h[:, None] - along_h[None, :] + WH - 1
    delta_w = along_w[:, None] - along_w[None, :] + WW - 1
    offsets = (delta_t * (2 * WH - 1) + delta_h) * (2 * WW - 1) + delta_w
    relabel = jax.random.permutation(jax.random.fold_in(key, 23), REL).astype(jnp.int32)
    return jnp.take(relabel, offsets.astype(jnp.int32)).astype(jnp.int32)


def strengthened(entries, key, source, target, parts, factor):
    owner, partner = [(jnp.arange(entries.shape[dim]) // (entries.shape[dim] // parts)).reshape([-1 if axis == dim else 1 for axis in range(entries.ndim)]) for dim in (source, target)]
    chosen = jax.random.permutation(key, parts)[partner]
    strong = (owner == chosen) | (owner == (partner + parts // 2) % parts)
    return jnp.where(strong, factor * entries, entries)


def shard_levels(rng, extent, cuts, least, largest):
    def one(axis_at, blocks):
        draws = jax.random.uniform(jax.random.fold_in(jax.random.fold_in(rng, 6), axis_at), (blocks,), jnp.float32, least / len(cuts), largest / len(cuts))
        return jnp.repeat(jnp.exp(draws), extent[axis_at] // blocks).reshape((-1,) + (1,) * (len(extent) - axis_at - 1))

    level = one(*cuts[0])
    for cut in cuts[1:]:
        level = level * one(*cut)
    return level


def scatter_about(own_key, extent, scale, most, cuts=(), held_as=jnp.bfloat16):
    entries = scale * jax.random.normal(own_key, extent, jnp.float32)
    if cuts:
        entries = entries * shard_levels(own_key, extent, cuts, -0.22, 0.18)
    return jnp.clip(entries, -most, most).astype(held_as)


def gaussian_with(own_key, dims, scale, most, cuts, heavy, kind=jnp.bfloat16):
    values = scale * jax.random.normal(own_key, dims, jnp.float32)
    if cuts:
        values = values * shard_levels(own_key, dims, cuts, -0.22, 0.18)
    return jnp.clip(strengthened(values, jax.random.fold_in(own_key, 3), *heavy), -most, most).astype(kind)


def setup_inputs(seed: int = 0) -> dict:
    splits = jax.random.split(jax.random.key(seed), 14)
    return {
        "inputs": gaussian_with(splits[0], (TOKENS, D), 1.0, 6.0, ((0, 32),), (0, 1, 32, 2.75), jnp.float32),
        "w_qkv": scatter_about(splits[1], (3, D, D), D ** -0.5, 0.25, ((1, 8), (2, 4)), jnp.float32),
        "qv_bias": scatter_about(splits[2], (2, D), 0.5, 3.0, (), jnp.float32),
        "w_proj": scatter_about(splits[3], (D, D), (D // 64) ** -0.5, 2.0, ((0, 4), (1, 8)), jnp.float32),
        "w_fc1": scatter_about(splits[4], (D, FF), D ** -0.5, 0.25, ((0, 8), (1, 4)), jnp.float32),
        "fc1_bias": scatter_about(splits[5], (FF,), 0.5, 3.0, (), jnp.float32),
        "w_fc2": scatter_about(splits[6], (FF, D), FF ** -0.5, 0.125, ((0, 4), (1, 8)), jnp.float32),
        "norm_gains": jnp.clip(1.0 + 0.18 * jax.random.normal(splits[7], (2, D), jnp.float32), 0.1, 1.9),
        "token_biases": scatter_about(splits[8], (4, D), 0.5, 3.0, (), jnp.float32),
        "table": scatter_about(splits[9], (REL, HEADS), 1.0, 6.0, (), jnp.float32),
        "shifts": draw_shifts(jax.random.fold_in(splits[13], 71), 0),
        "rel_index": draw_rel_index(jax.random.fold_in(splits[13], 71), 0),
        "cotangent": gaussian_with(splits[12], (TOKENS, D), 1.0, 6.0, ((0, 32),), (0, 1, 32, 2.75), jnp.float32),
    }


@jax.custom_vjp
def low(v):
    return lax.optimization_barrier(v.astype(jnp.bfloat16)).astype(jnp.float32)

@jax.custom_vjp
def low_back(v):
    return v

def low_keep(v):
    return (low(v), None)

def low_pass(kept, grad):
    return (grad,)

def back_keep(v):
    return (v, None)

def back_low(kept, grad):
    return (low(grad),)
low.defvjp(low_keep, low_pass)
low_back.defvjp(back_keep, back_low)

def matmul(left, right):
    return jnp.dot(left, right, precision=lax.Precision.HIGHEST, preferred_element_type=jnp.float32)

def layer_norm(values, gain, offset):
    average = lax.optimization_barrier(jnp.mean(values, -1, keepdims=True))
    centred = values - average
    spread = lax.optimization_barrier(jnp.mean(centred * centred, -1, keepdims=True))
    return centred * lax.rsqrt(spread + 1e-05) * gain + offset

def window_regions(shift_rows, first_window, count):
    window_ids = first_window + jnp.arange(count, dtype=jnp.int32)
    clip_ids = window_ids // WINS
    within = window_ids % WINS
    shift_take = jnp.take(shift_rows, clip_ids, axis=0)
    places = jnp.arange(WIN, dtype=jnp.int32)
    along_t = (within // 4)[:, None] * WT + (places // (WH * WW))[None, :]
    along_h = (within // 2 % 2)[:, None] * WH + (places // WW % WH)[None, :]
    along_w = (within % 2)[:, None] * WW + (places % WW)[None, :]
    region_t = (along_t >= GT - WT).astype(jnp.int32) + (along_t >= GT - shift_take[:, 0:1]).astype(jnp.int32)
    region_h = (along_h >= GH - WH).astype(jnp.int32) + (along_h >= GH - shift_take[:, 1:2]).astype(jnp.int32)
    region_w = (along_w >= GW - WW).astype(jnp.int32) + (along_w >= GW - shift_take[:, 2:3]).astype(jnp.int32)
    return region_t * 9 + region_h * 3 + region_w

def clip_block(clip_rows, shift_row, w_qkv, qv_bias, w_proj, w_fc1, fc1_bias, w_fc2, norm_gains, token_biases, table, rel_index):
    qkv_low = low(w_qkv)
    proj_low = low(w_proj)
    up_low = low(w_fc1)
    down_low = low(w_fc2)
    first = low(layer_norm(clip_rows, norm_gains[0], token_biases[0]))
    queries = low(low_back(matmul(first, qkv_low[0])) + qv_bias[0])
    keys = low(low_back(matmul(first, qkv_low[1])))
    values = low(low_back(matmul(first, qkv_low[2])) + qv_bias[1])
    regions = window_regions(shift_row[None, :], 0, WINS)
    bias = jnp.take(table, rel_index.reshape(-1), axis=0).reshape(WIN, WIN, HEADS).transpose(2, 0, 1)
    shape4 = (WINS, WIN, HEADS, HD)
    raw = jnp.einsum('wihd,wjhd->whij', queries.reshape(shape4), keys.reshape(shape4), precision=lax.Precision.HIGHEST)
    scores = low_back(raw) * HD ** (-0.5) + bias[None]
    same = regions[:, None, :, None] == regions[:, None, None, :]
    scores = jnp.where(same, scores, -1e+30)
    top = lax.optimization_barrier(jnp.max(scores, -1, keepdims=True))
    expo = jnp.exp(scores - top)
    probs = expo / lax.optimization_barrier(jnp.sum(expo, -1, keepdims=True))
    mixed = jnp.einsum('whij,wjhd->wihd', low(probs), values.reshape(shape4), precision=lax.Precision.HIGHEST)
    mixed = low(low_back(mixed.reshape(CLIP_TOK, D)))
    after_attn = clip_rows + low_back(matmul(mixed, proj_low)) + token_biases[1]
    second = low(layer_norm(after_attn, norm_gains[1], token_biases[2]))
    hidden = low_back(matmul(second, up_low)) + fc1_bias
    active = low(jax.nn.gelu(hidden, approximate=False))
    return after_attn + low_back(matmul(active, down_low)) + token_biases[3]

def reference(inputs, w_qkv, qv_bias, w_proj, w_fc1, fc1_bias, w_fc2, norm_gains, token_biases, table, shifts, rel_index, cotangent):

    def forward(inputs, w_qkv, qv_bias, w_proj, w_fc1, fc1_bias, w_fc2, norm_gains, token_biases, table):

        def one_clip(item):
            return jax.checkpoint(clip_block)(item[0], item[1], w_qkv, qv_bias, w_proj, w_fc1, fc1_bias, w_fc2, norm_gains, token_biases, table, rel_index)
        result = lax.map(one_clip, (inputs.reshape(-1, CLIP_TOK, D), shifts))
        return result.reshape(-1, D)
    out, pull = jax.vjp(forward, inputs, w_qkv, qv_bias, w_proj, w_fc1, fc1_bias, w_fc2, norm_gains, token_biases, table)
    grad_x, grad_qkv, grad_qv_bias, grad_proj, grad_fc1, grad_fc1_bias, grad_fc2, grad_gains, grad_biases, grad_table = pull(cotangent)
    return (out, grad_x, grad_qkv, grad_qv_bias, grad_proj, grad_fc1, grad_fc1_bias, grad_fc2, grad_gains, grad_biases, grad_table)
```

```python
import functools

import jax
import jax.numpy as jnp
from jax import lax
from jax.experimental import pallas as pl
from jax.experimental.pallas import tpu as pltpu
from jax.sharding import PartitionSpec as P

D = 512
HEADS = 16
HD = 32
FF = 2048
WT = 8
WH = 7
WW = 7
GT = 16
GH = 14
GW = 14
WIN = 392
REL = 2535
RELP = 2560
PARTS = 4
GW_COLS = D // PARTS
GHEADS = HEADS // PARTS
LOG2E = 1.4426950408889634
SCALE = HD ** (-0.5)
LOW = jnp.bfloat16
F32 = jnp.float32
NN = (((1,), (0,)), ((), ()))
NT = (((1,), (1,)), ((), ()))
VMEM_BYTES = 56 << 20
ROW_CUTS = ((0, 64), (64, 64), (128, 64), (192, 64), (256, 64), (320, 72))
LANE_CUTS = ((0, 1024), (768, 1920), (1664, 2560))


def product(left, right, dims=NN):
    return lax.dot_general(left, right, dims, preferred_element_type=F32)


def shaped(*dims, kind=F32):
    return jax.ShapeDtypeStruct(dims, kind)


def cost(micros):
    return pl.CostEstimate(flops=int(micros * 1e9), bytes_accessed=int(micros * 3.6e6), transcendentals=0)


def call(kernel, outs, args, micros):
    whole = pl.BlockSpec(memory_space=pltpu.VMEM)
    return pl.pallas_call(
        kernel,
        out_shape=outs,
        in_specs=[whole] * len(args),
        out_specs=[whole] * len(outs),
        cost_estimate=cost(micros),
        compiler_params=pltpu.CompilerParams(vmem_limit_bytes=VMEM_BYTES),
    )(*args)


def normed(values):
    centred = values - jnp.mean(values, -1, keepdims=True)
    rstd = lax.rsqrt(jnp.mean(centred * centred, -1, keepdims=True) + 1e-05)
    return centred * rstd, rstd


def first_norm_kernel(x_ref, gain_ref, off_ref, a1_ref, a1t_ref):
    for w in range(2):
        vhat, _ = normed(x_ref[w])
        a1 = vhat * gain_ref[...] + off_ref[...]
        a1_ref[w] = a1.astype(LOW)
        a1t_ref[w] = a1.T.astype(LOW)


def split3(values):
    high = values.astype(LOW)
    rest = values - high.astype(F32)
    mid = rest.astype(LOW)
    return high, mid, (rest - mid.astype(F32)).astype(LOW)


def rows_from_table_kernel(order_ref, table_ref, out_ref):
    table = jnp.concatenate(split3(table_ref[...]), axis=0)
    rows = lax.broadcasted_iota(jnp.int32, (RELP, 256), 0)
    for block in range(RELP // 256):
        cols = slice(block * 256, block * 256 + 256)
        picked = jnp.where(rows == order_ref[:, cols], 1.0, 0.0).astype(LOW)
        got = product(table, picked)
        out_ref[:, cols] = got[:HEADS] + got[HEADS : 2 * HEADS] + got[2 * HEADS :]


def rows_to_table_kernel(order_ref, rows_ref, out_ref):
    rows = jnp.concatenate(split3(rows_ref[...]), axis=0)
    ids = lax.broadcasted_iota(jnp.int32, (256, RELP), 0)
    for block in range(RELP // 256):
        picked = jnp.where(ids + block * 256 == order_ref[...], 1.0, 0.0).astype(LOW)
        got = product(rows, picked, NT)
        out_ref[:, block * 256 : block * 256 + 256] = got[:HEADS] + got[HEADS : 2 * HEADS] + got[2 * HEADS :]


def compaction(lane_ref, block):
    low, high = LANE_CUTS[block]
    ids = lax.broadcasted_iota(jnp.int32, (high - low, 256), 0) + low
    return jnp.where(ids == lane_ref[:, block * 256 : block * 256 + 256], 1.0, 0.0).astype(LOW)


def expand_kernel(lane_ref, rows_ref, bias_ref, left_s, wide_s, *pick_s):
    head = pl.program_id(0)

    @pl.when(head == 0)
    def _():
        for block in range(3):
            pick_s[block][...] = compaction(lane_ref, block)

    row = jnp.broadcast_to(rows_ref[pl.ds(head, 1), :], (8, RELP)) * LOG2E
    back = 7 - lax.broadcasted_iota(jnp.int32, (8, RELP), 0)
    for bit in range(3):
        row = jnp.where(((back >> bit) & 1) == 1, pltpu.roll(row, RELP - (1 << bit), 1), row)
    for hi in range(WH):
        rolled = pltpu.roll(row, (1 - (6 - hi) * 13) % RELP, 1)
        high = rolled.astype(LOW).astype(F32)
        left_s[8 * hi : 8 * hi + 8, :] = high
        left_s[56 + 8 * hi : 64 + 8 * hi, :] = rolled - high
    left = left_s[...].astype(LOW)
    for block in range(3):
        low, high = LANE_CUTS[block]
        got = product(left[:, low:high], pick_s[block][...])
        wide_s[:, block * 256 : block * 256 + 256] = got[:56] + got[56:]
    for ti in range(WT):
        off = 49 * (7 - ti)
        for hi in range(WH):
            tile = wide_s[8 * hi : 8 * hi + 8, :]
            if off:
                tile = pltpu.roll(tile, 768 - off, 1)
            at = 49 * ti + 7 * hi
            bias_ref[0, at : at + 7, :] = tile[:7, :WIN]


def expand_bias(lane_row, rows):
    return pl.pallas_call(
        expand_kernel,
        grid=(HEADS,),
        out_shape=shaped(HEADS, WIN, WIN),
        in_specs=[
            pl.BlockSpec((1, 768), lambda h: (0, 0)),
            pl.BlockSpec((HEADS, RELP), lambda h: (0, 0)),
        ],
        out_specs=pl.BlockSpec((1, WIN, WIN), lambda h: (h, 0, 0)),
        scratch_shapes=[
            pltpu.VMEM((112, RELP), F32),
            pltpu.VMEM((56, 768), F32),
        ]
        + [pltpu.VMEM((high - low, 256), LOW) for low, high in LANE_CUTS],
        cost_estimate=cost(17),
        compiler_params=pltpu.CompilerParams(vmem_limit_bytes=VMEM_BYTES),
    )(lane_row, rows)


def shrink_kernel(lane_ref, wide_ref, out_ref, *pick_s):
    head = pl.program_id(0)

    @pl.when(head == 0)
    def _():
        for block in range(3):
            low, high = LANE_CUTS[block]
            ids = lax.broadcasted_iota(jnp.int32, (256, high - low), 1) + low
            own = lane_ref[block * 256 : block * 256 + 256, :]
            pick_s[block][...] = jnp.where(ids == own, 1.0, 0.0).astype(LOW)

    used = (lax.broadcasted_iota(jnp.int32, (56, 768), 0) & 7) < 7
    wide = jnp.where(used, wide_ref[0], 0.0)
    high_part = wide.astype(LOW)
    both = jnp.concatenate([high_part.astype(F32), wide - high_part.astype(F32)], axis=0).astype(LOW)
    pieces = []
    for block in range(3):
        got = product(both[:, block * 256 : block * 256 + 256], pick_s[block][...])
        pieces.append(got[:56] + got[56:])
    left = 7 - lax.broadcasted_iota(jnp.int32, (8, RELP), 0)
    total = jnp.zeros((1, RELP), F32)
    for hi in range(WH):
        line = jnp.zeros((8, RELP), F32)
        for block in range(3):
            low, high = LANE_CUTS[block]
            line += jnp.pad(pieces[block][8 * hi : 8 * hi + 8, :], ((0, 0), (low, RELP - high)))
        for bit in range(3):
            line = jnp.where(((left >> bit) & 1) == 1, pltpu.roll(line, 1 << bit, 1), line)
        line = jnp.sum(line, axis=0, keepdims=True)
        total += pltpu.roll(line, ((6 - hi) * 13 - 1) % RELP, 1)
    out_ref[pl.ds(head, 1), :] = total


def shrink_bias(lane_column, wide):
    heads = wide.shape[0]
    return pl.pallas_call(
        shrink_kernel,
        grid=(heads,),
        out_shape=shaped(heads, RELP),
        in_specs=[
            pl.BlockSpec((768, 1), lambda h: (0, 0)),
            pl.BlockSpec((1, 56, 768), lambda h: (h, 0, 0)),
        ],
        out_specs=pl.BlockSpec((heads, RELP), lambda h: (0, 0)),
        scratch_shapes=[pltpu.VMEM((256, high - low), LOW) for low, high in LANE_CUTS],
        cost_estimate=cost(10),
        compiler_params=pltpu.CompilerParams(vmem_limit_bytes=VMEM_BYTES),
    )(lane_column, wide)


def attend_kernel(
    a1_ref, wa_ref, wb_ref, qvb_ref, bias_ref, rf_ref, rft_ref,
    p_ref, qt_ref, k_ref, vt_ref, o_ref, li_ref,
    q_s, ka_s, v_s, s_s, acc_s,
):
    step = pl.program_id(0)
    e = step % GHEADS
    lane = lax.broadcasted_iota(jnp.int32, (WIN, 128), 1) // HD

    def begin(w_ref):
        for w in range(2):
            qkv = product(a1_ref[w], w_ref[...])
            q = (qkv[:, :128] + qvb_ref[0, 0:1, :]) * (SCALE * LOG2E)
            k = qkv[:, 128:256]
            v = qkv[:, 256:384] + qvb_ref[0, 1:2, :]
            q_s[w] = q
            v_s[w] = v
            qt_ref[0, w] = q.T.astype(LOW)
            k_ref[0, w] = k.astype(LOW)
            vt_ref[0, w] = v.T.astype(LOW)
            ka_s[w, 0:128, :] = k.T.astype(LOW)
            ka_s[w, 128:256, :] = rft_ref[w]
            acc_s[w] = jnp.zeros((WIN, 256), F32)

    @pl.when(step == 0)
    def _():
        begin(wa_ref)

    @pl.when(step == GHEADS)
    def _():
        begin(wb_ref)

    mine = lane == e
    for w in range(2):
        q_wide = jnp.concatenate([jnp.where(mine, q_s[w], 0.0).astype(LOW), rf_ref[w]], axis=1)
        s_s[w] = product(q_wide, ka_s[w])
    for w in range(2):
        for start, count in ROW_CUTS:
            rows = slice(start, start + count)
            scores = s_s[w, rows, :] + bias_ref[0, rows, :]
            top = jnp.max(scores, axis=1, keepdims=True)
            p_ref[0, w, rows, :] = jnp.exp2(scores - top).astype(LOW)
    for w in range(2):
        v_wide = jnp.concatenate(
            [jnp.where(mine, v_s[w], 0.0).astype(LOW), jnp.where(mine, 1.0, 0.0).astype(LOW)], axis=1
        )
        acc_s[w] += product(p_ref[0, w], v_wide)

    @pl.when(e == GHEADS - 1)
    def _():
        for w in range(2):
            inverse = 1.0 / acc_s[w, :, 128:256]
            li_ref[0, w] = inverse
            o_ref[0, w] = acc_s[w, :, 0:128] * inverse


def held(*dims):
    return pl.BlockSpec(dims, lambda e: (0,) * len(dims))


def by_group(*dims):
    return pl.BlockSpec((1, *dims), lambda e: (e // GHEADS,) + (0,) * len(dims))


def by_head(*dims):
    return pl.BlockSpec((1, *dims), lambda e: (e,) + (0,) * len(dims))


def attend(first, a1, weights, qvb, bias, rf, rft):
    return pl.pallas_call(
        attend_kernel,
        grid=(2 * GHEADS,),
        out_shape=[
            shaped(2 * GHEADS, 2, WIN, WIN, kind=LOW),
            shaped(2, 2, 128, WIN, kind=LOW),
            shaped(2, 2, WIN, 128, kind=LOW),
            shaped(2, 2, 128, WIN, kind=LOW),
            shaped(2, 2, WIN, 128),
            shaped(2, 2, WIN, 128),
        ],
        in_specs=[
            held(2, WIN, D),
            held(D, 384),
            held(D, 384),
            pl.BlockSpec((1, 2, 128), lambda e: (first + e // GHEADS, 0, 0)),
            pl.BlockSpec((1, WIN, WIN), lambda e: (first * GHEADS + e, 0, 0)),
            held(2, WIN, 128),
            held(2, 128, WIN),
        ],
        out_specs=[
            by_head(2, WIN, WIN),
            by_group(2, 128, WIN),
            by_group(2, WIN, 128),
            by_group(2, 128, WIN),
            by_group(2, WIN, 128),
            by_group(2, WIN, 128),
        ],
        scratch_shapes=[
            pltpu.VMEM((2, WIN, 128), F32),
            pltpu.VMEM((2, 256, WIN), LOW),
            pltpu.VMEM((2, WIN, 128), F32),
            pltpu.VMEM((2, WIN, WIN), F32),
            pltpu.VMEM((2, WIN, 256), F32),
        ],
        cost_estimate=cost(14),
        compiler_params=pltpu.CompilerParams(vmem_limit_bytes=VMEM_BYTES),
    )(a1, *weights, qvb, bias, rf, rft)


def attend_back_kernel(
    do_ref, o_ref, li_ref, p_ref, qt_ref, k_ref, vt_ref, a1t_ref, gp_ref,
    dwa_ref, dwb_ref, wide_ref, low_ref, cs_ref,
    dop_s, dopt_s, nd_s, va_s, dp_s, ds_s, dq_s, dkt_s, dvt_s, db_s,
):
    step = pl.program_id(0)
    e = step % GHEADS
    lane = lax.broadcasted_iota(jnp.int32, (WIN, 128), 1) // HD

    @pl.when(e == 0)
    def _():
        for w in range(2):
            dop = do_ref[0, w].astype(F32) * li_ref[0, w]
            dop_s[w] = dop
            nd_s[w] = -(dop.astype(LOW).astype(F32) * o_ref[0, w])
            va_s[w, 0:128, :] = vt_ref[0, w]
            va_s[w, 128:256, :] = jnp.ones((128, WIN), LOW)
            dopt_s[w] = dop.T.astype(LOW)
            dq_s[w] = jnp.zeros((WIN, 128), F32)

    mine = lane == e
    first = pl.multiple_of(HD * e, HD)
    own = pl.ds(first, HD)
    for w in range(2):
        wide = jnp.concatenate(
            [jnp.where(mine, dop_s[w], 0.0).astype(LOW), jnp.where(mine, nd_s[w], 0.0).astype(LOW)], axis=1
        )
        dp_s[w] = product(wide, va_s[w])
    for w in range(2):
        dvt_s[w, own, :] = product(dopt_s[w, own, :], p_ref[0, w])
    for start, count in ROW_CUTS:
        rows = slice(start, start + count)
        one = p_ref[0, 0, rows, :].astype(F32) * dp_s[0, rows, :]
        two = p_ref[0, 1, rows, :].astype(F32) * dp_s[1, rows, :]
        db_s[rows, 0:WIN] = one + two
        ds_s[0, rows, :] = one.astype(LOW)
        ds_s[1, rows, :] = two.astype(LOW)
    for w in range(2):
        dkt_s[w, own, :] = product(qt_ref[0, w, own, :], ds_s[w])
        k_mine = jnp.where(mine, k_ref[0, w], jnp.zeros((WIN, 128), LOW))
        dq_s[w] += product(ds_s[w], k_mine)
    inside = lax.broadcasted_iota(jnp.int32, (8, 512), 1) < WIN
    for hi in range(WH):
        total = jnp.zeros((8, 768), F32)
        for ti in range(WT):
            at = 49 * ti + 7 * hi
            tile = jnp.where(inside, db_s[at : at + 8, :], 0.0)
            tile = jnp.concatenate([tile, jnp.zeros((8, 256), F32)], axis=1)
            off = 49 * (7 - ti)
            total += pltpu.roll(tile, off, 1) if off else tile
        wide_ref[0, 8 * hi : 8 * hi + 8, :] = total

    def finish(dw_ref):
        sum_q = jnp.zeros((1, 128), F32)
        sum_v = jnp.zeros((1, 128), F32)
        grad = jnp.zeros((D, 384), F32)
        for w in range(2):
            dq = dq_s[w] * SCALE
            dk = (dkt_s[w] * (1.0 / LOG2E)).T
            dv = dvt_s[w].T
            sum_q += jnp.sum(dq, axis=0, keepdims=True)
            sum_v += jnp.sum(dv, axis=0, keepdims=True)
            low = jnp.concatenate([dq, dk, dv], axis=1).astype(LOW)
            low_ref[0, w] = low
            grad += product(a1t_ref[w], low)
        dw_ref[:, 0:384] = grad.astype(LOW)
        dw_ref[:, 384:512] = gp_ref[0]
        cs_ref[0, 0:1, :] = sum_q
        cs_ref[0, 1:2, :] = sum_v

    @pl.when(step == GHEADS - 1)
    def _():
        finish(dwa_ref)

    @pl.when(step == 2 * GHEADS - 1)
    def _():
        finish(dwb_ref)


def attend_back(do, o, li, p, qt, k, vt, a1t, gproj):
    rows = by_group(2, WIN, 128)
    turned = by_group(2, 128, WIN)
    return pl.pallas_call(
        attend_back_kernel,
        grid=(2 * GHEADS,),
        out_shape=[
            shaped(D, 512, kind=LOW),
            shaped(D, 512, kind=LOW),
            shaped(2 * GHEADS, 56, 768),
            shaped(2, 2, WIN, 384, kind=LOW),
            shaped(2, 2, 128),
        ],
        in_specs=[
            rows, rows, rows, by_head(2, WIN, WIN),
            turned, rows, turned, held(2, D, WIN), by_group(D, 128),
        ],
        out_specs=[
            held(D, 512),
            held(D, 512),
            by_head(56, 768),
            by_group(2, WIN, 384),
            by_group(2, 128),
        ],
        scratch_shapes=[
            pltpu.VMEM((2, WIN, 128), F32),
            pltpu.VMEM((2, 128, WIN), LOW),
            pltpu.VMEM((2, WIN, 128), F32),
            pltpu.VMEM((2, 256, WIN), LOW),
            pltpu.VMEM((2, WIN, WIN), F32),
            pltpu.VMEM((2, WIN, WIN), LOW),
            pltpu.VMEM((2, WIN, 128), F32),
            pltpu.VMEM((2, 128, WIN), F32),
            pltpu.VMEM((2, 128, WIN), F32),
            pltpu.VMEM((400, 512), F32),
        ],
        cost_estimate=cost(15),
        compiler_params=pltpu.CompilerParams(vmem_limit_bytes=VMEM_BYTES),
    )(do, o, li, p, qt, k, vt, a1t, gproj)


def gelu_parts(v):
    size = jnp.abs(v)
    t = 1.0 / (1.0 + (0.3275911 * 0.7071067811865476) * size)
    bell = jnp.exp2(v * v * (-0.5 * LOG2E))
    poly = t * (0.127414796 + t * (-0.142248368 + t * (0.7107068705 + t * (-0.7265760135 + t * 0.5307027145))))
    tail = poly * bell
    phi = jnp.where(v >= 0.0, 1.0 - tail, tail)
    return v * phi, phi + v * bell * 0.3989422804014327


def norm_back(values, dy, gain):
    vhat, rstd = normed(values)
    scaled = dy * gain
    dv = rstd * (
        scaled - jnp.mean(scaled, -1, keepdims=True) - vhat * jnp.mean(scaled * vhat, -1, keepdims=True)
    )
    return dv, jnp.sum(dy * vhat, axis=0, keepdims=True), jnp.sum(dy, axis=0, keepdims=True)


ROWS = 2 * WIN


def middle_kernel(
    on_ref, of_ref, x_ref, cot_ref, tb_ref, gain_ref, hb_ref,
    u0, u1, u2, u3, w0, w1, w2, w3,
    out_ref, dafter_ref, dn_ref, df_ref, gpn_ref, gpf_ref, odd_ref, even_ref, sums_ref, ghb_ref,
    up_s, down_s, up_sem, down_sem, after_s, a2_s, a2t_s, g_s, gt_s, mix_s, out_s, da2_s, h_s, d_s, act_s, dh_s,
):
    step = pl.program_id(0)
    r = (2 * step + 1) % 5
    ups = [pltpu.make_async_copy(ref, up_s.at[i], up_sem.at[i]) for i, ref in enumerate((u0, u1, u2, u3))]
    downs = [pltpu.make_async_copy(ref, down_s.at[i], down_sem.at[i]) for i, ref in enumerate((w0, w1, w2, w3))]

    @pl.when(step == 0)
    def _():
        for i in (1, 3, 0, 2):
            ups[i].start()
        for i in (1, 3, 0, 2):
            downs[i].start()
        cot = jnp.concatenate([cot_ref[0], cot_ref[1]], axis=0)
        g_s[...] = cot.astype(LOW)
        gt_s[...] = cot.T.astype(LOW)
        for i in range(PARTS):
            ups[i].wait()
        weight = jnp.concatenate([up_s[i, :, 0:128] for i in range(PARTS)], axis=1)
        lows = []
        for w in range(2):
            mixed = jnp.concatenate([on_ref[0, w], on_ref[1, w], of_ref[0, w], of_ref[1, w]], axis=1).astype(LOW)
            mix_s[w] = mixed
            after = x_ref[w] + product(mixed, weight, NT) + tb_ref[1:2, :]
            after_s[w] = after
            vhat, _ = normed(after)
            lows.append(vhat * gain_ref[1:2, :] + tb_ref[2:3, :])
            out_s[WIN * w : WIN * w + WIN, :] = after + tb_ref[3:4, :]
        a2 = jnp.concatenate(lows, axis=0)
        a2_s[...] = a2.astype(LOW)
        a2t_s[...] = a2.T.astype(LOW)
        da2_s[...] = jnp.zeros((ROWS, D), F32)
        for i in range(PARTS):
            downs[i].wait()

    up = up_s[r, :, 128:640]
    down = down_s[r]
    h_s[...] = product(a2_s[...], up)
    d_s[...] = product(g_s[...], down)
    for cut in range(0, 512, 128):
        cols = slice(cut, cut + 128)
        line = hb_ref[r, :, cols]
        sums = jnp.zeros((1, 128), F32)
        for start in range(0, ROWS, 112):
            rows = slice(start, start + 112)
            act, slope = gelu_parts(h_s[rows, cols] + line)
            act_s[rows, cols] = act.astype(LOW)
            grad = d_s[rows, cols] * slope
            sums += jnp.sum(grad, axis=0, keepdims=True)
            dh_s[rows, cols] = grad.astype(LOW)
        ghb_ref[0, :, cols] = sums
    gup = product(a2t_s[...], dh_s[...]).astype(LOW)
    gdown = product(gt_s[...], act_s[...]).astype(LOW)

    @pl.when(step < 2)
    def _():
        odd_ref[0, :, 0:512] = gup
        odd_ref[0, :, 512:1024] = gdown

    @pl.when(step >= 2)
    def _():
        even_ref[0, :, 0:512] = gup
        even_ref[0, :, 512:1024] = gdown

    out_s[...] += product(act_s[...], down, NT)
    da2_s[...] += product(dh_s[...], up, NT)

    @pl.when(step == PARTS - 1)
    def _():
        weight = jnp.concatenate([up_s[i, :, 0:128] for i in range(PARTS)], axis=1)
        grad = jnp.zeros((D, D), F32)
        sums = [jnp.zeros((1, D), F32) for _ in range(4)]
        for w in range(2):
            own = slice(WIN * w, WIN * w + WIN)
            out_ref[w] = out_s[own, :]
            dv, dgain, doff = norm_back(after_s[w], da2_s[own, :], gain_ref[1:2, :])
            cot = cot_ref[w]
            dafter = cot + dv
            dafter_ref[w] = dafter
            turned = dafter.T.astype(LOW)
            dmix = product(dafter.astype(LOW), weight).astype(LOW)
            for i, (ref, at) in enumerate(((dn_ref, 0), (dn_ref, 1), (df_ref, 0), (df_ref, 1))):
                ref[at, w] = dmix[:, 128 * i : 128 * i + 128]
            grad += product(turned, mix_s[w])
            parts = (dgain, doff, jnp.sum(dafter, axis=0, keepdims=True), jnp.sum(cot, axis=0, keepdims=True))
            for i, part in enumerate(parts):
                sums[i] += part
        for i, (ref, at) in enumerate(((gpn_ref, 0), (gpn_ref, 1), (gpf_ref, 0), (gpf_ref, 1))):
            ref[at] = grad[:, 128 * i : 128 * i + 128].astype(LOW)
        for i in range(4):
            sums_ref[i : i + 1, :] = sums[i]


def middle(o_near, o_far, x, cot, biases, gains, hb, ups, downs):
    anywhere = pl.BlockSpec(memory_space=pl.ANY)
    wide = (1, D, 1024)
    return pl.pallas_call(
        middle_kernel,
        grid=(PARTS,),
        out_shape=[
            shaped(2, WIN, D), shaped(2, WIN, D),
            shaped(2, 2, WIN, 128, kind=LOW), shaped(2, 2, WIN, 128, kind=LOW),
            shaped(2, D, 128, kind=LOW), shaped(2, D, 128, kind=LOW),
            shaped(2, D, 1024, kind=LOW), shaped(2, D, 1024, kind=LOW),
            shaped(4, D), shaped(PARTS, 1, 512),
        ],
        in_specs=[
            held(2, 2, WIN, 128), held(2, 2, WIN, 128), held(2, WIN, D), held(2, WIN, D),
            held(4, D), held(2, D), held(PARTS, 1, 512),
        ]
        + [anywhere] * 8,
        out_specs=[
            held(2, WIN, D), held(2, WIN, D), held(2, 2, WIN, 128), held(2, 2, WIN, 128),
            held(2, D, 128), held(2, D, 128),
            pl.BlockSpec(wide, lambda s: (jnp.minimum(s, 1), 0, 0)),
            pl.BlockSpec(wide, lambda s: (jnp.maximum(s - 2, 0), 0, 0)),
            held(4, D),
            pl.BlockSpec((1, 1, 512), lambda s: ((2 * s + 1) % 5, 0, 0)),
        ],
        scratch_shapes=[
            pltpu.VMEM((PARTS, D, 640), LOW), pltpu.VMEM((PARTS, D, 512), LOW),
            pltpu.SemaphoreType.DMA((PARTS,)), pltpu.SemaphoreType.DMA((PARTS,)),
            pltpu.VMEM((2, WIN, D), F32),
            pltpu.VMEM((ROWS, D), LOW), pltpu.VMEM((D, ROWS), LOW),
            pltpu.VMEM((ROWS, D), LOW), pltpu.VMEM((D, ROWS), LOW),
            pltpu.VMEM((2, WIN, D), LOW),
            pltpu.VMEM((ROWS, D), F32), pltpu.VMEM((ROWS, D), F32),
            pltpu.VMEM((ROWS, 512), F32), pltpu.VMEM((ROWS, 512), F32),
            pltpu.VMEM((ROWS, 512), LOW), pltpu.VMEM((ROWS, 512), LOW),
        ],
        cost_estimate=cost(29),
        compiler_params=pltpu.CompilerParams(vmem_limit_bytes=VMEM_BYTES),
    )(o_near, o_far, x, cot, biases, gains, hb, *ups, *downs)


def last_kernel(
    x_ref, dafter_ref, gain_ref, ln_ref, lf_ref, w0, w1, w2, w3,
    gx_ref, sums_ref,
):
    sums = [jnp.zeros((1, D), F32) for _ in range(2)]
    for w in range(2):
        da1 = jnp.zeros((WIN, D), F32)
        for low, wt in ((ln_ref[0, w], w0), (ln_ref[1, w], w1), (lf_ref[0, w], w2), (lf_ref[1, w], w3)):
            da1 += product(low, wt[...], NT)
        dv, dgain, doff = norm_back(x_ref[w], da1, gain_ref[...])
        gx_ref[w] = dafter_ref[w] + dv
        sums[0] += dgain
        sums[1] += doff
    sums_ref[0:1, :] = sums[0]
    sums_ref[1:2, :] = sums[1]


def swap(values, axis, distance):
    count = lax.axis_size(axis)
    return lax.ppermute(values, axis, [(i, i ^ distance) for i in range(count)])


def bits_of(axis):
    return (lax.axis_size(axis) - 1).bit_length()


def interleaved(own, other, upper):
    return jnp.stack([jnp.where(upper, other, own), jnp.where(upper, own, other)], axis=1).reshape(
        -1, *own.shape[1:]
    )


def upper_of(axis, bit):
    return (lax.axis_index(axis) >> bit) % 2 == 1


def gathered(blocks, bits):
    for bit in bits:
        blocks = interleaved(blocks, swap(blocks, "dp", 1 << bit), upper_of("dp", bit))
    return blocks


def flat(blocks):
    return blocks.reshape(-1, blocks.shape[-1])


def halves(total, bit):
    pairs = total.reshape(-1, 2, *total.shape[1:])
    upper = upper_of("dp", bit)
    send = jnp.where(upper, pairs[:, 0], pairs[:, 1])
    keep = jnp.where(upper, pairs[:, 1], pairs[:, 0])
    return send.astype(LOW), keep.astype(F32)


def scattered(total, bits):
    for bit in bits:
        send, keep = halves(total, bit)
        total = keep + swap(send, "dp", 1 << bit).astype(F32)
    return total


def plus(one, two):
    return one.astype(F32) + two.astype(F32)


def by_distance(values, index):
    pairs = jnp.where(index % 2 == 1, values.reshape(2, 2, *values.shape[1:])[:, ::-1].reshape(values.shape), values)
    swapped = jnp.concatenate([pairs[2:], pairs[:2]], axis=0)
    return jnp.where(index >= 2, swapped, pairs)


def all_sum(values):
    for axis in ("mp", "dp"):
        for bit in range(bits_of(axis)):
            low = values.astype(LOW)
            values = plus(low, swap(low, axis, 1 << bit))
    return values


def window_regions(shift_row, first_window):
    within = first_window + jnp.arange(2, dtype=jnp.int32)
    places = jnp.arange(WIN, dtype=jnp.int32)
    along_t = (within // 4)[:, None] * WT + (places // (WH * WW))[None, :]
    along_h = (within // 2 % 2)[:, None] * WH + (places // WW % WH)[None, :]
    along_w = (within % 2)[:, None] * WW + (places % WW)[None, :]
    region_t = (along_t >= GT - WT).astype(jnp.int32) + (along_t >= GT - shift_row[0]).astype(jnp.int32)
    region_h = (along_h >= GH - WH).astype(jnp.int32) + (along_h >= GH - shift_row[1]).astype(jnp.int32)
    region_w = (along_w >= GW - WW).astype(jnp.int32) + (along_w >= GW - shift_row[2]).astype(jnp.int32)
    return region_t * 9 + region_h * 3 + region_w


def offset_order(rel_index):
    corners = rel_index.reshape(WT, WH, WW, WIN)[::7, ::6, ::6].reshape(2, 2, 2, WT, WH, WW)
    joined = jnp.concatenate([corners[1], corners[0][:, :, 1:]], axis=2)
    joined = jnp.concatenate([joined[1], joined[0][:, :, 1:]], axis=2)
    joined = jnp.concatenate([joined[1], joined[0][:, :, 1:]], axis=2)
    return jnp.pad(joined.reshape(1, REL), ((0, 0), (0, RELP - REL)), constant_values=-1)


def body(
    inputs,
    w_qkv,
    qv_bias,
    w_proj,
    w_fc1,
    fc1_bias,
    w_fc2,
    norm_gains,
    token_biases,
    table,
    shifts,
    rel_index,
    cotangent,
):
    part = lax.axis_index("mp")
    rows = w_qkv.shape[1]
    x = inputs.reshape(2, WIN, D)
    cot = cotangent.reshape(2, WIN, D)
    gain_one, gain_two = norm_gains[0:1], norm_gains[1:2]

    high_bits = tuple(reversed(range(1, bits_of("dp"))))
    low_bits = tuple(range(1, bits_of("dp")))
    shard_qkv = w_qkv.transpose(1, 0, 2).reshape(1, rows, 384).astype(LOW)
    shard_rest = jnp.concatenate([w_proj.T, w_fc1, w_fc2.T], axis=1).astype(LOW)[None]
    own = flat(gathered(shard_qkv, (*high_bits, 0)))
    across = swap(own, "mp", 2)
    qkv_parts = [own, swap(own, "mp", 1), across, swap(across, "mp", 1)]
    rest = gathered(shard_rest, high_bits)
    up_own = gathered(rest[:, :, :640], (0,))
    up_across = swap(up_own, "mp", 2)
    down_pair = jnp.stack([rest[:, :, 640:], swap(rest[:, :, 640:], "mp", 2)], axis=0)
    down_other = swap(down_pair, "dp", 1)
    down_own, down_across = (
        interleaved(down_pair[i], down_other[i], upper_of("dp", 0)) for i in range(2)
    )
    up_parts = [flat(up_own), flat(swap(up_own, "mp", 1)), flat(up_across), flat(swap(up_across, "mp", 1))]
    down_parts = [
        flat(down_own), flat(swap(down_own, "mp", 1)), flat(down_across), flat(swap(down_across, "mp", 1))
    ]

    regions = window_regions(shifts[0], part * 2)
    codes = jnp.arange(128, dtype=jnp.int32)
    rf = jnp.where(regions[:, :, None] == codes[None, None, :], -1e30, 0.0).astype(LOW)
    rft = jnp.where(regions[:, None, :] == codes[None, :, None], 0.0, 1.0).astype(LOW)
    order = offset_order(rel_index)
    column = jnp.arange(768, dtype=jnp.int32)
    lane_row = jnp.where(
        column < 15 * 49, column // 49 * 169 + column % 49 // 7 * 13 + column % 7, -1
    )
    lane_column = lane_row.reshape(768, 1)
    lane_row = lane_row.reshape(1, 768)
    table_rows = by_distance(table.T.reshape(PARTS, GHEADS, REL), part).reshape(HEADS, REL)
    table_rows = jnp.pad(table_rows, ((0, 0), (0, RELP - REL)))
    qvb_parts = by_distance(qv_bias.reshape(2, PARTS, 128).transpose(1, 0, 2), part)
    hb_parts = by_distance(fc1_bias.reshape(PARTS, 1, FF // PARTS), part)

    a1, a1t = call(
        first_norm_kernel,
        [shaped(2, WIN, D, kind=LOW), shaped(2, D, WIN, kind=LOW)],
        [x, gain_one, token_biases[0:1]],
        3,
    )
    (row_offsets,) = call(rows_from_table_kernel, [shaped(HEADS, RELP)], [order, table_rows], 4)
    bias = expand_bias(lane_row, row_offsets)

    near = attend(0, a1, qkv_parts[:2], qvb_parts, bias, rf, rft)
    far = attend(2, a1, qkv_parts[2:], qvb_parts, bias, rf, rft)
    out, dafter, do_near, do_far, gp_near, gp_far, odd, even, sums_two, g_hb = middle(
        near[4], far[4], x, cot, token_biases, norm_gains, hb_parts, up_parts, down_parts
    )

    mlp = plus(even, swap(odd, "mp", 1)).reshape(2, -1, rows, 1024)
    up_sum = plus(mlp[0, :, :, :512], swap(mlp[1, :, :, :512].astype(LOW), "mp", 2))
    up_sum = scattered(up_sum, (0,))
    down_send, down_keep = halves(mlp[:, :, :, 512:].transpose(1, 0, 2, 3), 0)
    down_sum = plus(down_keep, swap(down_send, "dp", 1))
    down_sum = plus(down_sum[:, 0], swap(down_sum[:, 1].astype(LOW), "mp", 2))

    def back(kept, do, gproj):
        p, qt, k, vt, o, li = kept
        return attend_back(do, o, li, p, qt, k, vt, a1t, gproj)

    two, three, wide_far, low_far, col_far = back(far, do_far, gp_far)
    far_sum = plus(two, swap(three, "mp", 1)).astype(LOW)
    far_sum = swap(far_sum, "mp", 2)
    zero, one, wide_near, low_near, col_near = back(near, do_near, gp_near)
    total = plus(plus(zero, swap(one, "mp", 1)), far_sum).reshape(-1, rows, 512)
    own_qkv = scattered(total, (0, *low_bits)).reshape(rows, 512)
    own_mlp = scattered(jnp.concatenate([up_sum, down_sum], axis=2), low_bits).reshape(rows, 1024)
    grad_x, sums_one = call(
        last_kernel,
        [shaped(2, WIN, D), shaped(2, D)],
        [x, dafter, gain_one, low_near, low_far, *qkv_parts],
        7,
    )
    offset_grads = jnp.concatenate(
        [shrink_bias(lane_column, wide_near), shrink_bias(lane_column, wide_far)], axis=0
    )

    hb = by_distance(g_hb, part).reshape(1, FF)
    pair = by_distance(jnp.concatenate([col_near, col_far], axis=0), part).transpose(1, 0, 2).reshape(2, D)
    small = jnp.concatenate(
        [
            sums_one, sums_two, pair, hb.reshape(4, D),
            by_distance(offset_grads.reshape(PARTS, GHEADS, RELP), part).reshape(-1, D),
        ],
        axis=0,
    )
    small = all_sum(small)
    grad_gains = jnp.concatenate([small[0:1], small[2:3]], axis=0)
    grad_biases = jnp.concatenate([small[1:2], small[4:5], small[3:4], small[5:6]], axis=0)
    grad_pair = small[6:8]
    grad_hidden = small[8:12].reshape(FF)
    (grad_table,) = call(
        rows_to_table_kernel, [shaped(HEADS, RELP)], [order, small[12:].reshape(HEADS, RELP)], 6
    )
    return (
        out.reshape(inputs.shape),
        grad_x.reshape(inputs.shape),
        own_qkv[:, :384].reshape(rows, 3, 128).transpose(1, 0, 2),
        grad_pair,
        own_qkv[:, 384:].T,
        own_mlp[:, :512],
        grad_hidden,
        own_mlp[:, 512:].T,
        grad_gains,
        grad_biases,
        grad_table[:, :REL].T,
    )


def solution(mesh):
    placed = (
        P(("dp", "mp"), None),
        P(None, "dp", "mp"),
        P(),
        P("mp", "dp"),
        P("dp", "mp"),
        P(),
        P("mp", "dp"),
        P(),
        P(),
        P(),
        P("dp", None),
        P(),
        P(("dp", "mp"), None),
    )
    return jax.shard_map(
        body,
        mesh=mesh,
        in_specs=placed,
        out_specs=(
            P(("dp", "mp"), None),
            P(("dp", "mp"), None),
            P(None, "dp", "mp"),
            P(),
            P("mp", "dp"),
            P("dp", "mp"),
            P(),
            P("mp", "dp"),
            P(),
            P(),
            P(),
        ),
        check_vma=False,
    )
```

```python
import functools

import jax
import jax.numpy as jnp
from jax import lax
from jax.experimental import pallas as pl
from jax.experimental.pallas import tpu as pltpu
from jax.sharding import PartitionSpec as P

D = 512
HEADS = 16
HD = 32
FF = 2048
WT = 8
WH = 7
WW = 7
GT = 16
GH = 14
GW = 14
WIN = 392
REL = 2535
RELP = 2560
PARTS = 4
GHEADS = HEADS // PARTS
LOG2E = 1.4426950408889634
SCALE = HD ** (-0.5)
LOW = jnp.bfloat16
F32 = jnp.float32
NN = (((1,), (0,)), ((), ()))
NT = (((1,), (1,)), ((), ()))
ROW_CUTS = ((0, 64), (64, 64), (128, 64), (192, 64), (256, 64), (320, 72))
LANE_CUTS = ((0, 1024), (768, 1920), (1664, 2560))


def product(left, right, dims=NN):
    return lax.dot_general(left, right, dims, preferred_element_type=F32)


def shaped(*dims, kind=F32):
    return jax.ShapeDtypeStruct(dims, kind)


def cost(micros):
    return pl.CostEstimate(flops=int(micros * 1e9), bytes_accessed=int(micros * 3.6e6), transcendentals=0)


WHOLE = pl.BlockSpec(memory_space=pltpu.VMEM)
ANYWHERE = pl.BlockSpec(memory_space=pl.ANY)
SCALAR = pl.BlockSpec(memory_space=pltpu.SMEM)
FAR = pl.BlockSpec(memory_space=pltpu.HBM)


def run(kernel, ins, outs, micros, mib, grid=(), scratch=(), after=()):
    count = len(ins)

    def inner(*refs):
        kernel(*refs[:count], *refs[count + len(after) :])

    return pl.pallas_call(
        inner,
        grid=grid,
        out_shape=[o[0] for o in outs],
        in_specs=[i[1] for i in ins] + [ANYWHERE] * len(after),
        out_specs=[o[1] for o in outs],
        scratch_shapes=list(scratch),
        cost_estimate=cost(micros),
        compiler_params=pltpu.CompilerParams(vmem_limit_bytes=mib << 20),
    )(*[i[0] for i in ins], *after)


def pinned(space, *dims, kind=F32):
    return space(dims, kind)


def once(value, *others):
    return lax.optimization_barrier((value, *others))[0]


def held(*dims):
    return pl.BlockSpec(dims, lambda e: (0,) * len(dims))


def normed(values):
    centred = values - jnp.mean(values, -1, keepdims=True)
    rstd = lax.rsqrt(jnp.mean(centred * centred, -1, keepdims=True) + 1e-05)
    return centred * rstd, rstd


def first_norm_kernel(x_ref, gain_ref, tb_ref, region_ref, a1_ref, a1t_ref, rf_ref, rft_ref):
    codes = lax.broadcasted_iota(jnp.int32, (128, WIN), 0)
    for w in range(2):
        vhat, _ = normed(x_ref[w])
        a1 = vhat * gain_ref[0:1, :] + tb_ref[0:1, :]
        a1_ref[w] = a1.astype(LOW)
        a1t_ref[w] = a1.T.astype(LOW)
        differs = jnp.where(codes == region_ref[w : w + 1, :], 0.0, 1.0)
        rft_ref[w] = differs.astype(LOW)
        rf_ref[w] = ((1.0 - differs.T) * -1e30).astype(LOW)


def split3(values):
    high = values.astype(LOW)
    rest = values - high.astype(F32)
    mid = rest.astype(LOW)
    return high, mid, (rest - mid.astype(F32)).astype(LOW)


def rows_from_table_kernel(order_ref, table_ref, lane_ref, column_ref, out_ref, *picks):
    table = jnp.concatenate(split3(table_ref[...]), axis=0)
    rows = lax.broadcasted_iota(jnp.int32, (REL, 256), 0)
    for block in range(RELP // 256):
        cols = slice(block * 256, block * 256 + 256)
        picked = jnp.where(rows == order_ref[:, cols], 1.0, 0.0).astype(LOW)
        got = product(table, picked)
        out_ref[:, cols] = (got[:HEADS] + got[HEADS : 2 * HEADS] + got[2 * HEADS :]) * LOG2E
    for block in range(3):
        low, high = LANE_CUTS[block]
        cols = slice(block * 256, block * 256 + 256)
        down = lax.broadcasted_iota(jnp.int32, (high - low, 256), 0) + low
        picks[block][...] = jnp.where(down == lane_ref[:, cols], 1.0, 0.0).astype(LOW)
        across = lax.broadcasted_iota(jnp.int32, (256, high - low), 1) + low
        picks[3 + block][...] = jnp.where(across == column_ref[cols, :], 1.0, 0.0).astype(LOW)


def rows_to_table_kernel(order_ref, rows_ref, out_ref):
    rows = jnp.concatenate(split3(rows_ref[...]), axis=0)
    ids = lax.broadcasted_iota(jnp.int32, (256, RELP), 0)
    for block in range(RELP // 256):
        picked = jnp.where(ids + block * 256 == order_ref[...], 1.0, 0.0).astype(LOW)
        got = product(rows, picked, NT)
        out_ref[:, block * 256 : block * 256 + 256] = got[:HEADS] + got[HEADS : 2 * HEADS] + got[2 * HEADS :]


def lanes_of(ti):
    off = 49 * (7 - ti)
    base = off // 128 * 128
    return base, off - base


def expand_kernel(group, part_ref, rows_ref, p0, p1, p2, bias_ref, left_s, wide_s):
    base_row = (part_ref[0] ^ group) * GHEADS
    back = 7 - lax.broadcasted_iota(jnp.int32, (8, RELP), 0)
    for h in range(GHEADS):
        row = jnp.broadcast_to(rows_ref[pl.ds(base_row + h, 1), :], (8, RELP))
        for bit in range(3):
            row = jnp.where(((back >> bit) & 1) == 1, pltpu.roll(row, RELP - (1 << bit), 1), row)
        for hi in range(WH):
            rolled = pltpu.roll(row, (1 - (6 - hi) * 13) % RELP, 1)
            high = rolled.astype(LOW).astype(F32)
            at = 112 * h + 8 * hi
            left_s[at : at + 8, :] = high
            left_s[at + 56 : at + 64, :] = rolled - high
    for block, pick in enumerate((p0, p1, p2)):
        low, high = LANE_CUTS[block]
        got = product(left_s[:, low:high].astype(LOW), pick[...])
        for h in range(GHEADS):
            wide_s[h, :, block * 256 : block * 256 + 256] = got[112 * h : 112 * h + 56] + got[112 * h + 56 : 112 * h + 112]
    for h in range(GHEADS):
        for ti in range(WT):
            base, by = lanes_of(ti)
            for hi in range(WH):
                tile = wide_s[h, 8 * hi : 8 * hi + 8, base : base + 512]
                if by:
                    tile = pltpu.roll(tile, 512 - by, 1)
                at = 49 * ti + 7 * hi
                bias_ref[h, at : at + 7, :] = tile[:7, :WIN]


def expand_bias(group, part, rows, picks, after):
    return run(
        functools.partial(expand_kernel, group),
        [(part, SCALAR), (rows, WHOLE)] + [(p, WHOLE) for p in picks],
        [(shaped(GHEADS, WIN, WIN), WHOLE)],
        3, 12,
        scratch=[pltpu.VMEM((112 * GHEADS, RELP), F32), pltpu.VMEM((GHEADS, 56, 768), F32)],
        after=after,
    )[0]


def shrunk(wide_refs, picks, spread_s, out_ref, at):
    heads = wide_refs.shape[0]
    used = (lax.broadcasted_iota(jnp.int32, (56, 256), 0) & 7) < 7
    spread_s[...] = jnp.zeros(spread_s.shape, F32)
    for block, pick in enumerate(picks):
        low, high = LANE_CUTS[block]
        parts = []
        for h in range(heads):
            wide = jnp.where(used, wide_refs[h, :, block * 256 : block * 256 + 256], 0.0)
            near = wide.astype(LOW).astype(F32)
            parts += [near, wide - near]
        got = product(jnp.concatenate(parts, axis=0).astype(LOW), pick[...])
        for h in range(heads):
            spread_s[h, :, low:high] += got[112 * h : 112 * h + 56] + got[112 * h + 56 : 112 * h + 112]
    left = 7 - lax.broadcasted_iota(jnp.int32, (8, RELP), 0)
    for h in range(heads):
        total = jnp.zeros((8, RELP), F32)
        for hi in range(WH):
            total += pltpu.roll(spread_s[h, 8 * hi : 8 * hi + 8, :], ((6 - hi) * 13 - 1) % RELP, 1)
        for bit in range(3):
            total = jnp.where(((left >> bit) & 1) == 1, pltpu.roll(total, 1 << bit, 1), total)
        out_ref[pl.ds(at + h, 1), 0:RELP] = jnp.sum(total, axis=0, keepdims=True)


def shrink_kernel(wide_ref, p0, p1, p2, out_ref, spread_s):
    shrunk(wide_ref, (p0, p1, p2), spread_s, out_ref, 0)


def shrink_bias(wide, picks, after):
    return run(
        shrink_kernel,
        [(wide, WHOLE)] + [(p, WHOLE) for p in picks],
        [(shaped(GHEADS, RELP), WHOLE)],
        1.4, 12,
        scratch=[pltpu.VMEM((GHEADS, 56, RELP), F32)],
        after=after,
    )[0]


def attend_kernel(
    pair, part_ref, a1_ref, wa_ref, wb_ref, qvb_ref, ba_ref, bb_ref, rf_ref, rft_ref,
    p_ref, qt_ref, k_ref, vt_ref, o_ref, li_ref,
    q_s, ka_s, v_s, s_s, acc_s, p_s, p_sem,
):
    step = pl.program_id(0)
    e = step % GHEADS
    slot = step % 2

    def away(at):
        return pltpu.make_async_copy(p_s.at[at % 2], p_ref.at[at], p_sem.at[at % 2])

    @pl.when(step >= 2)
    def _():
        away(step - 2).wait()

    lane = lax.broadcasted_iota(jnp.int32, (WIN, 128), 1) // HD

    def begin(w_ref, group):
        cols = pl.ds(pl.multiple_of((part_ref[0] ^ group) * 128, 128), 128)
        for w in range(2):
            qkv = product(a1_ref[w], w_ref[...])
            q = (qkv[:, :128] + qvb_ref[0:1, cols]) * (SCALE * LOG2E)
            k = qkv[:, 128:256]
            v = qkv[:, 256:384] + qvb_ref[1:2, cols]
            q_s[w] = q
            v_s[w] = v
            qt_ref[0, w] = q.T.astype(LOW)
            k_ref[0, w] = k.astype(LOW)
            vt_ref[0, w] = v.T.astype(LOW)
            ka_s[w, 0:128, :] = k.T.astype(LOW)
            ka_s[w, 128:256, :] = rft_ref[w]
            acc_s[w] = jnp.zeros((WIN, 256), F32)

    @pl.when(step == 0)
    def _():
        begin(wa_ref, 2 * pair)

    @pl.when(step == GHEADS)
    def _():
        begin(wb_ref, 2 * pair + 1)

    mine = lane == e
    for w in range(2):
        q_wide = jnp.concatenate([jnp.where(mine, q_s[w], 0.0).astype(LOW), rf_ref[w]], axis=1)
        s_s[w] = product(q_wide, ka_s[w])

    def soften(bias_ref):
        for w in range(2):
            for start, count in ROW_CUTS:
                rows = slice(start, start + count)
                scores = s_s[w, rows, :] + bias_ref[e, rows, :]
                top = jnp.max(scores, axis=1, keepdims=True)
                p_s[slot, w, rows, :] = jnp.exp2(scores - top).astype(LOW)

    @pl.when(step < GHEADS)
    def _():
        soften(ba_ref)

    @pl.when(step >= GHEADS)
    def _():
        soften(bb_ref)

    away(step).start()

    for w in range(2):
        v_wide = jnp.concatenate(
            [jnp.where(mine, v_s[w], 0.0).astype(LOW), jnp.where(mine, 1.0, 0.0).astype(LOW)], axis=1
        )
        acc_s[w] += product(p_s[slot, w], v_wide)

    @pl.when(e == GHEADS - 1)
    def _():
        for w in range(2):
            inverse = 1.0 / acc_s[w, :, 128:256]
            li_ref[0, w] = inverse
            o_ref[0, w] = acc_s[w, :, 0:128] * inverse

    @pl.when(step == 2 * GHEADS - 1)
    def _():
        away(step - 1).wait()
        away(step).wait()


def by_group(*dims):
    return pl.BlockSpec((1, *dims), lambda e: (e // GHEADS,) + (0,) * len(dims))


def by_head(*dims):
    return pl.BlockSpec((1, *dims), lambda e: (e,) + (0,) * len(dims))


def attend(pair, part, a1, weights, qvb, biases, rf, rft, after):
    rows, turned = by_group(2, WIN, 128), by_group(2, 128, WIN)
    return run(
        functools.partial(attend_kernel, pair),
        [
            (part, SCALAR), (a1, WHOLE), (weights[0], WHOLE), (weights[1], WHOLE), (qvb, WHOLE),
            (biases[0], WHOLE), (biases[1], WHOLE), (rf, WHOLE), (rft, WHOLE),
        ],
        [
            (pinned(pltpu.HBM, 2 * GHEADS, 2, WIN, WIN, kind=LOW), FAR),
            (pinned(pltpu.HBM, 2, 2, 128, WIN, kind=LOW), turned),
            (pinned(pltpu.HBM, 2, 2, WIN, 128, kind=LOW), rows),
            (pinned(pltpu.HBM, 2, 2, 128, WIN, kind=LOW), turned),
            (pinned(pltpu.HBM, 2, 2, WIN, 128), rows),
            (pinned(pltpu.HBM, 2, 2, WIN, 128), rows),
        ],
        11, 16,
        grid=(2 * GHEADS,),
        scratch=[
            pltpu.VMEM((2, WIN, 128), F32),
            pltpu.VMEM((2, 256, WIN), LOW),
            pltpu.VMEM((2, WIN, 128), F32),
            pltpu.VMEM((2, WIN, WIN), F32),
            pltpu.VMEM((2, WIN, 256), F32),
            pltpu.VMEM((2, 2, WIN, WIN), LOW),
            pltpu.SemaphoreType.DMA((2,)),
        ],
        after=after,
    )


def attend_back_kernel(
    at, do_ref, o_ref, li_ref, p_ref, qt_ref, k_ref, vt_ref, a1t_ref, gp_ref,
    dw_ref, wide_ref, low_ref, cs_ref,
    dop_s, dopt_s, nd_s, va_s, dp_s, ds_s, dq_s, dkt_s, dvt_s, db_s, p_s, p_sem,
):
    e = pl.program_id(0)

    def near(head):
        return pltpu.make_async_copy(p_ref.at[GHEADS * at + head], p_s.at[head % 2], p_sem.at[head % 2])

    @pl.when(e == 0)
    def _():
        near(e).start()

    @pl.when(e + 1 < GHEADS)
    def _():
        near(e + 1).start()

    slot = e % 2
    lane = lax.broadcasted_iota(jnp.int32, (WIN, 128), 1) // HD

    @pl.when(e == 0)
    def _():
        for w in range(2):
            dop = do_ref[0, w].astype(F32) * li_ref[0, w]
            dop_s[w] = dop
            nd_s[w] = -(dop.astype(LOW).astype(F32) * o_ref[0, w])
            va_s[w, 0:128, :] = vt_ref[0, w]
            va_s[w, 128:256, :] = jnp.ones((128, WIN), LOW)
            dopt_s[w] = dop.T.astype(LOW)
            dq_s[w] = jnp.zeros((WIN, 128), F32)

    mine = lane == e
    first = pl.multiple_of(HD * e, HD)
    own = pl.ds(first, HD)
    for w in range(2):
        wide = jnp.concatenate(
            [jnp.where(mine, dop_s[w], 0.0).astype(LOW), jnp.where(mine, nd_s[w], 0.0).astype(LOW)], axis=1
        )
        dp_s[w] = product(wide, va_s[w])
    near(e).wait()
    for w in range(2):
        dvt_s[w, own, :] = product(dopt_s[w, own, :], p_s[slot, w])
    for start, count in ROW_CUTS:
        rows = slice(start, start + count)
        one = p_s[slot, 0, rows, :].astype(F32) * dp_s[0, rows, :]
        two = p_s[slot, 1, rows, :].astype(F32) * dp_s[1, rows, :]
        db_s[rows, 0:WIN] = one + two
        ds_s[0, rows, :] = one.astype(LOW)
        ds_s[1, rows, :] = two.astype(LOW)
    for w in range(2):
        dkt_s[w, own, :] = product(qt_ref[0, w, own, :], ds_s[w])
        k_mine = jnp.where(mine, k_ref[0, w], jnp.zeros((WIN, 128), LOW))
        dq_s[w] += product(ds_s[w], k_mine)
    inside = lax.broadcasted_iota(jnp.int32, (8, 512), 1) < WIN
    for hi in range(WH):
        own_rows = slice(8 * hi, 8 * hi + 8)
        wide_ref[0, own_rows, :] = jnp.zeros((8, 768), F32)
        for base in (0, 128, 256):
            total = jnp.zeros((8, 512), F32)
            for ti in range(WT):
                lane_base, by = lanes_of(ti)
                if lane_base != base:
                    continue
                first_row = 49 * ti + 7 * hi
                tile = jnp.where(inside, db_s[first_row : first_row + 8, :], 0.0)
                total += pltpu.roll(tile, by, 1) if by else tile
            wide_ref[0, own_rows, base : base + 512] += total

    @pl.when(e == GHEADS - 1)
    def _():
        sum_q = jnp.zeros((1, 128), F32)
        sum_v = jnp.zeros((1, 128), F32)
        grad = jnp.zeros((D, 384), F32)
        for w in range(2):
            dq = dq_s[w] * SCALE
            dk = (dkt_s[w] * (1.0 / LOG2E)).T
            dv = dvt_s[w].T
            sum_q += jnp.sum(dq, axis=0, keepdims=True)
            sum_v += jnp.sum(dv, axis=0, keepdims=True)
            low = jnp.concatenate([dq, dk, dv], axis=1).astype(LOW)
            low_ref[w] = low
            grad += product(a1t_ref[w], low)
        dw_ref[:, 0:384] = grad.astype(LOW)
        dw_ref[:, 384:512] = gp_ref[0]
        cs_ref[0:1, :] = sum_q
        cs_ref[1:2, :] = sum_v


def attend_back(at, do, kept, a1t, gproj, after):
    p, qt, k, vt, o, li = kept
    do, o, li, qt, k, vt, a1t, gproj = (
        pltpu.with_memory_space_constraint(a, pltpu.HBM) for a in (do, o, li, qt, k, vt, a1t, gproj)
    )

    def group(*dims):
        return pl.BlockSpec((1, *dims), lambda e: (at,) + (0,) * len(dims))

    rows, turned = group(2, WIN, 128), group(2, 128, WIN)
    return run(
        functools.partial(attend_back_kernel, at),
        [
            (do, rows), (o, rows), (li, rows),
            (pltpu.with_memory_space_constraint(p, pltpu.HBM), FAR),
            (qt, turned), (k, rows), (vt, turned), (a1t, WHOLE), (gproj, group(D, 128)),
        ],
        [
            (shaped(D, 512, kind=LOW), held(D, 512)),
            (shaped(GHEADS, 56, 768), by_head(56, 768)),
            (shaped(2, WIN, 384, kind=LOW), held(2, WIN, 384)),
            (shaped(2, 128), held(2, 128)),
        ],
        6, 14,
        grid=(GHEADS,),
        scratch=[
            pltpu.VMEM((2, WIN, 128), F32),
            pltpu.VMEM((2, 128, WIN), LOW),
            pltpu.VMEM((2, WIN, 128), F32),
            pltpu.VMEM((2, 256, WIN), LOW),
            pltpu.VMEM((2, WIN, WIN), F32),
            pltpu.VMEM((2, WIN, WIN), LOW),
            pltpu.VMEM((2, WIN, 128), F32),
            pltpu.VMEM((2, 128, WIN), F32),
            pltpu.VMEM((2, 128, WIN), F32),
            pltpu.VMEM((400, 512), F32),
            pltpu.VMEM((2, 2, WIN, WIN), LOW),
            pltpu.SemaphoreType.DMA((2,)),
        ],
        after=after,
    )


def gelu_parts(v):
    size = jnp.abs(v)
    t = 1.0 / (1.0 + (0.3275911 * 0.7071067811865476) * size)
    bell = jnp.exp2(v * v * (-0.5 * LOG2E))
    poly = t * (0.127414796 + t * (-0.142248368 + t * (0.7107068705 + t * (-0.7265760135 + t * 0.5307027145))))
    tail = poly * bell
    phi = jnp.where(v >= 0.0, 1.0 - tail, tail)
    return v * phi, phi + v * bell * 0.3989422804014327


def norm_back(values, dy, gain):
    vhat, rstd = normed(values)
    scaled = dy * gain
    dv = rstd * (
        scaled - jnp.mean(scaled, -1, keepdims=True) - vhat * jnp.mean(scaled * vhat, -1, keepdims=True)
    )
    return dv, jnp.sum(dy * vhat, axis=0, keepdims=True), jnp.sum(dy, axis=0, keepdims=True)


ROWS = 2 * WIN


def middle_kernel(
    part_ref, on_ref, of_ref, x_ref, cot_ref, tb_ref, gain_ref, hb_ref,
    u0, u1, u2, u3, w0, w1, w2, w3,
    out_ref, dafter_ref, dn_ref, df_ref, gpn_ref, gpf_ref, odd_ref, even_ref, sums_ref, ghb_ref,
    up_s, down_s, after_s, a2_s, a2t_s, g_s, gt_s, mix_s, da2_s, h_s, d_s, act_s, dh_s,
):
    step = pl.program_id(0)
    r = (2 * step + 1) % 5
    ups, downs = (u0, u1, u2, u3), (w0, w1, w2, w3)

    @pl.when(step == 0)
    def _():
        cot = jnp.concatenate([cot_ref[0], cot_ref[1]], axis=0)
        g_s[...] = cot.astype(LOW)
        gt_s[...] = cot.T.astype(LOW)
        weight = jnp.concatenate([u[:, 0:128] for u in ups], axis=1)
        lows = []
        for w in range(2):
            mixed = jnp.concatenate([on_ref[0, w], on_ref[1, w], of_ref[0, w], of_ref[1, w]], axis=1).astype(LOW)
            mix_s[w] = mixed
            after = x_ref[w] + product(mixed, weight, NT) + tb_ref[1:2, :]
            after_s[w] = after
            vhat, _ = normed(after)
            lows.append(vhat * gain_ref[1:2, :] + tb_ref[2:3, :])
            out_ref[WIN * w : WIN * w + WIN, :] = after + tb_ref[3:4, :]
        a2 = jnp.concatenate(lows, axis=0)
        a2_s[...] = a2.astype(LOW)
        a2t_s[...] = a2.T.astype(LOW)
        da2_s[...] = jnp.zeros((ROWS, D), F32)

    for i in range(PARTS):

        @pl.when(r == i)
        def _():
            up_s[...] = ups[i][:, 128:640]
            down_s[...] = downs[i][...]

    up = up_s[...]
    down = down_s[...]
    h_s[...] = product(a2_s[...], up)
    d_s[...] = product(g_s[...], down)
    for cut in range(0, 512, 128):
        cols = slice(cut, cut + 128)
        line = hb_ref[r ^ part_ref[0], :, cols]
        sums = jnp.zeros((1, 128), F32)
        for start in range(0, ROWS, 112):
            rows = slice(start, start + 112)
            act, slope = gelu_parts(h_s[rows, cols] + line)
            act_s[rows, cols] = act.astype(LOW)
            grad = d_s[rows, cols] * slope
            sums += jnp.sum(grad, axis=0, keepdims=True)
            dh_s[rows, cols] = grad.astype(LOW)
        ghb_ref[r ^ part_ref[0], :, cols] = sums
    gup = product(a2t_s[...], dh_s[...]).astype(LOW)
    gdown = product(gt_s[...], act_s[...]).astype(LOW)

    @pl.when(step < 2)
    def _():
        odd_ref[0, :, 0:512] = gup
        odd_ref[0, :, 512:1024] = gdown

    @pl.when(step >= 2)
    def _():
        even_ref[0, :, 0:512] = gup
        even_ref[0, :, 512:1024] = gdown

    out_ref[...] += product(act_s[...], down, NT)
    da2_s[...] += product(dh_s[...], up, NT)

    @pl.when(step == PARTS - 1)
    def _():
        weight = jnp.concatenate([u[:, 0:128] for u in ups], axis=1)
        grad = jnp.zeros((D, D), F32)
        sums = [jnp.zeros((1, D), F32) for _ in range(4)]
        for w in range(2):
            own = slice(WIN * w, WIN * w + WIN)
            dv, dgain, doff = norm_back(after_s[w], da2_s[own, :], gain_ref[1:2, :])
            cot = cot_ref[w]
            dafter = cot + dv
            dafter_ref[w] = dafter
            turned = dafter.T.astype(LOW)
            dmix = product(dafter.astype(LOW), weight).astype(LOW)
            for i, (ref, at) in enumerate(((dn_ref, 0), (dn_ref, 1), (df_ref, 0), (df_ref, 1))):
                ref[at, w] = dmix[:, 128 * i : 128 * i + 128]
            grad += product(turned, mix_s[w])
            parts = (dgain, doff, jnp.sum(dafter, axis=0, keepdims=True), jnp.sum(cot, axis=0, keepdims=True))
            for i, part in enumerate(parts):
                sums[i] += part
        for i, (ref, at) in enumerate(((gpn_ref, 0), (gpn_ref, 1), (gpf_ref, 0), (gpf_ref, 1))):
            ref[at] = grad[:, 128 * i : 128 * i + 128].astype(LOW)
        for i in range(4):
            sums_ref[i : i + 1, :] = sums[i]


def middle(part, o_near, o_far, x, cot, biases, gains, hb, ups, downs):
    wide = (1, D, 1024)
    pairs = held(2, 2, WIN, 128)
    return run(
        middle_kernel,
        [(part, SCALAR)]
        + [(a, WHOLE) for a in (o_near, o_far, x, cot, biases, gains, hb)]
        + [(a, WHOLE) for a in (*ups, *downs)],
        [
            (shaped(ROWS, D), held(ROWS, D)), (shaped(2, WIN, D), held(2, WIN, D)),
            (pinned(pltpu.HBM, 2, 2, WIN, 128, kind=LOW), pairs), (pinned(pltpu.HBM, 2, 2, WIN, 128, kind=LOW), pairs),
            (pinned(pltpu.HBM, 2, D, 128, kind=LOW), held(2, D, 128)), (pinned(pltpu.HBM, 2, D, 128, kind=LOW), held(2, D, 128)),
            (shaped(2, D, 1024, kind=LOW), pl.BlockSpec(wide, lambda s: (jnp.minimum(s, 1), 0, 0))),
            (shaped(2, D, 1024, kind=LOW), pl.BlockSpec(wide, lambda s: (jnp.maximum(s - 2, 0), 0, 0))),
            (shaped(4, D), held(4, D)), (shaped(PARTS, 1, 512), held(PARTS, 1, 512)),
        ],
        24, 24,
        grid=(PARTS,),
        scratch=[
            pltpu.VMEM((D, 512), LOW), pltpu.VMEM((D, 512), LOW),
            pltpu.VMEM((2, WIN, D), F32),
            pltpu.VMEM((ROWS, D), LOW), pltpu.VMEM((D, ROWS), LOW),
            pltpu.VMEM((ROWS, D), LOW), pltpu.VMEM((D, ROWS), LOW),
            pltpu.VMEM((2, WIN, D), LOW),
            pltpu.VMEM((ROWS, D), F32),
            pltpu.VMEM((ROWS, 512), F32), pltpu.VMEM((ROWS, 512), F32),
            pltpu.VMEM((ROWS, 512), LOW), pltpu.VMEM((ROWS, 512), LOW),
        ],
    )


PACK = RELP + D


def last_kernel(
    part_ref, x_ref, dafter_ref, gain_ref, l0, l1, l2, l3, w0, w1, w2, w3,
    c0, c1, c2, c3, two_ref, ghb_ref, wide_ref, p0, p1, p2, e1, e2, e3,
    gx_ref, pack_ref, spread_s, pack_s,
):
    sums = [jnp.zeros((1, D), F32) for _ in range(2)]
    for w in range(2):
        da1 = jnp.zeros((WIN, D), F32)
        for low, wt in ((l0, w0), (l1, w1), (l2, w2), (l3, w3)):
            da1 += product(low[w], wt[...], NT)
        dv, dgain, doff = norm_back(x_ref[w], da1, gain_ref[0:1, :])
        gx_ref[w] = dafter_ref[w] + dv
        sums[0] += dgain
        sums[1] += doff
    cols = slice(RELP, PACK)
    pack_s[0:1, cols] = sums[0]
    pack_s[1:2, cols] = sums[1]
    pack_s[2:6, cols] = two_ref[...]
    for group, c in enumerate((c0, c1, c2, c3)):
        own = pl.ds(pl.multiple_of(RELP + (part_ref[0] ^ group) * 128, 128), 128)
        pack_s[6:8, own] = c[...]
    for i in range(PARTS):
        pack_s[8 + i : 9 + i, cols] = ghb_ref[i]
    pack_s[12:16, cols] = jnp.zeros((4, D), F32)
    for group, rows in enumerate((e1, e2, e3)):
        for h in range(GHEADS):
            pack_s[pl.ds((part_ref[0] ^ (group + 1)) * GHEADS + h, 1), 0:RELP] = rows[h : h + 1, :]
    shrunk(wide_ref, (p0, p1, p2), spread_s, pack_s, part_ref[0] * GHEADS)
    pack_ref[...] = pack_s[...].astype(LOW)


def swap(values, axis, distance):
    count = lax.axis_size(axis)
    return lax.ppermute(values, axis, [(i, i ^ distance) for i in range(count)])


def bits_of(axis):
    return (lax.axis_size(axis) - 1).bit_length()


def interleaved(own, other, upper):
    place = jnp.arange(2, dtype=jnp.int32).reshape(1, 2, *(1,) * (own.ndim - 1))
    mine = place == upper.astype(jnp.int32)
    return jnp.where(mine, own[:, None], other[:, None]).reshape(-1, *own.shape[1:])


def upper_of(axis, bit):
    return (lax.axis_index(axis) >> bit) % 2 == 1


def gathered(blocks, bits):
    for bit in bits:
        blocks = interleaved(blocks, swap(blocks, "dp", 1 << bit), upper_of("dp", bit))
    return blocks


def flat(blocks):
    return blocks.reshape(-1, blocks.shape[-1])


def half(total, bit, mine):
    pairs = total.reshape(-1, 2, *total.shape[1:])
    return jnp.where(upper_of("dp", bit) == mine, pairs[:, 1], pairs[:, 0])


def halves(total, bit):
    return half(total, bit, False).astype(LOW), half(total, bit, True).astype(F32)


def plus(one, two):
    return one.astype(F32) + two.astype(F32)


def window_regions(shift_row, first_window):
    within = first_window + jnp.arange(2, dtype=jnp.int32)
    places = jnp.arange(WIN, dtype=jnp.int32)
    along_t = (within // 4)[:, None] * WT + (places // (WH * WW))[None, :]
    along_h = (within // 2 % 2)[:, None] * WH + (places // WW % WH)[None, :]
    along_w = (within % 2)[:, None] * WW + (places % WW)[None, :]
    region_t = (along_t >= GT - WT).astype(jnp.int32) + (along_t >= GT - shift_row[0]).astype(jnp.int32)
    region_h = (along_h >= GH - WH).astype(jnp.int32) + (along_h >= GH - shift_row[1]).astype(jnp.int32)
    region_w = (along_w >= GW - WW).astype(jnp.int32) + (along_w >= GW - shift_row[2]).astype(jnp.int32)
    return region_t * 9 + region_h * 3 + region_w


def offset_order(rel_index):
    corners = rel_index.reshape(WT, WH, WW, WIN)[::7, ::6, ::6].reshape(2, 2, 2, WT, WH, WW)
    joined = jnp.concatenate([corners[1], corners[0][:, :, 1:]], axis=2)
    joined = jnp.concatenate([joined[1], joined[0][:, :, 1:]], axis=2)
    joined = jnp.concatenate([joined[1], joined[0][:, :, 1:]], axis=2)
    return jnp.pad(joined.reshape(1, REL), ((0, 0), (0, RELP - REL)), constant_values=-1)


def body(
    inputs,
    w_qkv,
    qv_bias,
    w_proj,
    w_fc1,
    fc1_bias,
    w_fc2,
    norm_gains,
    token_biases,
    table,
    shifts,
    rel_index,
    cotangent,
):
    index = lax.axis_index("mp")
    part = index.astype(jnp.int32).reshape(1)
    rows = w_qkv.shape[1]
    x = inputs.reshape(2, WIN, D)
    cot = cotangent.reshape(2, WIN, D)
    high_bits = tuple(reversed(range(1, bits_of("dp"))))
    low_bits = tuple(range(1, bits_of("dp")))

    shard_qkv = w_qkv.transpose(1, 0, 2).reshape(1, rows, 384).astype(LOW)
    shard_rest = jnp.concatenate([w_proj.T, w_fc1, w_fc2.T], axis=1).astype(LOW)[None]
    qkv_first = gathered(shard_qkv, high_bits[:1])
    qkv_high = gathered(qkv_first, high_bits[1:])
    own = flat(gathered(qkv_high, (0,)))
    qkv_parts = [own, swap(own, "mp", 1)]
    across = swap(own, "mp", 2)
    rest = gathered(shard_rest, high_bits)
    up_own = gathered(rest[:, :, :640], (0,))
    up_across = swap(up_own, "mp", 2)
    down_across = swap(rest[:, :, 640:], "mp", 2)
    regions = window_regions(once(shifts, qkv_first)[0], index * 2)
    order = offset_order(once(rel_index, qkv_first))
    column = jnp.arange(768, dtype=jnp.int32)
    lane_row = jnp.where(
        column < 15 * 49, column // 49 * 169 + column % 49 // 7 * 13 + column % 7, -1
    )
    a1, a1t, rf, rft = run(
        first_norm_kernel,
        [(a, WHOLE) for a in (x, norm_gains, token_biases, regions)],
        [
            (shaped(2, WIN, D, kind=LOW), WHOLE), (pinned(pltpu.HBM, 2, D, WIN, kind=LOW), WHOLE),
            (shaped(2, WIN, 128, kind=LOW), WHOLE), (shaped(2, 128, WIN, kind=LOW), WHOLE),
        ],
        2, 16,
        after=(qkv_first,),
    )
    row_offsets, *picks = run(
        rows_from_table_kernel,
        [(a, WHOLE) for a in (order, table.T, lane_row.reshape(1, 768), lane_row.reshape(768, 1))],
        [(shaped(HEADS, RELP), WHOLE)]
        + [(shaped(high - low, 256, kind=LOW), WHOLE) for low, high in LANE_CUTS]
        + [(shaped(256, high - low, kind=LOW), WHOLE) for low, high in LANE_CUTS],
        4, 20,
        after=(qkv_high,),
    )
    out_picks, back_picks = picks[:3], picks[3:]
    near_bias = [expand_bias(r, part, row_offsets, out_picks, (qkv_high,)) for r in (0, 1)]
    near = attend(0, part, a1, qkv_parts[:2], qv_bias, near_bias, rf, rft, (rest,))
    across = once(across, near[4])
    qkv_parts += [across, swap(across, "mp", 1)]
    down_pair = jnp.stack([rest[:, :, 640:], once(down_across, near[4])], axis=0)
    down_other = swap(down_pair, "dp", 1)
    down_own, down_across = (
        interleaved(down_pair[i], down_other[i], upper_of("dp", 0)) for i in range(2)
    )
    far_bias = [expand_bias(r, part, row_offsets, out_picks, (near[4],)) for r in (2, 3)]
    far = attend(1, part, a1, qkv_parts[2:], qv_bias, far_bias, rf, rft, (up_own,))
    up_parts = [flat(up_own), flat(swap(up_own, "mp", 1)), flat(up_across), flat(swap(once(up_across, far[4]), "mp", 1))]
    down_parts = [
        flat(down_own), flat(swap(down_own, "mp", 1)), flat(down_across), flat(swap(down_across, "mp", 1))
    ]
    out, dafter, do_near, do_far, gp_near, gp_far, odd, even, sums_two, g_hb = middle(
        part, near[4], far[4], x, cot, token_biases, norm_gains, fc1_bias.reshape(PARTS, 1, 512), up_parts, down_parts
    )

    three, wide3, low3, col3 = attend_back(1, do_far, far, a1t, gp_far, ())
    blocks = even.reshape(2, -1, rows, 1024)
    other = swap(odd, "mp", 1).reshape(2, -1, rows, 1024)
    up_send = plus(blocks[1, :, :, :512], other[1, :, :, :512]).astype(LOW)
    turned = [a[:, :, :, 512:].transpose(1, 0, 2, 3) for a in (blocks, other)]
    down_send = plus(*(half(a, 0, False) for a in turned)).astype(LOW)
    two, wide2, low2, col2 = attend_back(0, do_far, far, a1t, gp_far, (up_send, down_send, three))
    up_sum = plus(plus(blocks[0, :, :, :512], other[0, :, :, :512]), swap(up_send, "mp", 2))
    down_sum = plus(plus(*(half(a, 0, True) for a in turned)), swap(down_send, "dp", 1))
    far_sum = plus(two, swap(three, "mp", 1)).astype(LOW)
    one, wide1, low1, col1 = attend_back(1, do_near, near, a1t, gp_near, (far_sum,))
    far_sum = swap(far_sum, "mp", 2)
    up_send, up_keep = halves(up_sum, 0)
    down_send, down_keep = down_sum[:, 1].astype(LOW), down_sum[:, 0]
    zero, wide0, low0, col0 = attend_back(0, do_near, near, a1t, gp_near, (up_send, down_send, one))
    up_sum = plus(up_keep, swap(up_send, "dp", 1))
    down_sum = plus(down_keep, swap(down_send, "mp", 2))
    total = plus(plus(zero, swap(one, "mp", 1)), far_sum).reshape(-1, rows, 512)
    rows_by = [shrink_bias(w, back_picks, ()) for w in (wide1, wide2, wide3)]
    send, keep = halves(total, 0)
    grad_x, pack = run(
        last_kernel,
        [(part, SCALAR)]
        + [
            (a, WHOLE)
            for a in (
                x, dafter, norm_gains, low0, low1, low2, low3, *qkv_parts, col0, col1, col2, col3,
                sums_two, g_hb, wide0, *back_picks, *rows_by,
            )
        ],
        [(shaped(2, WIN, D), WHOLE), (shaped(HEADS, PACK, kind=LOW), WHOLE)],
        4, 20,
        scratch=[pltpu.VMEM((GHEADS, 56, RELP), F32), pltpu.VMEM((HEADS, PACK), F32)],
        after=(send, up_sum, down_sum),
    )
    summed = jnp.concatenate([up_sum, down_sum], axis=2)
    total = plus(keep, swap(send, "dp", 1))
    mp_steps = [("mp", 1 << bit) for bit in range(bits_of("mp"))]
    steps = mp_steps + [("dp", 1 << bit) for bit in range(bits_of("dp"))]
    queue = [("qkv", bit) for bit in low_bits] + [("mlp", bit) for bit in low_bits]
    queue.sort(key=lambda item: (item[1], item[0] == "qkv"))
    state = {"qkv": total, "mlp": summed}
    pending = None
    for place, (axis, distance) in enumerate(steps):
        mine = pack.astype(LOW)
        theirs = swap(mine, axis, distance)
        if pending is not None:
            name, keep, got = pending
            state[name] = plus(keep, once(got, mine))
            pending = None
        if place >= 1 and queue:
            name, bit = queue.pop(0)
            send, keep = halves(once(state[name], mine), bit)
            theirs = once(theirs, send)
            pending = (name, keep, swap(send, "dp", 1 << bit))
        pack = plus(mine, theirs)
    if pending is not None:
        state[pending[0]] = plus(pending[1], pending[2])
    for name, bit in queue:
        send, keep = halves(state[name], bit)
        state[name] = plus(keep, swap(send, "dp", 1 << bit))
    own_qkv = state["qkv"].reshape(rows, 512)
    own_mlp = state["mlp"].reshape(rows, 1024)
    small = pack[:, RELP:]
    (grad_table,) = run(
        rows_to_table_kernel,
        [(order, WHOLE), (pack[:, :RELP], WHOLE)],
        [(shaped(HEADS, RELP), WHOLE)],
        4, 20,
    )
    return (
        out.reshape(inputs.shape),
        grad_x.reshape(inputs.shape),
        own_qkv[:, :384].reshape(rows, 3, 128).transpose(1, 0, 2),
        small[6:8],
        own_qkv[:, 384:].T,
        own_mlp[:, :512],
        small[8:12].reshape(FF),
        own_mlp[:, 512:].T,
        jnp.concatenate([small[0:1], small[2:3]], axis=0),
        jnp.concatenate([small[1:2], small[4:5], small[3:4], small[5:6]], axis=0),
        grad_table[:, :REL].T,
    )


def solution(mesh):
    placed = (
        P(("dp", "mp"), None),
        P(None, "dp", "mp"),
        P(),
        P("mp", "dp"),
        P("dp", "mp"),
        P(),
        P("mp", "dp"),
        P(),
        P(),
        P(),
        P("dp", None),
        P(),
        P(("dp", "mp"), None),
    )
    return jax.shard_map(
        body,
        mesh=mesh,
        in_specs=placed,
        out_specs=(
            P(("dp", "mp"), None),
            P(("dp", "mp"), None),
            P(None, "dp", "mp"),
            P(),
            P("mp", "dp"),
            P("dp", "mp"),
            P(),
            P("mp", "dp"),
            P(),
            P(),
            P(),
        ),
        check_vma=False,
    )
```

```python
import functools

import jax
import jax.numpy as jnp
from jax import lax
from jax.experimental import pallas as pl
from jax.experimental.pallas import tpu as pltpu
from jax.sharding import PartitionSpec as P

D = 512
HEADS = 16
HD = 32
FF = 2048
WT = 8
WH = 7
WW = 7
GT = 16
GH = 14
GW = 14
WIN = 392
REL = 2535
RELP = 2560
PACK = RELP + D
WINS = 8
PARTS = 4
GHEADS = HEADS // PARTS
LOG2E = 1.4426950408889634
SCALE = HD ** (-0.5)
LOW = jnp.bfloat16
F32 = jnp.float32
NN = (((1,), (0,)), ((), ()))
NT = (((1,), (1,)), ((), ()))
ROW_CUTS = ((0, 64), (64, 64), (128, 64), (192, 64), (256, 64), (320, 72))
LANE_CUTS = ((0, 1024), (768, 1920), (1664, 2560))


def product(left, right, dims=NN):
    return lax.dot_general(left, right, dims, preferred_element_type=F32)


def shaped(*dims, kind=F32):
    return jax.ShapeDtypeStruct(dims, kind)


def cost(micros):
    return pl.CostEstimate(flops=int(micros * 1e9), bytes_accessed=int(micros * 3.6e6), transcendentals=0)


WHOLE = pl.BlockSpec(memory_space=pltpu.VMEM)
ANYWHERE = pl.BlockSpec(memory_space=pl.ANY)
SCALAR = pl.BlockSpec(memory_space=pltpu.SMEM)
FAR = pl.BlockSpec(memory_space=pltpu.HBM)


def run(kernel, ins, outs, micros, mib, grid=(), scratch=(), after=()):
    count = len(ins)

    def inner(*refs):
        kernel(*refs[:count], *refs[count + len(after) :])

    return pl.pallas_call(
        inner,
        grid=grid,
        out_shape=[o[0] for o in outs],
        in_specs=[i[1] for i in ins] + [ANYWHERE] * len(after),
        out_specs=[o[1] for o in outs],
        scratch_shapes=list(scratch),
        cost_estimate=cost(micros),
        compiler_params=pltpu.CompilerParams(vmem_limit_bytes=mib << 20),
    )(*[i[0] for i in ins], *after)


def pinned(space, *dims, kind=F32):
    return space(dims, kind)


def once(value, *others):
    return lax.optimization_barrier((value, *others))[0]


def held(*dims):
    return pl.BlockSpec(dims, lambda e: (0,) * len(dims))


def normed(values):
    centred = values - jnp.mean(values, -1, keepdims=True)
    rstd = lax.rsqrt(jnp.mean(centred * centred, -1, keepdims=True) + 1e-05)
    return centred * rstd, rstd


def first_norm_kernel(part_ref, shift_ref, x_ref, gain_ref, tb_ref, place_ref, a1_ref, a1t_ref, rf_ref, rft_ref):
    codes = lax.broadcasted_iota(jnp.int32, (128, WIN), 0)
    for w in range(2):
        window = (2 * part_ref[0] + w) % WINS
        region = jnp.zeros((1, WIN), jnp.int32)
        for axis, (length, size, along) in enumerate(
            ((WT, GT, window // 4), (WH, GH, window // 2 % 2), (WW, GW, window % 2))
        ):
            cell = place_ref[axis : axis + 1, :] + along * length
            halves_in = (cell >= size - length).astype(jnp.int32)
            shifted = (cell >= size - shift_ref[0, axis]).astype(jnp.int32)
            region = region * 3 + halves_in + shifted
        vhat, _ = normed(x_ref[w])
        a1 = vhat * gain_ref[0:1, :] + tb_ref[0:1, :]
        a1_ref[w] = a1.astype(LOW)
        a1t_ref[w] = a1.T.astype(LOW)
        differs = jnp.where(codes == region, 0.0, 1.0)
        rft_ref[w] = differs.astype(LOW)
        rf_ref[w] = ((1.0 - differs.T) * -1e30).astype(LOW)


def rest_kernel(proj_ref, up_ref, down_ref, out_ref):
    out_ref[...] = jnp.concatenate([proj_ref[...], up_ref[...], down_ref[...]], axis=1).astype(LOW)


def split3(values):
    high = values.astype(LOW)
    rest = values - high.astype(F32)
    mid = rest.astype(LOW)
    return high, mid, (rest - mid.astype(F32)).astype(LOW)


def rows_from_table_kernel(order_ref, table_ref, lane_ref, column_ref, out_ref, *picks):
    table = jnp.concatenate(split3(table_ref[...]), axis=0)
    rows = lax.broadcasted_iota(jnp.int32, (REL, 256), 0)
    for block in range(RELP // 256):
        cols = slice(block * 256, block * 256 + 256)
        picked = jnp.where(rows == order_ref[:, cols], 1.0, 0.0).astype(LOW)
        got = product(table, picked)
        out_ref[:, cols] = (got[:HEADS] + got[HEADS : 2 * HEADS] + got[2 * HEADS :]) * LOG2E
    for block in range(3):
        low, high = LANE_CUTS[block]
        cols = slice(block * 256, block * 256 + 256)
        down = lax.broadcasted_iota(jnp.int32, (high - low, 256), 0) + low
        picks[block][...] = jnp.where(down == lane_ref[:, cols], 1.0, 0.0).astype(LOW)
        across = lax.broadcasted_iota(jnp.int32, (256, high - low), 1) + low
        picks[3 + block][...] = jnp.where(across == column_ref[cols, :], 1.0, 0.0).astype(LOW)


def rows_to_table_kernel(order_ref, pack_ref, out_ref, gains_ref, biases_ref, pair_ref, hidden_ref):
    rows = jnp.concatenate(split3(pack_ref[:, 0:RELP]), axis=0)
    ids = lax.broadcasted_iota(jnp.int32, (256, RELP), 0)
    for start in range(0, REL, 256):
        count = min(256, REL - start)
        picked = jnp.where(ids + start == order_ref[...], 1.0, 0.0).astype(LOW)
        got = product(rows, picked, NT)
        got = got[:HEADS] + got[HEADS : 2 * HEADS] + got[2 * HEADS :]
        out_ref[:, start : start + count] = got[:, :count]
    cols = slice(RELP, PACK)
    for i, at in enumerate((0, 2)):
        gains_ref[i : i + 1, :] = pack_ref[at : at + 1, cols]
    for i, at in enumerate((1, 4, 3, 5)):
        biases_ref[i : i + 1, :] = pack_ref[at : at + 1, cols]
    pair_ref[...] = pack_ref[6:8, cols]
    hidden_ref[...] = pack_ref[8:12, cols]


def unpack_qkv_kernel(qkv_ref, out_ref, proj_ref):
    for i in range(3):
        out_ref[i] = qkv_ref[:, 128 * i : 128 * i + 128]
    proj_ref[...] = qkv_ref[:, 384:512]


def unpack_mlp_kernel(mlp_ref, up_ref, down_ref):
    up_ref[...] = mlp_ref[:, 0:512]
    down_ref[...] = mlp_ref[:, 512:1024]


def lanes_of(ti):
    off = 49 * (7 - ti)
    base = off // 128 * 128
    return base, off - base


def expand_kernel(pair, part_ref, rows_ref, p0, p1, p2, bias_ref, left_s, wide_s):
    group = 2 * pair + pl.program_id(0)
    base_row = (part_ref[0] ^ group) * GHEADS
    back = 7 - lax.broadcasted_iota(jnp.int32, (8, RELP), 0)
    for h in range(GHEADS):
        row = jnp.broadcast_to(rows_ref[pl.ds(base_row + h, 1), :], (8, RELP))
        for bit in range(3):
            row = jnp.where(((back >> bit) & 1) == 1, pltpu.roll(row, RELP - (1 << bit), 1), row)
        for hi in range(WH):
            rolled = pltpu.roll(row, (1 - (6 - hi) * 13) % RELP, 1)
            at = 56 * h + 8 * hi
            left_s[at : at + 8, :] = rolled
    for block, pick in enumerate((p0, p1, p2)):
        low, high = LANE_CUTS[block]
        got = product(left_s[:, low:high].astype(LOW), pick[...])
        for h in range(GHEADS):
            wide_s[h, :, block * 256 : block * 256 + 256] = got[56 * h : 56 * h + 56]
    for h in range(GHEADS):
        for ti in range(WT):
            base, by = lanes_of(ti)
            for hi in range(WH):
                tile = wide_s[h, 8 * hi : 8 * hi + 8, base : base + 512]
                if by:
                    tile = pltpu.roll(tile, 512 - by, 1)
                at = 49 * ti + 7 * hi
                bias_ref[h, at : at + 7, :] = tile[:7, :WIN]


def expand_bias(pair, part, rows, picks, after):
    return run(
        functools.partial(expand_kernel, pair),
        [(part, SCALAR), (rows, WHOLE)] + [(p, WHOLE) for p in picks],
        [(shaped(2 * GHEADS, WIN, WIN), pl.BlockSpec((GHEADS, WIN, WIN), lambda g: (g, 0, 0)))],
        5, 14,
        grid=(2,),
        scratch=[pltpu.VMEM((56 * GHEADS, RELP), F32), pltpu.VMEM((GHEADS, 56, 768), F32)],
        after=after,
    )[0]


def shrunk(wide_refs, picks, spread_s, out_ref, at):
    heads = wide_refs.shape[0]
    used = (lax.broadcasted_iota(jnp.int32, (56, 256), 0) & 7) < 7
    spread_s[...] = jnp.zeros(spread_s.shape, F32)
    for block, pick in enumerate(picks):
        low, high = LANE_CUTS[block]
        parts = []
        for h in range(heads):
            wide = jnp.where(used, wide_refs[h, :, block * 256 : block * 256 + 256], 0.0)
            near = wide.astype(LOW).astype(F32)
            parts += [near, wide - near]
        got = product(jnp.concatenate(parts, axis=0).astype(LOW), pick[...])
        for h in range(heads):
            spread_s[h, :, low:high] += got[112 * h : 112 * h + 56] + got[112 * h + 56 : 112 * h + 112]
    left = 7 - lax.broadcasted_iota(jnp.int32, (8, RELP), 0)
    for h in range(heads):
        total = jnp.zeros((8, RELP), F32)
        for hi in range(WH):
            total += pltpu.roll(spread_s[h, 8 * hi : 8 * hi + 8, :], ((6 - hi) * 13 - 1) % RELP, 1)
        for bit in range(3):
            total = jnp.where(((left >> bit) & 1) == 1, pltpu.roll(total, 1 << bit, 1), total)
        out_ref[pl.ds(at + h, 1), 0:RELP] = jnp.sum(total, axis=0, keepdims=True)


def shrink_kernel(wide_ref, p0, p1, p2, out_ref, spread_s):
    shrunk(wide_ref, (p0, p1, p2), spread_s, out_ref, 0)


def shrink_bias(wide, picks, after):
    return run(
        shrink_kernel,
        [(wide, WHOLE)] + [(p, WHOLE) for p in picks],
        [(shaped(GHEADS, RELP), WHOLE)],
        1.4, 12,
        scratch=[pltpu.VMEM((GHEADS, 56, RELP), F32)],
        after=after,
    )[0]


def attend_kernel(
    pair, part_ref, a1_ref, wa_ref, wb_ref, qvb_ref, bias_ref, rf_ref, rft_ref,
    p_ref, qt_ref, k_ref, vt_ref, o_ref, li_ref,
    q_s, ka_s, v_s, s_s, acc_s, p_s, p_sem,
):
    step = pl.program_id(0)
    e = step % GHEADS
    slot = step % 2

    def away(at):
        return pltpu.make_async_copy(p_s.at[at % 2], p_ref.at[at], p_sem.at[at % 2])

    @pl.when(step >= 2)
    def _():
        away(step - 2).wait()

    lane = lax.broadcasted_iota(jnp.int32, (WIN, 128), 1) // HD

    def begin(w_ref, group):
        cols = pl.ds(pl.multiple_of((part_ref[0] ^ group) * 128, 128), 128)
        for w in range(2):
            qkv = product(a1_ref[w], w_ref[...])
            q = (qkv[:, :128] + qvb_ref[0:1, cols]) * (SCALE * LOG2E)
            k = qkv[:, 128:256]
            v = qkv[:, 256:384] + qvb_ref[1:2, cols]
            q_s[w] = q
            v_s[w] = v
            qt_ref[0, w] = q.T.astype(LOW)
            k_ref[0, w] = k.astype(LOW)
            vt_ref[0, w] = v.T.astype(LOW)
            ka_s[w, 0:128, :] = k.T.astype(LOW)
            ka_s[w, 128:256, :] = rft_ref[w]
            acc_s[w] = jnp.zeros((WIN, 256), F32)

    @pl.when(step == 0)
    def _():
        begin(wa_ref, 2 * pair)

    @pl.when(step == GHEADS)
    def _():
        begin(wb_ref, 2 * pair + 1)

    mine = lane == e
    for w in range(2):
        q_wide = jnp.concatenate([jnp.where(mine, q_s[w], 0.0).astype(LOW), rf_ref[w]], axis=1)
        s_s[w] = product(q_wide, ka_s[w])

    for w in range(2):
        for start, count in ROW_CUTS:
            rows = slice(start, start + count)
            scores = s_s[w, rows, :] + bias_ref[0, rows, :]
            top = jnp.max(scores, axis=1, keepdims=True)
            p_s[slot, w, rows, :] = jnp.exp2(scores - top).astype(LOW)
        v_wide = jnp.concatenate(
            [jnp.where(mine, v_s[w], 0.0).astype(LOW), jnp.where(mine, 1.0, 0.0).astype(LOW)], axis=1
        )
        acc_s[w] += product(p_s[slot, w], v_wide)
    away(step).start()

    @pl.when(e == GHEADS - 1)
    def _():
        for w in range(2):
            inverse = 1.0 / acc_s[w, :, 128:256]
            li_ref[0, w] = inverse
            o_ref[0, w] = acc_s[w, :, 0:128] * inverse

    @pl.when(step == 2 * GHEADS - 1)
    def _():
        away(step - 1).wait()
        away(step).wait()


def by_group(*dims):
    return pl.BlockSpec((1, *dims), lambda e: (e // GHEADS,) + (0,) * len(dims))


def by_head(*dims):
    return pl.BlockSpec((1, *dims), lambda e: (e,) + (0,) * len(dims))


def attend(pair, part, a1, weights, qvb, bias, rf, rft, after):
    rows, turned = by_group(2, WIN, 128), by_group(2, 128, WIN)
    return run(
        functools.partial(attend_kernel, pair),
        [
            (part, SCALAR), (a1, WHOLE), (weights[0], WHOLE), (weights[1], WHOLE), (qvb, WHOLE),
            (bias, by_head(WIN, WIN)), (rf, WHOLE), (rft, WHOLE),
        ],
        [
            (pinned(pltpu.HBM, 2 * GHEADS, 2, WIN, WIN, kind=LOW), FAR),
            (pinned(pltpu.HBM, 2, 2, 128, WIN, kind=LOW), turned),
            (pinned(pltpu.HBM, 2, 2, WIN, 128, kind=LOW), rows),
            (pinned(pltpu.HBM, 2, 2, 128, WIN, kind=LOW), turned),
            (shaped(2, 2, WIN, 128), rows),
            (shaped(2, 2, WIN, 128), rows),
        ],
        11, 16,
        grid=(2 * GHEADS,),
        scratch=[
            pltpu.VMEM((2, WIN, 128), F32),
            pltpu.VMEM((2, 256, WIN), LOW),
            pltpu.VMEM((2, WIN, 128), F32),
            pltpu.VMEM((2, WIN, WIN), F32),
            pltpu.VMEM((2, WIN, 256), F32),
            pltpu.VMEM((2, 2, WIN, WIN), LOW),
            pltpu.SemaphoreType.DMA((2,)),
        ],
        after=after,
    )


def attend_back_kernel(
    at, dop_ref, nd_ref, p_ref, qt_ref, k_ref, vt_ref, a1t_ref, gp_ref,
    dw_ref, wide_ref, low_ref, cs_ref,
    dopt_s, va_s, dp_s, ds_s, dq_s, dkt_s, dvt_s, db_s, p_s, p_sem, a1t_s, a1t_sem,
):
    e = pl.program_id(0)

    def near(head):
        return pltpu.make_async_copy(p_ref.at[GHEADS * at + head], p_s.at[head % 2], p_sem.at[head % 2])

    later = pltpu.make_async_copy(a1t_ref, a1t_s, a1t_sem)

    @pl.when(e == 0)
    def _():
        near(e).start()
        later.start()

    @pl.when(e + 1 < GHEADS)
    def _():
        near(e + 1).start()

    slot = e % 2
    lane = lax.broadcasted_iota(jnp.int32, (WIN, 128), 1) // HD

    @pl.when(e == 0)
    def _():
        for w in range(2):
            va_s[w, 0:128, :] = vt_ref[0, w]
            va_s[w, 128:256, :] = jnp.ones((128, WIN), LOW)
            dopt_s[w] = dop_ref[0, w].astype(F32).T.astype(LOW)
            dq_s[w] = jnp.zeros((WIN, 128), F32)

    mine = lane == e
    first = pl.multiple_of(HD * e, HD)
    own = pl.ds(first, HD)
    for w in range(2):
        wide = jnp.concatenate(
            [jnp.where(mine, ref[0, w], jnp.zeros((WIN, 128), LOW)) for ref in (dop_ref, nd_ref)], axis=1
        )
        dp_s[w] = product(wide, va_s[w])
    near(e).wait()
    for w in range(2):
        dvt_s[w, own, :] = product(dopt_s[w, own, :], p_s[slot, w])
    for start, count in ROW_CUTS:
        rows = slice(start, start + count)
        one = p_s[slot, 0, rows, :].astype(F32) * dp_s[0, rows, :]
        two = p_s[slot, 1, rows, :].astype(F32) * dp_s[1, rows, :]
        db_s[rows, 0:WIN] = one + two
        ds_s[0, rows, :] = one.astype(LOW)
        ds_s[1, rows, :] = two.astype(LOW)
    for w in range(2):
        dkt_s[w, own, :] = product(qt_ref[0, w, own, :], ds_s[w])
        k_mine = jnp.where(mine, k_ref[0, w], jnp.zeros((WIN, 128), LOW))
        dq_s[w] += product(ds_s[w], k_mine)
    inside = lax.broadcasted_iota(jnp.int32, (8, 512), 1) < WIN
    for hi in range(WH):
        own_rows = slice(8 * hi, 8 * hi + 8)
        wide_ref[0, own_rows, :] = jnp.zeros((8, 768), F32)
        for base in (0, 128, 256):
            total = jnp.zeros((8, 512), F32)
            for ti in range(WT):
                lane_base, by = lanes_of(ti)
                if lane_base != base:
                    continue
                first_row = 49 * ti + 7 * hi
                tile = jnp.where(inside, db_s[first_row : first_row + 8, :], 0.0)
                total += pltpu.roll(tile, by, 1) if by else tile
            wide_ref[0, own_rows, base : base + 512] += total

    @pl.when(e == GHEADS - 1)
    def _():
        sum_q = jnp.zeros((1, 128), F32)
        sum_v = jnp.zeros((1, 128), F32)
        grad = jnp.zeros((D, 384), F32)
        later.wait()
        for w in range(2):
            dq = dq_s[w] * SCALE
            dk = (dkt_s[w] * (1.0 / LOG2E)).T
            dv = dvt_s[w].T
            sum_q += jnp.sum(dq, axis=0, keepdims=True)
            sum_v += jnp.sum(dv, axis=0, keepdims=True)
            low = jnp.concatenate([dq, dk, dv], axis=1).astype(LOW)
            low_ref[w] = low
            grad += product(a1t_s[w], low)
        dw_ref[:, 0:384] = grad.astype(LOW)
        dw_ref[:, 384:512] = gp_ref[0]
        cs_ref[0:1, :] = sum_q
        cs_ref[1:2, :] = sum_v


def attend_back(at, dop, nd, kept, a1t, gproj, after):
    p, qt, k, vt, _, _ = kept
    dop, nd, qt, k, vt, a1t, gproj = (
        pltpu.with_memory_space_constraint(a, pltpu.HBM) for a in (dop, nd, qt, k, vt, a1t, gproj)
    )

    def group(*dims):
        return pl.BlockSpec((1, *dims), lambda e: (at,) + (0,) * len(dims))

    rows, turned = group(2, WIN, 128), group(2, 128, WIN)
    return run(
        functools.partial(attend_back_kernel, at),
        [
            (dop, rows), (nd, rows),
            (pltpu.with_memory_space_constraint(p, pltpu.HBM), FAR),
            (qt, turned), (k, rows), (vt, turned), (a1t, FAR), (gproj, group(D, 128)),
        ],
        [
            (shaped(D, 512, kind=LOW), held(D, 512)),
            (shaped(GHEADS, 56, 768), by_head(56, 768)),
            (shaped(2, WIN, 384, kind=LOW), held(2, WIN, 384)),
            (shaped(2, 128), held(2, 128)),
        ],
        6, 16,
        grid=(GHEADS,),
        scratch=[
            pltpu.VMEM((2, 128, WIN), LOW),
            pltpu.VMEM((2, 256, WIN), LOW),
            pltpu.VMEM((2, WIN, WIN), F32),
            pltpu.VMEM((2, WIN, WIN), LOW),
            pltpu.VMEM((2, WIN, 128), F32),
            pltpu.VMEM((2, 128, WIN), F32),
            pltpu.VMEM((2, 128, WIN), F32),
            pltpu.VMEM((400, 512), F32),
            pltpu.VMEM((2, 2, WIN, WIN), LOW),
            pltpu.SemaphoreType.DMA((2,)),
            pltpu.VMEM((2, D, WIN), LOW),
            pltpu.SemaphoreType.DMA(()),
        ],
        after=after,
    )


def gelu_parts(v):
    size = jnp.abs(v)
    t = 1.0 / (1.0 + (0.3275911 * 0.7071067811865476) * size)
    bell = jnp.exp2(v * v * (-0.5 * LOG2E))
    poly = t * (0.127414796 + t * (-0.142248368 + t * (0.7107068705 + t * (-0.7265760135 + t * 0.5307027145))))
    tail = poly * bell
    phi = jnp.where(v >= 0.0, 1.0 - tail, tail)
    return v * phi, phi + v * bell * 0.3989422804014327


def norm_back(values, dy, gain):
    vhat, rstd = normed(values)
    scaled = dy * gain
    dv = rstd * (
        scaled - jnp.mean(scaled, -1, keepdims=True) - vhat * jnp.mean(scaled * vhat, -1, keepdims=True)
    )
    return dv, jnp.sum(dy * vhat, axis=0, keepdims=True), jnp.sum(dy, axis=0, keepdims=True)


ROWS = 2 * WIN


def middle_kernel(
    part_ref, on_ref, of_ref, lin_ref, lif_ref, x_ref, cot_ref, tb_ref, gain_ref, hb_ref,
    u0, u1, u2, u3, w0, w1, w2, w3,
    out_ref, dafter_ref, dn_ref, df_ref, nn_ref, nf_ref, gpn_ref, gpf_ref,
    odd_up, odd_down, even_up, even_down, sums_ref, ghb_ref,
    up_s, down_s, after_s, a2_s, a2t_s, g_s, gt_s, mix_s, da2_s, h_s, d_s, act_s, dh_s,
):
    step = pl.program_id(0)
    r = (2 * step + 1) % 5
    ups, downs = (u0, u1, u2, u3), (w0, w1, w2, w3)

    @pl.when(step == 0)
    def _():
        cot = jnp.concatenate([cot_ref[0], cot_ref[1]], axis=0)
        g_s[...] = cot.astype(LOW)
        gt_s[...] = cot.T.astype(LOW)
        weight = jnp.concatenate([u[:, 0:128] for u in ups], axis=1)
        lows = []
        for w in range(2):
            mixed = jnp.concatenate([on_ref[0, w], on_ref[1, w], of_ref[0, w], of_ref[1, w]], axis=1).astype(LOW)
            mix_s[w] = mixed
            after = x_ref[w] + product(mixed, weight, NT) + tb_ref[1:2, :]
            after_s[w] = after
            vhat, _ = normed(after)
            lows.append(vhat * gain_ref[1:2, :] + tb_ref[2:3, :])
            out_ref[WIN * w : WIN * w + WIN, :] = after + tb_ref[3:4, :]
        a2 = jnp.concatenate(lows, axis=0)
        a2_s[...] = a2.astype(LOW)
        a2t_s[...] = a2.T.astype(LOW)
        da2_s[...] = jnp.zeros((ROWS, D), F32)

    for i in range(PARTS):

        @pl.when(r == i)
        def _():
            up_s[...] = ups[i][:, 128:640]
            down_s[...] = downs[i][...]

    up = up_s[...]
    down = down_s[...]
    h_s[...] = product(a2_s[...], up)
    d_s[...] = product(g_s[...], down)
    for cut in range(0, 512, 128):
        cols = slice(cut, cut + 128)
        line = hb_ref[r ^ part_ref[0], :, cols]
        sums = jnp.zeros((1, 128), F32)
        for start in range(0, ROWS, 112):
            rows = slice(start, start + 112)
            act, slope = gelu_parts(h_s[rows, cols] + line)
            act_s[rows, cols] = act.astype(LOW)
            grad = d_s[rows, cols] * slope
            sums += jnp.sum(grad, axis=0, keepdims=True)
            dh_s[rows, cols] = grad.astype(LOW)
        ghb_ref[r ^ part_ref[0], :, cols] = sums
    gup = product(a2t_s[...], dh_s[...]).astype(LOW)
    gdown = product(gt_s[...], act_s[...]).astype(LOW)

    @pl.when(step < 2)
    def _():
        odd_up[0] = gup
        odd_down[0] = gdown

    @pl.when(step >= 2)
    def _():
        even_up[0] = gup
        even_down[0] = gdown

    out_ref[...] += product(act_s[...], down, NT)
    da2_s[...] += product(dh_s[...], up, NT)

    @pl.when(step == PARTS - 1)
    def _():
        weight = jnp.concatenate([u[:, 0:128] for u in ups], axis=1)
        grad = jnp.zeros((D, D), F32)
        sums = [jnp.zeros((1, D), F32) for _ in range(4)]
        for w in range(2):
            own = slice(WIN * w, WIN * w + WIN)
            dv, dgain, doff = norm_back(after_s[w], da2_s[own, :], gain_ref[1:2, :])
            cot = cot_ref[w]
            dafter = cot + dv
            dafter_ref[w] = dafter
            turned = dafter.T.astype(LOW)
            dmix = product(dafter.astype(LOW), weight)
            for i in range(PARTS):
                at = i % 2
                d_ref, n_ref, l_ref, m_ref = (
                    (dn_ref, nn_ref, lin_ref, on_ref) if i < 2 else (df_ref, nf_ref, lif_ref, of_ref)
                )
                dop = (dmix[:, 128 * i : 128 * i + 128] * l_ref[at, w]).astype(LOW)
                d_ref[at, w] = dop
                n_ref[at, w] = (-(dop.astype(F32) * m_ref[at, w])).astype(LOW)
            grad += product(turned, mix_s[w])
            parts = (dgain, doff, jnp.sum(dafter, axis=0, keepdims=True), jnp.sum(cot, axis=0, keepdims=True))
            for i, part in enumerate(parts):
                sums[i] += part
        for i, (ref, at) in enumerate(((gpn_ref, 0), (gpn_ref, 1), (gpf_ref, 0), (gpf_ref, 1))):
            ref[at] = grad[:, 128 * i : 128 * i + 128].astype(LOW)
        for i in range(4):
            sums_ref[i : i + 1, :] = sums[i]


def middle(part, o_near, o_far, li_near, li_far, x, cot, biases, gains, hb, ups, downs):
    wide = (1, D, 512)
    pairs = held(2, 2, WIN, 128)
    return run(
        middle_kernel,
        [(part, SCALAR)]
        + [(a, WHOLE) for a in (o_near, o_far, li_near, li_far, x, cot, biases, gains, hb)]
        + [(a, WHOLE) for a in (*ups, *downs)],
        [
            (shaped(ROWS, D), held(ROWS, D)), (shaped(2, WIN, D), held(2, WIN, D)),
            *[(pinned(pltpu.HBM, 2, 2, WIN, 128, kind=LOW), pairs)] * 4,
            (pinned(pltpu.HBM, 2, D, 128, kind=LOW), held(2, D, 128)), (pinned(pltpu.HBM, 2, D, 128, kind=LOW), held(2, D, 128)),
            *[(shaped(2, D, 512, kind=LOW), pl.BlockSpec(wide, lambda s: (jnp.minimum(s, 1), 0, 0)))] * 2,
            *[(shaped(2, D, 512, kind=LOW), pl.BlockSpec(wide, lambda s: (jnp.maximum(s - 2, 0), 0, 0)))] * 2,
            (shaped(4, D), held(4, D)), (shaped(PARTS, 1, 512), held(PARTS, 1, 512)),
        ],
        24, 24,
        grid=(PARTS,),
        scratch=[
            pltpu.VMEM((D, 512), LOW), pltpu.VMEM((D, 512), LOW),
            pltpu.VMEM((2, WIN, D), F32),
            pltpu.VMEM((ROWS, D), LOW), pltpu.VMEM((D, ROWS), LOW),
            pltpu.VMEM((ROWS, D), LOW), pltpu.VMEM((D, ROWS), LOW),
            pltpu.VMEM((2, WIN, D), LOW),
            pltpu.VMEM((ROWS, D), F32),
            pltpu.VMEM((ROWS, 512), F32), pltpu.VMEM((ROWS, 512), F32),
            pltpu.VMEM((ROWS, 512), LOW), pltpu.VMEM((ROWS, 512), LOW),
        ],
    )


def last_kernel(
    part_ref, x_ref, dafter_ref, gain_ref, l0, l1, l2, l3, w0, w1, w2, w3,
    c0, c1, c2, c3, two_ref, ghb_ref, wide_ref, p0, p1, p2, e1, e2, e3,
    gx_ref, pack_ref, spread_s, pack_s,
):
    sums = [jnp.zeros((1, D), F32) for _ in range(2)]
    for w in range(2):
        da1 = jnp.zeros((WIN, D), F32)
        for low, wt in ((l0, w0), (l1, w1), (l2, w2), (l3, w3)):
            da1 += product(low[w], wt[...], NT)
        dv, dgain, doff = norm_back(x_ref[w], da1, gain_ref[0:1, :])
        gx_ref[w] = dafter_ref[w] + dv
        sums[0] += dgain
        sums[1] += doff
    cols = slice(RELP, PACK)
    pack_s[0:1, cols] = sums[0]
    pack_s[1:2, cols] = sums[1]
    pack_s[2:6, cols] = two_ref[...]
    for group, c in enumerate((c0, c1, c2, c3)):
        own = pl.ds(pl.multiple_of(RELP + (part_ref[0] ^ group) * 128, 128), 128)
        pack_s[6:8, own] = c[...]
    for i in range(PARTS):
        pack_s[8 + i : 9 + i, cols] = ghb_ref[i]
    pack_s[12:16, cols] = jnp.zeros((4, D), F32)
    for group, rows in enumerate((e1, e2, e3)):
        for h in range(GHEADS):
            pack_s[pl.ds((part_ref[0] ^ (group + 1)) * GHEADS + h, 1), 0:RELP] = rows[h : h + 1, :]
    shrunk(wide_ref, (p0, p1, p2), spread_s, pack_s, part_ref[0] * GHEADS)
    pack_ref[...] = pack_s[...].astype(LOW)


def swap(values, axis, distance):
    count = lax.axis_size(axis)
    return lax.ppermute(values, axis, [(i, i ^ distance) for i in range(count)])


def bits_of(axis):
    return (lax.axis_size(axis) - 1).bit_length()


def interleaved(own, other, upper):
    place = jnp.arange(2, dtype=jnp.int32).reshape(1, 2, *(1,) * (own.ndim - 1))
    mine = place == upper.astype(jnp.int32)
    return jnp.where(mine, own[:, None], other[:, None]).reshape(-1, *own.shape[1:])


def upper_of(axis, bit):
    return (lax.axis_index(axis) >> bit) % 2 == 1


def gathered(blocks, bits):
    for bit in bits:
        blocks = interleaved(blocks, swap(blocks, "dp", 1 << bit), upper_of("dp", bit))
    return blocks


def flat(blocks):
    return blocks.reshape(-1, blocks.shape[-1])


def half(total, bit, mine):
    pairs = total.reshape(-1, 2, *total.shape[1:])
    return jnp.where(upper_of("dp", bit) == mine, pairs[:, 1], pairs[:, 0])


def halves(total, bit):
    return half(total, bit, False).astype(LOW), half(total, bit, True).astype(F32)


def plus(one, two):
    return one.astype(F32) + two.astype(F32)


def offset_order(rel_index):
    corners = rel_index.reshape(WT, WH, WW, WIN)[::7, ::6, ::6].reshape(2, 2, 2, WT, WH, WW)
    joined = jnp.concatenate([corners[1], corners[0][:, :, 1:]], axis=2)
    joined = jnp.concatenate([joined[1], joined[0][:, :, 1:]], axis=2)
    joined = jnp.concatenate([joined[1], joined[0][:, :, 1:]], axis=2)
    return jnp.pad(joined.reshape(1, REL), ((0, 0), (0, RELP - REL)), constant_values=-1)


def body(
    inputs,
    w_qkv,
    qv_bias,
    w_proj,
    w_fc1,
    fc1_bias,
    w_fc2,
    norm_gains,
    token_biases,
    table,
    shifts,
    rel_index,
    cotangent,
):
    index = lax.axis_index("mp")
    part = index.astype(jnp.int32).reshape(1)
    rows = w_qkv.shape[1]
    x = inputs.reshape(2, WIN, D)
    cot = cotangent.reshape(2, WIN, D)
    high_bits = tuple(reversed(range(1, bits_of("dp"))))
    low_bits = tuple(range(1, bits_of("dp")))

    shard_qkv = w_qkv.transpose(1, 0, 2).reshape(1, rows, 384).astype(LOW)
    (shard_rest,) = run(
        rest_kernel,
        [(a, WHOLE) for a in (w_proj.T, w_fc1, w_fc2.T)],
        [(shaped(rows, 1152, kind=LOW), WHOLE)],
        1, 8,
    )
    shard_rest = shard_rest[None]
    qkv_first = gathered(shard_qkv, high_bits[:1])
    qkv_high = gathered(qkv_first, high_bits[1:])
    own = flat(gathered(qkv_high, (0,)))
    qkv_parts = [own, swap(own, "mp", 1)]
    across = swap(own, "mp", 2)
    rest = gathered(shard_rest, high_bits)
    up_own = gathered(rest[:, :, :640], (0,))
    up_across = swap(up_own, "mp", 2)
    down_across = swap(rest[:, :, 640:], "mp", 2)
    places = jnp.arange(WIN, dtype=jnp.int32)
    places = jnp.stack([places // (WH * WW), places // WW % WH, places % WW])
    order = offset_order(once(rel_index, qkv_first))
    column = jnp.arange(768, dtype=jnp.int32)
    lane_row = jnp.where(
        column < 15 * 49, column // 49 * 169 + column % 49 // 7 * 13 + column % 7, -1
    )
    a1, a1t, rf, rft = run(
        first_norm_kernel,
        [(part, SCALAR), (shifts, SCALAR)] + [(a, WHOLE) for a in (x, norm_gains, token_biases, places)],
        [
            (shaped(2, WIN, D, kind=LOW), WHOLE), (pinned(pltpu.HBM, 2, D, WIN, kind=LOW), WHOLE),
            (shaped(2, WIN, 128, kind=LOW), WHOLE), (shaped(2, 128, WIN, kind=LOW), WHOLE),
        ],
        2, 16,
        after=(qkv_first,),
    )
    row_offsets, *picks = run(
        rows_from_table_kernel,
        [(a, WHOLE) for a in (order, table.T, lane_row.reshape(1, 768), lane_row.reshape(768, 1))],
        [(shaped(HEADS, RELP), WHOLE)]
        + [(shaped(high - low, 256, kind=LOW), WHOLE) for low, high in LANE_CUTS]
        + [(shaped(256, high - low, kind=LOW), WHOLE) for low, high in LANE_CUTS],
        4, 20,
        after=(qkv_high,),
    )
    out_picks, back_picks = picks[:3], picks[3:]
    near_bias = expand_bias(0, part, row_offsets, out_picks, (qkv_high,))
    near = attend(0, part, a1, qkv_parts[:2], qv_bias, near_bias, rf, rft, (rest,))
    across = once(across, near[4])
    qkv_parts += [across, swap(across, "mp", 1)]
    down_pair = jnp.stack([rest[:, :, 640:], once(down_across, near[4])], axis=0)
    down_other = swap(down_pair, "dp", 1)
    down_own, down_across = (
        interleaved(down_pair[i], down_other[i], upper_of("dp", 0)) for i in range(2)
    )
    far_bias = expand_bias(1, part, row_offsets, out_picks, (near[4], up_own, down_pair))
    far = attend(1, part, a1, qkv_parts[2:], qv_bias, far_bias, rf, rft, (up_own,))
    up_parts = [flat(up_own), flat(swap(up_own, "mp", 1)), flat(up_across), flat(swap(once(up_across, far[4]), "mp", 1))]
    down_parts = [
        flat(down_own), flat(swap(down_own, "mp", 1)), flat(down_across), flat(swap(down_across, "mp", 1))
    ]
    (
        out, dafter, dop_near, dop_far, nd_near, nd_far, gp_near, gp_far,
        odd_up, odd_down, even_up, even_down, sums_two, g_hb,
    ) = middle(
        part, near[4], far[4], near[5], far[5], x, cot, token_biases, norm_gains, fc1_bias.reshape(PARTS, 1, 512), up_parts, down_parts
    )

    three, wide3, low3, col3 = attend_back(1, dop_far, nd_far, far, a1t, gp_far, ())
    got_up = swap(odd_up, "mp", 1).reshape(2, -1, rows, 512)
    got_down = swap(odd_down, "mp", 1).reshape(2, -1, rows, 512)
    even_up = even_up.reshape(2, -1, rows, 512)
    even_down = even_down.reshape(2, -1, rows, 512)
    up_send = plus(even_up[1], got_up[1]).astype(LOW)
    turned = [a.transpose(1, 0, 2, 3) for a in (even_down, got_down)]
    down_send = plus(*(half(a, 0, False) for a in turned)).astype(LOW)
    two, wide2, low2, col2 = attend_back(0, dop_far, nd_far, far, a1t, gp_far, (up_send, down_send, three))
    up_sum = plus(plus(even_up[0], got_up[0]), swap(up_send, "mp", 2))
    down_sum = plus(plus(*(half(a, 0, True) for a in turned)), swap(down_send, "dp", 1))
    far_sum = plus(two, swap(three, "mp", 1)).astype(LOW)
    one, wide1, low1, col1 = attend_back(1, dop_near, nd_near, near, a1t, gp_near, (far_sum,))
    far_sum = swap(far_sum, "mp", 2)
    up_send, up_keep = halves(up_sum, 0)
    down_send, down_keep = down_sum[:, 1].astype(LOW), down_sum[:, 0]
    zero, wide0, low0, col0 = attend_back(0, dop_near, nd_near, near, a1t, gp_near, (up_send, down_send, one))
    up_sum = plus(up_keep, swap(up_send, "dp", 1))
    down_sum = plus(down_keep, swap(down_send, "mp", 2))
    total = plus(plus(zero, swap(one, "mp", 1)), far_sum).reshape(-1, rows, 512)
    rows_by = [shrink_bias(w, back_picks, ()) for w in (wide1, wide2, wide3)]
    send, keep = halves(total, 0)
    grad_x, pack = run(
        last_kernel,
        [(part, SCALAR)]
        + [
            (a, WHOLE)
            for a in (
                x, dafter, norm_gains, low0, low1, low2, low3, *qkv_parts, col0, col1, col2, col3,
                sums_two, g_hb, wide0, *back_picks, *rows_by,
            )
        ],
        [(shaped(2, WIN, D), WHOLE), (shaped(HEADS, PACK, kind=LOW), WHOLE)],
        4, 20,
        scratch=[pltpu.VMEM((GHEADS, 56, RELP), F32), pltpu.VMEM((HEADS, PACK), F32)],
        after=(send, up_sum, down_sum),
    )
    summed = jnp.concatenate([up_sum, down_sum], axis=2)
    total = plus(keep, swap(send, "dp", 1))
    mp_steps = [("mp", 1 << bit) for bit in range(bits_of("mp"))]
    steps = mp_steps + [("dp", 1 << bit) for bit in range(bits_of("dp"))]
    queue = [("qkv", bit) for bit in low_bits] + [("mlp", bit) for bit in low_bits]
    queue.sort(key=lambda item: (item[1], item[0] == "qkv"))
    state = {"qkv": total, "mlp": summed}
    pending = None
    for place, (axis, distance) in enumerate(steps):
        mine = pack.astype(LOW)
        theirs = swap(mine, axis, distance)
        if pending is not None:
            name, keep, got = pending
            state[name] = plus(keep, once(got, mine))
            pending = None
        if place >= 1 and queue:
            name, bit = queue.pop(0)
            send, keep = halves(once(state[name], mine), bit)
            theirs = once(theirs, send)
            pending = (name, keep, swap(send, "dp", 1 << bit))
        pack = plus(mine, theirs)
    if pending is not None:
        state[pending[0]] = plus(pending[1], pending[2])
    for name, bit in queue:
        send, keep = halves(state[name], bit)
        state[name] = plus(keep, swap(send, "dp", 1 << bit))
    own_qkv = state["qkv"].reshape(rows, 512)
    own_mlp = state["mlp"].reshape(rows, 1024)
    grad_qkv, grad_proj = run(
        unpack_qkv_kernel,
        [(own_qkv, WHOLE)],
        [(pinned(pltpu.HBM, *dims), held(*dims)) for dims in ((3, rows, 128), (rows, 128))],
        1, 8,
        grid=(1,),
    )
    grad_up, grad_down = run(
        unpack_mlp_kernel,
        [(own_mlp, WHOLE)],
        [(pinned(pltpu.HBM, rows, 512), held(rows, 512))] * 2,
        1, 8,
        grid=(1,),
    )
    grad_table, grad_gains, grad_biases, grad_pair, grad_hidden = run(
        rows_to_table_kernel,
        [(order, WHOLE), (pack, WHOLE)],
        [(shaped(*dims), WHOLE) for dims in ((HEADS, REL), (2, D), (4, D), (2, D), (4, D))],
        4, 20,
        after=(grad_qkv, grad_proj, grad_up, grad_down),
    )
    return (
        out.reshape(inputs.shape),
        grad_x.reshape(inputs.shape),
        grad_qkv,
        grad_pair,
        grad_proj.T,
        grad_up,
        grad_hidden.reshape(FF),
        grad_down.T,
        grad_gains,
        grad_biases,
        grad_table.T,
    )


def solution(mesh):
    placed = (
        P(("dp", "mp"), None),
        P(None, "dp", "mp"),
        P(),
        P("mp", "dp"),
        P("dp", "mp"),
        P(),
        P("mp", "dp"),
        P(),
        P(),
        P(),
        P("dp", None),
        P(),
        P(("dp", "mp"), None),
    )
    return jax.shard_map(
        body,
        mesh=mesh,
        in_specs=placed,
        out_specs=(
            P(("dp", "mp"), None),
            P(("dp", "mp"), None),
            P(None, "dp", "mp"),
            P(),
            P("mp", "dp"),
            P("dp", "mp"),
            P(),
            P("mp", "dp"),
            P(),
            P(),
            P(),
        ),
        check_vma=False,
    )
```

```python
import functools

import jax
import jax.numpy as jnp
from jax import lax
from jax.experimental import pallas as pl
from jax.experimental.pallas import tpu as pltpu
from jax.sharding import PartitionSpec as P

D = 512
HEADS = 16
HD = 32
FF = 2048
WT = 8
WH = 7
WW = 7
GT = 16
GH = 14
GW = 14
WIN = 392
REL = 2535
RELP = 2560
PACK = RELP + D
WINS = 8
PARTS = 4
GHEADS = HEADS // PARTS
LOG2E = 1.4426950408889634
SCALE = HD ** (-0.5)
LOW = jnp.bfloat16
F32 = jnp.float32
NN = (((1,), (0,)), ((), ()))
NT = (((1,), (1,)), ((), ()))
ROW_CUTS = ((0, 64), (64, 64), (128, 64), (192, 64), (256, 64), (320, 72))
LANE_CUTS = ((0, 1024), (768, 1920), (1664, 2560))


def product(left, right, dims=NN):
    return lax.dot_general(left, right, dims, preferred_element_type=F32)


def shaped(*dims, kind=F32):
    return jax.ShapeDtypeStruct(dims, kind)


def cost(micros):
    return pl.CostEstimate(flops=int(micros * 1e9), bytes_accessed=int(micros * 3.6e6), transcendentals=0)


WHOLE = pl.BlockSpec(memory_space=pltpu.VMEM)
ANYWHERE = pl.BlockSpec(memory_space=pl.ANY)
SCALAR = pl.BlockSpec(memory_space=pltpu.SMEM)
FAR = pl.BlockSpec(memory_space=pltpu.HBM)


def run(kernel, ins, outs, micros, mib, grid=(), scratch=(), after=()):
    count = len(ins)

    def inner(*refs):
        kernel(*refs[:count], *refs[count + len(after) :])

    return pl.pallas_call(
        inner,
        grid=grid,
        out_shape=[o[0] for o in outs],
        in_specs=[i[1] for i in ins] + [ANYWHERE] * len(after),
        out_specs=[o[1] for o in outs],
        scratch_shapes=list(scratch),
        cost_estimate=cost(micros),
        compiler_params=pltpu.CompilerParams(vmem_limit_bytes=mib << 20),
    )(*[i[0] for i in ins], *after)


def pinned(space, *dims, kind=F32):
    return space(dims, kind)


def once(value, *others):
    return lax.optimization_barrier((value, *others))[0]


def held(*dims):
    return pl.BlockSpec(dims, lambda e: (0,) * len(dims))


def normed(values):
    centred = values - jnp.mean(values, -1, keepdims=True)
    rstd = lax.rsqrt(jnp.mean(centred * centred, -1, keepdims=True) + 1e-05)
    return centred * rstd, rstd


def first_norm_kernel(part_ref, shift_ref, x_ref, gain_ref, tb_ref, place_ref, a1_ref, a1t_ref, rf_ref, rft_ref):
    codes = lax.broadcasted_iota(jnp.int32, (128, WIN), 0)
    for w in range(2):
        window = (2 * part_ref[0] + w) % WINS
        region = jnp.zeros((1, WIN), jnp.int32)
        for axis, (length, size, along) in enumerate(
            ((WT, GT, window // 4), (WH, GH, window // 2 % 2), (WW, GW, window % 2))
        ):
            cell = place_ref[axis : axis + 1, :] + along * length
            halves_in = (cell >= size - length).astype(jnp.int32)
            shifted = (cell >= size - shift_ref[0, axis]).astype(jnp.int32)
            region = region * 3 + halves_in + shifted
        vhat, _ = normed(x_ref[w])
        a1 = vhat * gain_ref[0:1, :] + tb_ref[0:1, :]
        a1_ref[w] = a1.astype(LOW)
        a1t_ref[w] = a1.T.astype(LOW)
        differs = jnp.where(codes == region, 0.0, 1.0)
        rft_ref[w] = differs.astype(LOW)
        rf_ref[w] = ((1.0 - differs.T) * -1e30).astype(LOW)


def rest_kernel(proj_ref, up_ref, down_ref, out_ref):
    out_ref[...] = jnp.concatenate([proj_ref[...], up_ref[...], down_ref[...]], axis=1).astype(LOW)


def split3(values):
    high = values.astype(LOW)
    rest = values - high.astype(F32)
    mid = rest.astype(LOW)
    return high, mid, (rest - mid.astype(F32)).astype(LOW)


def rows_from_table_kernel(order_ref, table_ref, lane_ref, column_ref, out_ref, *picks):
    table = jnp.concatenate(split3(table_ref[...]), axis=0)
    rows = lax.broadcasted_iota(jnp.int32, (REL, 256), 0)
    for block in range(RELP // 256):
        cols = slice(block * 256, block * 256 + 256)
        picked = jnp.where(rows == order_ref[:, cols], 1.0, 0.0).astype(LOW)
        got = product(table, picked)
        out_ref[:, cols] = (got[:HEADS] + got[HEADS : 2 * HEADS] + got[2 * HEADS :]) * LOG2E
    for block in range(3):
        low, high = LANE_CUTS[block]
        cols = slice(block * 256, block * 256 + 256)
        down = lax.broadcasted_iota(jnp.int32, (high - low, 256), 0) + low
        picks[block][...] = jnp.where(down == lane_ref[:, cols], 1.0, 0.0).astype(LOW)
        across = lax.broadcasted_iota(jnp.int32, (256, high - low), 1) + low
        picks[3 + block][...] = jnp.where(across == column_ref[cols, :], 1.0, 0.0).astype(LOW)


def rows_to_table_kernel(order_ref, pack_ref, out_ref, gains_ref, biases_ref, pair_ref, hidden_ref):
    rows = jnp.concatenate(split3(pack_ref[:, 0:RELP]), axis=0)
    ids = lax.broadcasted_iota(jnp.int32, (256, RELP), 0)
    for start in range(0, REL, 256):
        count = min(256, REL - start)
        picked = jnp.where(ids + start == order_ref[...], 1.0, 0.0).astype(LOW)
        got = product(rows, picked, NT)
        got = got[:HEADS] + got[HEADS : 2 * HEADS] + got[2 * HEADS :]
        out_ref[:, start : start + count] = got[:, :count]
    cols = slice(RELP, PACK)
    for i, at in enumerate((0, 2)):
        gains_ref[i : i + 1, :] = pack_ref[at : at + 1, cols]
    for i, at in enumerate((1, 4, 3, 5)):
        biases_ref[i : i + 1, :] = pack_ref[at : at + 1, cols]
    pair_ref[...] = pack_ref[6:8, cols]
    hidden_ref[...] = pack_ref[8:12, cols]


def unpack_qkv_kernel(qkv_ref, out_ref, proj_ref):
    for i in range(3):
        out_ref[i] = qkv_ref[:, 128 * i : 128 * i + 128]
    proj_ref[...] = qkv_ref[:, 384:512]


def unpack_mlp_kernel(mlp_ref, up_ref, down_ref):
    up_ref[...] = mlp_ref[:, 0:512]
    down_ref[...] = mlp_ref[:, 512:1024]


def lanes_of(ti):
    off = 49 * (7 - ti)
    base = off // 128 * 128
    return base, off - base


def expand_kernel(pair, part_ref, rows_ref, p0, p1, p2, bias_ref, left_s, wide_s):
    group = 2 * pair + pl.program_id(0)
    base_row = (part_ref[0] ^ group) * GHEADS
    back = 7 - lax.broadcasted_iota(jnp.int32, (8, RELP), 0)
    for h in range(GHEADS):
        row = jnp.broadcast_to(rows_ref[pl.ds(base_row + h, 1), :], (8, RELP))
        for bit in range(3):
            row = jnp.where(((back >> bit) & 1) == 1, pltpu.roll(row, RELP - (1 << bit), 1), row)
        for hi in range(WH):
            rolled = pltpu.roll(row, (1 - (6 - hi) * 13) % RELP, 1)
            at = 56 * h + 8 * hi
            left_s[at : at + 8, :] = rolled
    for block, pick in enumerate((p0, p1, p2)):
        low, high = LANE_CUTS[block]
        got = product(left_s[:, low:high].astype(LOW), pick[...])
        for h in range(GHEADS):
            wide_s[h, :, block * 256 : block * 256 + 256] = got[56 * h : 56 * h + 56]
    for h in range(GHEADS):
        for ti in range(WT):
            base, by = lanes_of(ti)
            for hi in range(WH):
                tile = wide_s[h, 8 * hi : 8 * hi + 8, base : base + 512]
                if by:
                    tile = pltpu.roll(tile, 512 - by, 1)
                at = 49 * ti + 7 * hi
                bias_ref[h, at : at + 7, :] = tile[:7, :WIN]


def expand_bias(pair, part, rows, picks, after):
    return run(
        functools.partial(expand_kernel, pair),
        [(part, SCALAR), (rows, WHOLE)] + [(p, WHOLE) for p in picks],
        [(shaped(2 * GHEADS, WIN, WIN), pl.BlockSpec((GHEADS, WIN, WIN), lambda g: (g, 0, 0)))],
        5, 14,
        grid=(2,),
        scratch=[pltpu.VMEM((56 * GHEADS, RELP), F32), pltpu.VMEM((GHEADS, 56, 768), F32)],
        after=after,
    )[0]


def shrunk(wide_refs, picks, spread_s, out_ref, at):
    heads = wide_refs.shape[0]
    used = (lax.broadcasted_iota(jnp.int32, (56, 256), 0) & 7) < 7
    spread_s[...] = jnp.zeros(spread_s.shape, F32)
    for block, pick in enumerate(picks):
        low, high = LANE_CUTS[block]
        parts = []
        for h in range(heads):
            wide = jnp.where(used, wide_refs[h, :, block * 256 : block * 256 + 256], 0.0)
            near = wide.astype(LOW).astype(F32)
            parts += [near, wide - near]
        got = product(jnp.concatenate(parts, axis=0).astype(LOW), pick[...])
        for h in range(heads):
            spread_s[h, :, low:high] += got[112 * h : 112 * h + 56] + got[112 * h + 56 : 112 * h + 112]
    left = 7 - lax.broadcasted_iota(jnp.int32, (8, RELP), 0)
    for h in range(heads):
        total = jnp.zeros((8, RELP), F32)
        for hi in range(WH):
            total += pltpu.roll(spread_s[h, 8 * hi : 8 * hi + 8, :], ((6 - hi) * 13 - 1) % RELP, 1)
        for bit in range(3):
            total = jnp.where(((left >> bit) & 1) == 1, pltpu.roll(total, 1 << bit, 1), total)
        out_ref[pl.ds(at + h, 1), 0:RELP] = jnp.sum(total, axis=0, keepdims=True)


def shrink_kernel(wide_ref, p0, p1, p2, out_ref, spread_s):
    shrunk(wide_ref, (p0, p1, p2), spread_s, out_ref, 0)


def shrink_bias(wide, picks, after):
    return run(
        shrink_kernel,
        [(wide, WHOLE)] + [(p, WHOLE) for p in picks],
        [(shaped(GHEADS, RELP), WHOLE)],
        1.4, 12,
        scratch=[pltpu.VMEM((GHEADS, 56, RELP), F32)],
        after=after,
    )[0]


def attend_kernel(
    pair, part_ref, a1_ref, wa_ref, wb_ref, qvb_ref, bias_ref, rf_ref, rft_ref,
    p_ref, qt_ref, k_ref, vt_ref, o_ref, li_ref,
    q_s, ka_s, v_s, s_s, acc_s, p_s, p_sem,
):
    step = pl.program_id(0)
    e = step % GHEADS
    slot = step % 2

    def away(at):
        return pltpu.make_async_copy(p_s.at[at % 2], p_ref.at[at], p_sem.at[at % 2])

    @pl.when(step >= 2)
    def _():
        away(step - 2).wait()

    lane = lax.broadcasted_iota(jnp.int32, (WIN, 128), 1) // HD

    def begin(w_ref, group):
        cols = pl.ds(pl.multiple_of((part_ref[0] ^ group) * 128, 128), 128)
        for w in range(2):
            qkv = product(a1_ref[w], w_ref[...])
            q = (qkv[:, :128] + qvb_ref[0:1, cols]) * (SCALE * LOG2E)
            k = qkv[:, 128:256]
            v = qkv[:, 256:384] + qvb_ref[1:2, cols]
            q_s[w] = q
            v_s[w] = v
            qt_ref[0, w] = q.T.astype(LOW)
            k_ref[0, w] = k.astype(LOW)
            vt_ref[0, w] = v.T.astype(LOW)
            ka_s[w, 0:128, :] = k.T.astype(LOW)
            ka_s[w, 128:256, :] = rft_ref[w]
            acc_s[w] = jnp.zeros((WIN, 256), F32)

    @pl.when(step == 0)
    def _():
        begin(wa_ref, 2 * pair)

    @pl.when(step == GHEADS)
    def _():
        begin(wb_ref, 2 * pair + 1)

    mine = lane == e
    for w in range(2):
        q_wide = jnp.concatenate([jnp.where(mine, q_s[w], 0.0).astype(LOW), rf_ref[w]], axis=1)
        s_s[w] = product(q_wide, ka_s[w])

    for w in range(2):
        for start, count in ROW_CUTS:
            rows = slice(start, start + count)
            scores = s_s[w, rows, :] + bias_ref[0, rows, :]
            top = jnp.max(scores, axis=1, keepdims=True)
            p_s[slot, w, rows, :] = jnp.exp2(scores - top).astype(LOW)
        v_wide = jnp.concatenate(
            [jnp.where(mine, v_s[w], 0.0).astype(LOW), jnp.where(mine, 1.0, 0.0).astype(LOW)], axis=1
        )
        acc_s[w] += product(p_s[slot, w], v_wide)
    away(step).start()

    @pl.when(e == GHEADS - 1)
    def _():
        for w in range(2):
            inverse = 1.0 / acc_s[w, :, 128:256]
            li_ref[0, w] = inverse
            o_ref[0, w] = acc_s[w, :, 0:128] * inverse

    @pl.when(step == 2 * GHEADS - 1)
    def _():
        away(step - 1).wait()
        away(step).wait()


def by_group(*dims):
    return pl.BlockSpec((1, *dims), lambda e: (e // GHEADS,) + (0,) * len(dims))


def by_head(*dims):
    return pl.BlockSpec((1, *dims), lambda e: (e,) + (0,) * len(dims))


def attend(pair, part, a1, weights, qvb, bias, rf, rft, after):
    rows, turned = by_group(2, WIN, 128), by_group(2, 128, WIN)
    return run(
        functools.partial(attend_kernel, pair),
        [
            (part, SCALAR), (a1, WHOLE), (weights[0], WHOLE), (weights[1], WHOLE), (qvb, WHOLE),
            (bias, by_head(WIN, WIN)), (rf, WHOLE), (rft, WHOLE),
        ],
        [
            (pinned(pltpu.HBM, 2 * GHEADS, 2, WIN, WIN, kind=LOW), FAR),
            (pinned(pltpu.HBM, 2, 2, 128, WIN, kind=LOW), turned),
            (pinned(pltpu.HBM, 2, 2, WIN, 128, kind=LOW), rows),
            (pinned(pltpu.HBM, 2, 2, 128, WIN, kind=LOW), turned),
            (shaped(2, 2, WIN, 128), rows),
            (shaped(2, 2, WIN, 128), rows),
        ],
        11, 16,
        grid=(2 * GHEADS,),
        scratch=[
            pltpu.VMEM((2, WIN, 128), F32),
            pltpu.VMEM((2, 256, WIN), LOW),
            pltpu.VMEM((2, WIN, 128), F32),
            pltpu.VMEM((2, WIN, WIN), F32),
            pltpu.VMEM((2, WIN, 256), F32),
            pltpu.VMEM((2, 2, WIN, WIN), LOW),
            pltpu.SemaphoreType.DMA((2,)),
        ],
        after=after,
    )


def attend_back_kernel(
    at, dop_ref, nd_ref, p_ref, qt_ref, k_ref, vt_ref, a1t_ref, gp_ref,
    dw_ref, wide_ref, low_ref, cs_ref,
    dopt_s, va_s, dp_s, ds_s, dq_s, dkt_s, dvt_s, db_s, p_s, p_sem, a1t_s, a1t_sem,
):
    e = pl.program_id(0)

    def near(head):
        return pltpu.make_async_copy(p_ref.at[GHEADS * at + head], p_s.at[head % 2], p_sem.at[head % 2])

    later = pltpu.make_async_copy(a1t_ref, a1t_s, a1t_sem)

    @pl.when(e == 0)
    def _():
        near(e).start()
        later.start()

    @pl.when(e + 1 < GHEADS)
    def _():
        near(e + 1).start()

    slot = e % 2
    lane = lax.broadcasted_iota(jnp.int32, (WIN, 128), 1) // HD

    @pl.when(e == 0)
    def _():
        for w in range(2):
            va_s[w, 0:128, :] = vt_ref[0, w]
            va_s[w, 128:256, :] = jnp.ones((128, WIN), LOW)
            dopt_s[w] = dop_ref[0, w].astype(F32).T.astype(LOW)
            dq_s[w] = jnp.zeros((WIN, 128), F32)

    mine = lane == e
    first = pl.multiple_of(HD * e, HD)
    own = pl.ds(first, HD)
    for w in range(2):
        wide = jnp.concatenate(
            [jnp.where(mine, ref[0, w], jnp.zeros((WIN, 128), LOW)) for ref in (dop_ref, nd_ref)], axis=1
        )
        dp_s[w] = product(wide, va_s[w])
    near(e).wait()
    for w in range(2):
        dvt_s[w, own, :] = product(dopt_s[w, own, :], p_s[slot, w])
    for start, count in ROW_CUTS:
        rows = slice(start, start + count)
        one = p_s[slot, 0, rows, :].astype(F32) * dp_s[0, rows, :]
        two = p_s[slot, 1, rows, :].astype(F32) * dp_s[1, rows, :]
        db_s[rows, 0:WIN] = one + two
        ds_s[0, rows, :] = one.astype(LOW)
        ds_s[1, rows, :] = two.astype(LOW)
    for w in range(2):
        dkt_s[w, own, :] = product(qt_ref[0, w, own, :], ds_s[w])
        k_mine = jnp.where(mine, k_ref[0, w], jnp.zeros((WIN, 128), LOW))
        dq_s[w] += product(ds_s[w], k_mine)
    inside = lax.broadcasted_iota(jnp.int32, (8, 512), 1) < WIN
    for hi in range(WH):
        own_rows = slice(8 * hi, 8 * hi + 8)
        wide_ref[0, own_rows, :] = jnp.zeros((8, 768), F32)
        for base in (0, 128, 256):
            total = jnp.zeros((8, 512), F32)
            for ti in range(WT):
                lane_base, by = lanes_of(ti)
                if lane_base != base:
                    continue
                first_row = 49 * ti + 7 * hi
                tile = jnp.where(inside, db_s[first_row : first_row + 8, :], 0.0)
                total += pltpu.roll(tile, by, 1) if by else tile
            wide_ref[0, own_rows, base : base + 512] += total

    @pl.when(e == GHEADS - 1)
    def _():
        sum_q = jnp.zeros((1, 128), F32)
        sum_v = jnp.zeros((1, 128), F32)
        grad = jnp.zeros((D, 384), F32)
        later.wait()
        for w in range(2):
            dq = dq_s[w] * SCALE
            dk = (dkt_s[w] * (1.0 / LOG2E)).T
            dv = dvt_s[w].T
            sum_q += jnp.sum(dq, axis=0, keepdims=True)
            sum_v += jnp.sum(dv, axis=0, keepdims=True)
            low = jnp.concatenate([dq, dk, dv], axis=1).astype(LOW)
            low_ref[w] = low
            grad += product(a1t_s[w], low)
        dw_ref[:, 0:384] = grad.astype(LOW)
        dw_ref[:, 384:512] = gp_ref[0]
        cs_ref[0:1, :] = sum_q
        cs_ref[1:2, :] = sum_v


def attend_back(at, dop, nd, kept, a1t, gproj, after):
    p, qt, k, vt, _, _ = kept
    dop, nd, qt, k, vt, a1t, gproj = (
        pltpu.with_memory_space_constraint(a, pltpu.HBM) for a in (dop, nd, qt, k, vt, a1t, gproj)
    )

    def group(*dims):
        return pl.BlockSpec((1, *dims), lambda e: (at,) + (0,) * len(dims))

    rows, turned = group(2, WIN, 128), group(2, 128, WIN)
    return run(
        functools.partial(attend_back_kernel, at),
        [
            (dop, rows), (nd, rows),
            (pltpu.with_memory_space_constraint(p, pltpu.HBM), FAR),
            (qt, turned), (k, rows), (vt, turned), (a1t, FAR), (gproj, group(D, 128)),
        ],
        [
            (shaped(D, 512, kind=LOW), held(D, 512)),
            (shaped(GHEADS, 56, 768), by_head(56, 768)),
            (shaped(2, WIN, 384, kind=LOW), held(2, WIN, 384)),
            (shaped(2, 128), held(2, 128)),
        ],
        6, 16,
        grid=(GHEADS,),
        scratch=[
            pltpu.VMEM((2, 128, WIN), LOW),
            pltpu.VMEM((2, 256, WIN), LOW),
            pltpu.VMEM((2, WIN, WIN), F32),
            pltpu.VMEM((2, WIN, WIN), LOW),
            pltpu.VMEM((2, WIN, 128), F32),
            pltpu.VMEM((2, 128, WIN), F32),
            pltpu.VMEM((2, 128, WIN), F32),
            pltpu.VMEM((400, 512), F32),
            pltpu.VMEM((2, 2, WIN, WIN), LOW),
            pltpu.SemaphoreType.DMA((2,)),
            pltpu.VMEM((2, D, WIN), LOW),
            pltpu.SemaphoreType.DMA(()),
        ],
        after=after,
    )


def gelu_parts(v):
    size = jnp.abs(v)
    t = 1.0 / (1.0 + (0.3275911 * 0.7071067811865476) * size)
    bell = jnp.exp2(v * v * (-0.5 * LOG2E))
    poly = t * (0.127414796 + t * (-0.142248368 + t * (0.7107068705 + t * (-0.7265760135 + t * 0.5307027145))))
    tail = poly * bell
    phi = jnp.where(v >= 0.0, 1.0 - tail, tail)
    return v * phi, phi + v * bell * 0.3989422804014327


def norm_back(values, dy, gain):
    vhat, rstd = normed(values)
    scaled = dy * gain
    dv = rstd * (
        scaled - jnp.mean(scaled, -1, keepdims=True) - vhat * jnp.mean(scaled * vhat, -1, keepdims=True)
    )
    return dv, jnp.sum(dy * vhat, axis=0, keepdims=True), jnp.sum(dy, axis=0, keepdims=True)


ROWS = 2 * WIN


def before_kernel(
    on_ref, of_ref, x_ref, cot_ref, tb_ref, gain_ref, u0, u1, u2, u3,
    after_ref, a2_ref, a2t_ref, g_ref, gt_ref, mix_ref,
):
    weight = jnp.concatenate([u[:, 0:128] for u in (u0, u1, u2, u3)], axis=1)
    lows = []
    for w in range(2):
        mixed = jnp.concatenate([on_ref[0, w], on_ref[1, w], of_ref[0, w], of_ref[1, w]], axis=1).astype(LOW)
        mix_ref[w] = mixed
        after = x_ref[w] + product(mixed, weight, NT) + tb_ref[1:2, :]
        after_ref[w] = after
        vhat, _ = normed(after)
        lows.append(vhat * gain_ref[1:2, :] + tb_ref[2:3, :])
    a2 = jnp.concatenate(lows, axis=0)
    a2_ref[...] = a2.astype(LOW)
    a2t_ref[...] = a2.T.astype(LOW)
    cot = jnp.concatenate([cot_ref[0], cot_ref[1]], axis=0)
    g_ref[...] = cot.astype(LOW)
    gt_ref[...] = cot.T.astype(LOW)


def before(o_near, o_far, x, cot, biases, gains, ups):
    return run(
        before_kernel,
        [(a, WHOLE) for a in (o_near, o_far, x, cot, biases, gains, *ups)],
        [
            (shaped(2, WIN, D), WHOLE), (shaped(ROWS, D, kind=LOW), WHOLE), (shaped(D, ROWS, kind=LOW), WHOLE),
            (shaped(ROWS, D, kind=LOW), WHOLE), (shaped(D, ROWS, kind=LOW), WHOLE), (shaped(2, WIN, D, kind=LOW), WHOLE),
        ],
        4, 16,
    )


def feed_step(
    r, part_ref, a2_ref, a2t_ref, g_ref, gt_ref, hb_ref, up, down,
    out_ref, da2_ref, gup_ref, gdown_ref, ghb_ref, h_s, d_s, act_s, dh_s,
):
    h_s[...] = product(a2_ref[...], up)
    d_s[...] = product(g_ref[...], down)
    for cut in range(0, 512, 128):
        cols = slice(cut, cut + 128)
        line = hb_ref[r ^ part_ref[0], :, cols]
        sums = jnp.zeros((1, 128), F32)
        for start in range(0, ROWS, 112):
            rows = slice(start, start + 112)
            act, slope = gelu_parts(h_s[rows, cols] + line)
            act_s[rows, cols] = act.astype(LOW)
            grad = d_s[rows, cols] * slope
            sums += jnp.sum(grad, axis=0, keepdims=True)
            dh_s[rows, cols] = grad.astype(LOW)
        ghb_ref[0, :, cols] = sums
    gup_ref[0] = product(a2t_ref[...], dh_s[...]).astype(LOW)
    gdown_ref[0] = product(gt_ref[...], act_s[...]).astype(LOW)
    out_ref[...] += product(act_s[...], down, NT)
    da2_ref[...] += product(dh_s[...], up, NT)


def picked_weights(step, ups, downs, up_s, down_s):
    for i in range(2):

        @pl.when(step == i)
        def _():
            up_s[...] = ups[i][:, 128:640]
            down_s[...] = downs[i][...]


def feed_odd_kernel(
    part_ref, a2_ref, a2t_ref, g_ref, gt_ref, hb_ref, ua, ub, wa, wb, after_ref, tb_ref,
    out_ref, da2_ref, gup_ref, gdown_ref, ghb_ref,
    up_s, down_s, *work,
):
    step = pl.program_id(0)

    @pl.when(step == 0)
    def _():
        for w in range(2):
            out_ref[WIN * w : WIN * w + WIN, :] = after_ref[w] + tb_ref[3:4, :]
        da2_ref[...] = jnp.zeros((ROWS, D), F32)

    picked_weights(step, (ua, ub), (wa, wb), up_s, down_s)
    feed_step(
        2 * step + 1, part_ref, a2_ref, a2t_ref, g_ref, gt_ref, hb_ref, up_s[...], down_s[...],
        out_ref, da2_ref, gup_ref, gdown_ref, ghb_ref, *work,
    )


def feed_even_kernel(
    part_ref, a2_ref, a2t_ref, g_ref, gt_ref, hb_ref, ua, ub, wa, wb, after_ref,
    out_in, da2_in, on_ref, of_ref, lin_ref, lif_ref, mix_ref, cot_ref, gain_ref, uc, ud,
    out_ref, gup_ref, gdown_ref, ghb_ref, dafter_ref, dn_ref, df_ref, nn_ref, nf_ref, gpn_ref, gpf_ref, sums_ref,
    up_s, down_s, da2_s, *work,
):
    step = pl.program_id(0)

    @pl.when(step == 0)
    def _():
        out_ref[...] = out_in[...]
        da2_s[...] = da2_in[...]

    picked_weights(step, (ua, ub), (wa, wb), up_s, down_s)
    feed_step(
        2 * step, part_ref, a2_ref, a2t_ref, g_ref, gt_ref, hb_ref, up_s[...], down_s[...],
        out_ref, da2_s, gup_ref, gdown_ref, ghb_ref, *work,
    )

    @pl.when(step == 1)
    def _():
        weight = jnp.concatenate([u[:, 0:128] for u in (ua, uc, ub, ud)], axis=1)
        grad = jnp.zeros((D, D), F32)
        sums = [jnp.zeros((1, D), F32) for _ in range(4)]
        for w in range(2):
            own = slice(WIN * w, WIN * w + WIN)
            dv, dgain, doff = norm_back(after_ref[w], da2_s[own, :], gain_ref[1:2, :])
            cot = cot_ref[w]
            dafter = cot + dv
            dafter_ref[w] = dafter
            turned = dafter.T.astype(LOW)
            dmix = product(dafter.astype(LOW), weight)
            for i in range(PARTS):
                at = i % 2
                d_ref, n_ref, l_ref, m_ref = (
                    (dn_ref, nn_ref, lin_ref, on_ref) if i < 2 else (df_ref, nf_ref, lif_ref, of_ref)
                )
                dop = (dmix[:, 128 * i : 128 * i + 128] * l_ref[at, w]).astype(LOW)
                d_ref[at, w] = dop
                n_ref[at, w] = (-(dop.astype(F32) * m_ref[at, w])).astype(LOW)
            grad += product(turned, mix_ref[w])
            parts = (dgain, doff, jnp.sum(dafter, axis=0, keepdims=True), jnp.sum(cot, axis=0, keepdims=True))
            for i, part in enumerate(parts):
                sums[i] += part
        for i, (ref, at) in enumerate(((gpn_ref, 0), (gpn_ref, 1), (gpf_ref, 0), (gpf_ref, 1))):
            ref[at] = grad[:, 128 * i : 128 * i + 128].astype(LOW)
        for i in range(4):
            sums_ref[i : i + 1, :] = sums[i]


FEED_WORK = [
    pltpu.VMEM((ROWS, 512), F32), pltpu.VMEM((ROWS, 512), F32),
    pltpu.VMEM((ROWS, 512), LOW), pltpu.VMEM((ROWS, 512), LOW),
]
STEP_OUTS = [
    (shaped(2, D, 512, kind=LOW), pl.BlockSpec((1, D, 512), lambda s: (s, 0, 0))),
    (shaped(2, D, 512, kind=LOW), pl.BlockSpec((1, D, 512), lambda s: (s, 0, 0))),
    (shaped(2, 1, 512), pl.BlockSpec((1, 1, 512), lambda s: (s, 0, 0))),
]


def feed_odd(part, known, hb, ups, downs, after, biases):
    return run(
        feed_odd_kernel,
        [(part, SCALAR)] + [(a, WHOLE) for a in (*known, hb, *ups, *downs, after, biases)],
        [(shaped(ROWS, D), held(ROWS, D)), (shaped(ROWS, D), held(ROWS, D)), *STEP_OUTS],
        9, 24,
        grid=(2,),
        scratch=[pltpu.VMEM((D, 512), LOW), pltpu.VMEM((D, 512), LOW), *FEED_WORK],
    )


def feed_even(part, known, hb, ups, downs, after, out, da2, o_near, o_far, li_near, li_far, mix, cot, gains, others):
    pairs = held(2, 2, WIN, 128)
    return run(
        feed_even_kernel,
        [(part, SCALAR)]
        + [
            (a, WHOLE)
            for a in (
                *known, hb, *ups, *downs, after, out, da2, o_near, o_far, li_near, li_far, mix, cot, gains, *others,
            )
        ],
        [
            (shaped(ROWS, D), held(ROWS, D)), *STEP_OUTS, (shaped(2, WIN, D), held(2, WIN, D)),
            *[(pinned(pltpu.HBM, 2, 2, WIN, 128, kind=LOW), pairs)] * 4,
            *[(pinned(pltpu.HBM, 2, D, 128, kind=LOW), held(2, D, 128))] * 2,
            (shaped(4, D), held(4, D)),
        ],
        13, 28,
        grid=(2,),
        scratch=[pltpu.VMEM((D, 512), LOW), pltpu.VMEM((D, 512), LOW), pltpu.VMEM((ROWS, D), F32), *FEED_WORK],
    )


def last_kernel(
    part_ref, x_ref, dafter_ref, gain_ref, l0, l1, l2, l3, w0, w1, w2, w3,
    c0, c1, c2, c3, two_ref, odd_ref, even_ref, wide_ref, p0, p1, p2, e1, e2, e3,
    gx_ref, pack_ref, spread_s, pack_s,
):
    sums = [jnp.zeros((1, D), F32) for _ in range(2)]
    for w in range(2):
        da1 = jnp.zeros((WIN, D), F32)
        for low, wt in ((l0, w0), (l1, w1), (l2, w2), (l3, w3)):
            da1 += product(low[w], wt[...], NT)
        dv, dgain, doff = norm_back(x_ref[w], da1, gain_ref[0:1, :])
        gx_ref[w] = dafter_ref[w] + dv
        sums[0] += dgain
        sums[1] += doff
    cols = slice(RELP, PACK)
    pack_s[0:1, cols] = sums[0]
    pack_s[1:2, cols] = sums[1]
    pack_s[2:6, cols] = two_ref[...]
    for group, c in enumerate((c0, c1, c2, c3)):
        own = pl.ds(pl.multiple_of(RELP + (part_ref[0] ^ group) * 128, 128), 128)
        pack_s[6:8, own] = c[...]
    for i in range(PARTS):
        pack_s[pl.ds(8 + (part_ref[0] ^ i), 1), cols] = (odd_ref if i % 2 else even_ref)[i // 2]
    pack_s[12:16, cols] = jnp.zeros((4, D), F32)
    for group, rows in enumerate((e1, e2, e3)):
        for h in range(GHEADS):
            pack_s[pl.ds((part_ref[0] ^ (group + 1)) * GHEADS + h, 1), 0:RELP] = rows[h : h + 1, :]
    shrunk(wide_ref, (p0, p1, p2), spread_s, pack_s, part_ref[0] * GHEADS)
    pack_ref[...] = pack_s[...].astype(LOW)


def swap(values, axis, distance):
    count = lax.axis_size(axis)
    return lax.ppermute(values, axis, [(i, i ^ distance) for i in range(count)])


def bits_of(axis):
    return (lax.axis_size(axis) - 1).bit_length()


def interleaved(own, other, upper):
    place = jnp.arange(2, dtype=jnp.int32).reshape(1, 2, *(1,) * (own.ndim - 1))
    mine = place == upper.astype(jnp.int32)
    return jnp.where(mine, own[:, None], other[:, None]).reshape(-1, *own.shape[1:])


def upper_of(axis, bit):
    return (lax.axis_index(axis) >> bit) % 2 == 1


def gathered(blocks, bits):
    for bit in bits:
        blocks = interleaved(blocks, swap(blocks, "dp", 1 << bit), upper_of("dp", bit))
    return blocks


def flat(blocks):
    return blocks.reshape(-1, blocks.shape[-1])


def half(total, bit, mine):
    pairs = total.reshape(-1, 2, *total.shape[1:])
    return jnp.where(upper_of("dp", bit) == mine, pairs[:, 1], pairs[:, 0])


def halves(total, bit):
    return half(total, bit, False).astype(LOW), half(total, bit, True).astype(F32)


def plus(one, two):
    return one.astype(F32) + two.astype(F32)


def offset_order(rel_index):
    corners = rel_index.reshape(WT, WH, WW, WIN)[::7, ::6, ::6].reshape(2, 2, 2, WT, WH, WW)
    joined = jnp.concatenate([corners[1], corners[0][:, :, 1:]], axis=2)
    joined = jnp.concatenate([joined[1], joined[0][:, :, 1:]], axis=2)
    joined = jnp.concatenate([joined[1], joined[0][:, :, 1:]], axis=2)
    return jnp.pad(joined.reshape(1, REL), ((0, 0), (0, RELP - REL)), constant_values=-1)


def body(
    inputs,
    w_qkv,
    qv_bias,
    w_proj,
    w_fc1,
    fc1_bias,
    w_fc2,
    norm_gains,
    token_biases,
    table,
    shifts,
    rel_index,
    cotangent,
):
    index = lax.axis_index("mp")
    part = index.astype(jnp.int32).reshape(1)
    rows = w_qkv.shape[1]
    x = inputs.reshape(2, WIN, D)
    cot = cotangent.reshape(2, WIN, D)
    high_bits = tuple(reversed(range(1, bits_of("dp"))))
    low_bits = tuple(range(1, bits_of("dp")))

    shard_qkv = w_qkv.transpose(1, 0, 2).reshape(1, rows, 384).astype(LOW)
    (shard_rest,) = run(
        rest_kernel,
        [(a, WHOLE) for a in (w_proj.T, w_fc1, w_fc2.T)],
        [(shaped(rows, 1152, kind=LOW), WHOLE)],
        1, 8,
    )
    shard_rest = shard_rest[None]
    qkv_first = gathered(shard_qkv, high_bits[:1])
    qkv_high = gathered(qkv_first, high_bits[1:])
    own = flat(gathered(qkv_high, (0,)))
    qkv_parts = [own, swap(own, "mp", 1)]
    across = swap(own, "mp", 2)
    rest = gathered(shard_rest, high_bits)
    up_own = gathered(rest[:, :, :640], (0,))
    up_across = swap(up_own, "mp", 2)
    down_across = swap(rest[:, :, 640:], "mp", 2)
    places = jnp.arange(WIN, dtype=jnp.int32)
    places = jnp.stack([places // (WH * WW), places // WW % WH, places % WW])
    order = offset_order(once(rel_index, qkv_first))
    column = jnp.arange(768, dtype=jnp.int32)
    lane_row = jnp.where(
        column < 15 * 49, column // 49 * 169 + column % 49 // 7 * 13 + column % 7, -1
    )
    a1, a1t, rf, rft = run(
        first_norm_kernel,
        [(part, SCALAR), (shifts, SCALAR)] + [(a, WHOLE) for a in (x, norm_gains, token_biases, places)],
        [
            (shaped(2, WIN, D, kind=LOW), WHOLE), (pinned(pltpu.HBM, 2, D, WIN, kind=LOW), WHOLE),
            (shaped(2, WIN, 128, kind=LOW), WHOLE), (shaped(2, 128, WIN, kind=LOW), WHOLE),
        ],
        2, 16,
        after=(qkv_first,),
    )
    row_offsets, *picks = run(
        rows_from_table_kernel,
        [(a, WHOLE) for a in (order, table.T, lane_row.reshape(1, 768), lane_row.reshape(768, 1))],
        [(shaped(HEADS, RELP), WHOLE)]
        + [(shaped(high - low, 256, kind=LOW), WHOLE) for low, high in LANE_CUTS]
        + [(shaped(256, high - low, kind=LOW), WHOLE) for low, high in LANE_CUTS],
        4, 20,
        after=(qkv_high,),
    )
    out_picks, back_picks = picks[:3], picks[3:]
    near_bias = expand_bias(0, part, row_offsets, out_picks, (qkv_high,))
    near = attend(0, part, a1, qkv_parts[:2], qv_bias, near_bias, rf, rft, (rest,))
    across = once(across, near[4])
    qkv_parts += [across, swap(across, "mp", 1)]
    down_pair = jnp.stack([rest[:, :, 640:], once(down_across, near[4])], axis=0)
    down_other = swap(down_pair, "dp", 1)
    down_own, down_across = (
        interleaved(down_pair[i], down_other[i], upper_of("dp", 0)) for i in range(2)
    )
    far_bias = expand_bias(1, part, row_offsets, out_picks, (near[4], up_own, down_pair))
    far = attend(1, part, a1, qkv_parts[2:], qv_bias, far_bias, rf, rft, (up_own,))
    up_parts = [flat(up_own), flat(swap(up_own, "mp", 1)), flat(up_across), flat(swap(once(up_across, far[4]), "mp", 1))]
    down_parts = [
        flat(down_own), flat(swap(down_own, "mp", 1)), flat(down_across), flat(swap(down_across, "mp", 1))
    ]
    hb = fc1_bias.reshape(PARTS, 1, 512)
    after, *known, mix = before(near[4], far[4], x, cot, token_biases, norm_gains, up_parts)
    out, da2, odd_up, odd_down, hb_odd = feed_odd(
        part, known, hb, up_parts[1::2], down_parts[1::2], after, token_biases
    )
    out, even_up, even_down, hb_even, dafter, dop_near, dop_far, nd_near, nd_far, gp_near, gp_far, sums_two = feed_even(
        part, known, hb, up_parts[::2], down_parts[::2], after, out, da2,
        near[4], far[4], near[5], far[5], mix, cot, norm_gains, up_parts[1::2],
    )
    got_up = swap(odd_up, "mp", 1).reshape(2, -1, rows, 512)
    got_down = swap(odd_down, "mp", 1).reshape(2, -1, rows, 512)
    even_up = even_up.reshape(2, -1, rows, 512)
    even_down = even_down.reshape(2, -1, rows, 512)
    up_send = plus(even_up[1], got_up[1]).astype(LOW)
    turned = [a.transpose(1, 0, 2, 3) for a in (even_down, got_down)]
    down_send = plus(*(half(a, 0, False) for a in turned)).astype(LOW)
    three, wide3, low3, col3 = attend_back(1, dop_far, nd_far, far, a1t, gp_far, (up_send, down_send))
    two, wide2, low2, col2 = attend_back(0, dop_far, nd_far, far, a1t, gp_far, (three,))
    up_sum = plus(plus(even_up[0], got_up[0]), swap(up_send, "mp", 2))
    down_sum = plus(plus(*(half(a, 0, True) for a in turned)), swap(down_send, "dp", 1))
    far_sum = plus(two, swap(three, "mp", 1)).astype(LOW)
    up_send, up_keep = halves(up_sum, 0)
    down_send, down_keep = down_sum[:, 1].astype(LOW), down_sum[:, 0]
    one, wide1, low1, col1 = attend_back(
        1, dop_near, nd_near, near, a1t, gp_near, (far_sum, up_send, down_send)
    )
    far_sum = swap(far_sum, "mp", 2)
    up_sum = plus(up_keep, swap(up_send, "dp", 1))
    down_sum = plus(down_keep, swap(down_send, "mp", 2))
    summed = jnp.concatenate([up_sum, down_sum], axis=2)
    mlp_send, mlp_keep = halves(summed, 1)
    zero, wide0, low0, col0 = attend_back(0, dop_near, nd_near, near, a1t, gp_near, (mlp_send, one))
    summed = plus(mlp_keep, swap(mlp_send, "dp", 2))
    mlp_send, mlp_keep = halves(summed, 2)
    total = plus(plus(zero, swap(one, "mp", 1)), far_sum).reshape(-1, rows, 512)
    rows_by = [shrink_bias(w, back_picks, ()) for w in (wide1, wide2, wide3)]
    send, keep = halves(total, 0)
    grad_x, pack = run(
        last_kernel,
        [(part, SCALAR)]
        + [
            (a, WHOLE)
            for a in (
                x, dafter, norm_gains, low0, low1, low2, low3, *qkv_parts, col0, col1, col2, col3,
                sums_two, hb_odd, hb_even, wide0, *back_picks, *rows_by,
            )
        ],
        [(shaped(2, WIN, D), WHOLE), (shaped(HEADS, PACK, kind=LOW), WHOLE)],
        4, 20,
        scratch=[pltpu.VMEM((GHEADS, 56, RELP), F32), pltpu.VMEM((HEADS, PACK), F32)],
        after=(send, mlp_send),
    )
    total = plus(keep, swap(send, "dp", 1))
    summed = plus(mlp_keep, swap(mlp_send, "dp", 4))
    mp_steps = [("mp", 1 << bit) for bit in range(bits_of("mp"))]
    steps = mp_steps + [("dp", 1 << bit) for bit in range(bits_of("dp"))]
    queue = [("qkv", bit) for bit in low_bits] + [("mlp", bit) for bit in low_bits[2:]]
    queue.sort(key=lambda item: (item[1], item[0] == "qkv"))
    state = {"qkv": total, "mlp": summed}
    pending = None
    for place, (axis, distance) in enumerate(steps):
        mine = pack.astype(LOW)
        theirs = swap(mine, axis, distance)
        if pending is not None:
            name, keep, got = pending
            state[name] = plus(keep, once(got, mine))
            pending = None
        if place >= 1 and queue:
            name, bit = queue.pop(0)
            send, keep = halves(once(state[name], mine), bit)
            theirs = once(theirs, send)
            pending = (name, keep, swap(send, "dp", 1 << bit))
        pack = plus(mine, theirs)
    if pending is not None:
        state[pending[0]] = plus(pending[1], pending[2])
    for name, bit in queue:
        send, keep = halves(state[name], bit)
        state[name] = plus(keep, swap(send, "dp", 1 << bit))
    own_qkv = state["qkv"].reshape(rows, 512)
    own_mlp = state["mlp"].reshape(rows, 1024)
    grad_qkv, grad_proj = run(
        unpack_qkv_kernel,
        [(own_qkv, WHOLE)],
        [(pinned(pltpu.HBM, *dims), held(*dims)) for dims in ((3, rows, 128), (rows, 128))],
        1, 8,
        grid=(1,),
    )
    grad_up, grad_down = run(
        unpack_mlp_kernel,
        [(own_mlp, WHOLE)],
        [(pinned(pltpu.HBM, rows, 512), held(rows, 512))] * 2,
        1, 8,
        grid=(1,),
    )
    grad_table, grad_gains, grad_biases, grad_pair, grad_hidden = run(
        rows_to_table_kernel,
        [(order, WHOLE), (pack, WHOLE)],
        [(shaped(*dims), WHOLE) for dims in ((HEADS, REL), (2, D), (4, D), (2, D), (4, D))],
        4, 20,
        after=(grad_qkv, grad_proj, grad_up, grad_down),
    )
    return (
        out.reshape(inputs.shape),
        grad_x.reshape(inputs.shape),
        grad_qkv,
        grad_pair,
        grad_proj.T,
        grad_up,
        grad_hidden.reshape(FF),
        grad_down.T,
        grad_gains,
        grad_biases,
        grad_table.T,
    )


def solution(mesh):
    placed = (
        P(("dp", "mp"), None),
        P(None, "dp", "mp"),
        P(),
        P("mp", "dp"),
        P("dp", "mp"),
        P(),
        P("mp", "dp"),
        P(),
        P(),
        P(),
        P("dp", None),
        P(),
        P(("dp", "mp"), None),
    )
    return jax.shard_map(
        body,
        mesh=mesh,
        in_specs=placed,
        out_specs=(
            P(("dp", "mp"), None),
            P(("dp", "mp"), None),
            P(None, "dp", "mp"),
            P(),
            P("mp", "dp"),
            P("dp", "mp"),
            P(),
            P("mp", "dp"),
            P(),
            P(),
            P(),
        ),
        check_vma=False,
    )
```

```python
import functools

import jax
import jax.numpy as jnp
from jax import lax
from jax.experimental import pallas as pl
from jax.experimental.pallas import tpu as pltpu
from jax.sharding import PartitionSpec as P

D = 512
HEADS = 16
HD = 32
FF = 2048
WT = 8
WH = 7
WW = 7
GT = 16
GH = 14
GW = 14
WIN = 392
REL = 2535
RELP = 2560
PACK = RELP + D
WINS = 8
PARTS = 4
GHEADS = HEADS // PARTS
LOG2E = 1.4426950408889634
SCALE = HD ** (-0.5)
LOW = jnp.bfloat16
F32 = jnp.float32
NN = (((1,), (0,)), ((), ()))
NT = (((1,), (1,)), ((), ()))
ROW_CUTS = ((0, 64), (64, 64), (128, 64), (192, 64), (256, 64), (320, 72))
LANE_CUTS = ((0, 1024), (768, 1920), (1664, 2560))


def product(left, right, dims=NN):
    return lax.dot_general(left, right, dims, preferred_element_type=F32)


def shaped(*dims, kind=F32):
    return jax.ShapeDtypeStruct(dims, kind)


def cost(micros):
    return pl.CostEstimate(flops=int(micros * 1e9), bytes_accessed=int(micros * 3.6e6), transcendentals=0)


WHOLE = pl.BlockSpec(memory_space=pltpu.VMEM)
ANYWHERE = pl.BlockSpec(memory_space=pl.ANY)
SCALAR = pl.BlockSpec(memory_space=pltpu.SMEM)
FAR = pl.BlockSpec(memory_space=pltpu.HBM)


def run(kernel, ins, outs, micros, mib, grid=(), scratch=(), after=()):
    count = len(ins)

    def inner(*refs):
        kernel(*refs[:count], *refs[count + len(after) :])

    return pl.pallas_call(
        inner,
        grid=grid,
        out_shape=[o[0] for o in outs],
        in_specs=[i[1] for i in ins] + [ANYWHERE] * len(after),
        out_specs=[o[1] for o in outs],
        scratch_shapes=list(scratch),
        cost_estimate=cost(micros),
        compiler_params=pltpu.CompilerParams(vmem_limit_bytes=mib << 20),
    )(*[i[0] for i in ins], *after)


def pinned(space, *dims, kind=F32):
    return space(dims, kind)


def once(value, *others):
    return lax.optimization_barrier((value, *others))[0]


def held(*dims):
    return pl.BlockSpec(dims, lambda e: (0,) * len(dims))


def normed(values):
    centred = values - jnp.mean(values, -1, keepdims=True)
    rstd = lax.rsqrt(jnp.mean(centred * centred, -1, keepdims=True) + 1e-05)
    return centred * rstd, rstd


def first_norm_kernel(part_ref, shift_ref, x_ref, gain_ref, tb_ref, place_ref, a1_ref, a1t_ref, rf_ref, rft_ref):
    codes = lax.broadcasted_iota(jnp.int32, (128, WIN), 0)
    for w in range(2):
        window = (2 * part_ref[0] + w) % WINS
        region = jnp.zeros((1, WIN), jnp.int32)
        for axis, (length, size, along) in enumerate(
            ((WT, GT, window // 4), (WH, GH, window // 2 % 2), (WW, GW, window % 2))
        ):
            cell = place_ref[axis : axis + 1, :] + along * length
            halves_in = (cell >= size - length).astype(jnp.int32)
            shifted = (cell >= size - shift_ref[0, axis]).astype(jnp.int32)
            region = region * 3 + halves_in + shifted
        vhat, _ = normed(x_ref[w])
        a1 = vhat * gain_ref[0:1, :] + tb_ref[0:1, :]
        a1_ref[w] = a1.astype(LOW)
        a1t_ref[w] = a1.T.astype(LOW)
        differs = jnp.where(codes == region, 0.0, 1.0)
        rft_ref[w] = differs.astype(LOW)
        rf_ref[w] = ((1.0 - differs.T) * -1e30).astype(LOW)


def rest_kernel(proj_ref, up_ref, down_ref, out_ref):
    out_ref[...] = jnp.concatenate([proj_ref[...], up_ref[...], down_ref[...]], axis=1).astype(LOW)


def split3(values):
    high = values.astype(LOW)
    rest = values - high.astype(F32)
    mid = rest.astype(LOW)
    return high, mid, (rest - mid.astype(F32)).astype(LOW)


def rows_from_table_kernel(order_ref, table_ref, lane_ref, column_ref, out_ref, *picks):
    table = jnp.concatenate(split3(table_ref[...]), axis=0)
    rows = lax.broadcasted_iota(jnp.int32, (REL, 256), 0)
    for block in range(RELP // 256):
        cols = slice(block * 256, block * 256 + 256)
        picked = jnp.where(rows == order_ref[:, cols], 1.0, 0.0).astype(LOW)
        got = product(table, picked)
        out_ref[:, cols] = (got[:HEADS] + got[HEADS : 2 * HEADS] + got[2 * HEADS :]) * LOG2E
    for block in range(3):
        low, high = LANE_CUTS[block]
        cols = slice(block * 256, block * 256 + 256)
        down = lax.broadcasted_iota(jnp.int32, (high - low, 256), 0) + low
        picks[block][...] = jnp.where(down == lane_ref[:, cols], 1.0, 0.0).astype(LOW)
        across = lax.broadcasted_iota(jnp.int32, (256, high - low), 1) + low
        picks[3 + block][...] = jnp.where(across == column_ref[cols, :], 1.0, 0.0).astype(LOW)


def rows_to_table_kernel(order_ref, pack_ref, out_ref, gains_ref, biases_ref, pair_ref, hidden_ref):
    rows = jnp.concatenate(split3(pack_ref[:, 0:RELP]), axis=0)
    ids = lax.broadcasted_iota(jnp.int32, (256, RELP), 0)
    for start in range(0, REL, 256):
        count = min(256, REL - start)
        picked = jnp.where(ids + start == order_ref[...], 1.0, 0.0).astype(LOW)
        got = product(rows, picked, NT)
        got = got[:HEADS] + got[HEADS : 2 * HEADS] + got[2 * HEADS :]
        out_ref[:, start : start + count] = got[:, :count]
    cols = slice(RELP, PACK)
    for i, at in enumerate((0, 2)):
        gains_ref[i : i + 1, :] = pack_ref[at : at + 1, cols]
    for i, at in enumerate((1, 4, 3, 5)):
        biases_ref[i : i + 1, :] = pack_ref[at : at + 1, cols]
    pair_ref[...] = pack_ref[6:8, cols]
    hidden_ref[...] = pack_ref[8:12, cols]


def unpack_qkv_kernel(qkv_ref, out_ref, proj_ref):
    for i in range(3):
        out_ref[i] = qkv_ref[:, 128 * i : 128 * i + 128]
    proj_ref[...] = qkv_ref[:, 384:512]


def unpack_mlp_kernel(mlp_ref, up_ref, down_ref):
    up_ref[...] = mlp_ref[:, 0:512]
    down_ref[...] = mlp_ref[:, 512:1024]


def lanes_of(ti):
    off = 49 * (7 - ti)
    base = off // 128 * 128
    return base, off - base


def expand_kernel(pair, part_ref, rows_ref, p0, p1, p2, bias_ref, left_s, wide_s):
    group = 2 * pair + pl.program_id(0)
    base_row = (part_ref[0] ^ group) * GHEADS
    back = 7 - lax.broadcasted_iota(jnp.int32, (8, RELP), 0)
    for h in range(GHEADS):
        row = jnp.broadcast_to(rows_ref[pl.ds(base_row + h, 1), :], (8, RELP))
        for bit in range(3):
            row = jnp.where(((back >> bit) & 1) == 1, pltpu.roll(row, RELP - (1 << bit), 1), row)
        for hi in range(WH):
            rolled = pltpu.roll(row, (1 - (6 - hi) * 13) % RELP, 1)
            at = 56 * h + 8 * hi
            left_s[at : at + 8, :] = rolled
    for block, pick in enumerate((p0, p1, p2)):
        low, high = LANE_CUTS[block]
        got = product(left_s[:, low:high].astype(LOW), pick[...])
        for h in range(GHEADS):
            wide_s[h, :, block * 256 : block * 256 + 256] = got[56 * h : 56 * h + 56]
    for h in range(GHEADS):
        for ti in range(WT):
            base, by = lanes_of(ti)
            for hi in range(WH):
                tile = wide_s[h, 8 * hi : 8 * hi + 8, base : base + 512]
                if by:
                    tile = pltpu.roll(tile, 512 - by, 1)
                at = 49 * ti + 7 * hi
                bias_ref[h, at : at + 7, :] = tile[:7, :WIN]


def expand_bias(pair, part, rows, picks, after):
    return run(
        functools.partial(expand_kernel, pair),
        [(part, SCALAR), (rows, WHOLE)] + [(p, WHOLE) for p in picks],
        [(shaped(2 * GHEADS, WIN, WIN), pl.BlockSpec((GHEADS, WIN, WIN), lambda g: (g, 0, 0)))],
        5, 14,
        grid=(2,),
        scratch=[pltpu.VMEM((56 * GHEADS, RELP), F32), pltpu.VMEM((GHEADS, 56, 768), F32)],
        after=after,
    )[0]


def shrunk(wide_refs, picks, spread_s, out_ref, at):
    heads = wide_refs.shape[0]
    used = (lax.broadcasted_iota(jnp.int32, (56, 256), 0) & 7) < 7
    spread_s[...] = jnp.zeros(spread_s.shape, F32)
    for block, pick in enumerate(picks):
        low, high = LANE_CUTS[block]
        parts = []
        for h in range(heads):
            wide = jnp.where(used, wide_refs[h, :, block * 256 : block * 256 + 256], 0.0)
            near = wide.astype(LOW).astype(F32)
            parts += [near, wide - near]
        got = product(jnp.concatenate(parts, axis=0).astype(LOW), pick[...])
        for h in range(heads):
            spread_s[h, :, low:high] += got[112 * h : 112 * h + 56] + got[112 * h + 56 : 112 * h + 112]
    left = 7 - lax.broadcasted_iota(jnp.int32, (8, RELP), 0)
    for h in range(heads):
        total = jnp.zeros((8, RELP), F32)
        for hi in range(WH):
            total += pltpu.roll(spread_s[h, 8 * hi : 8 * hi + 8, :], ((6 - hi) * 13 - 1) % RELP, 1)
        for bit in range(3):
            total = jnp.where(((left >> bit) & 1) == 1, pltpu.roll(total, 1 << bit, 1), total)
        out_ref[pl.ds(at + h, 1), 0:RELP] = jnp.sum(total, axis=0, keepdims=True)


def shrink_kernel(wide_ref, p0, p1, p2, out_ref, spread_s):
    shrunk(wide_ref, (p0, p1, p2), spread_s, out_ref, 0)


def shrink_bias(wide, picks, after):
    return run(
        shrink_kernel,
        [(wide, WHOLE)] + [(p, WHOLE) for p in picks],
        [(shaped(GHEADS, RELP), WHOLE)],
        1.4, 12,
        scratch=[pltpu.VMEM((GHEADS, 56, RELP), F32)],
        after=after,
    )[0]


P_SLOTS = 3


def attend_kernel(
    pair, part_ref, a1_ref, wa_ref, wb_ref, qvb_ref, bias_ref, rf_ref, rft_ref,
    p_ref, qt_ref, k_ref, vt_ref, o_ref, li_ref,
    q_s, ka_s, v_s, s_s, acc_s, p_s, p_sem,
):
    lane = lax.broadcasted_iota(jnp.int32, (WIN, 128), 1) // HD
    zero = jnp.zeros((WIN, 128), LOW)

    def away(at):
        slot = at % P_SLOTS
        return pltpu.make_async_copy(p_s.at[slot], p_ref.at[at], p_sem.at[slot])

    for g, w_ref in enumerate((wa_ref, wb_ref)):
        cols = pl.ds(pl.multiple_of((part_ref[0] ^ (2 * pair + g)) * 128, 128), 128)
        for w in range(2):
            qkv = product(a1_ref[w], w_ref[:, 0:384] if w_ref.shape[1] > 384 else w_ref[...])
            q = (qkv[:, :128] + qvb_ref[0:1, cols]) * (SCALE * LOG2E)
            k = qkv[:, 128:256]
            v = qkv[:, 256:384] + qvb_ref[1:2, cols]
            q_s[g, w] = q.astype(LOW)
            v_s[g, w] = v.astype(LOW)
            qt_ref[g, w] = q.T.astype(LOW)
            k_ref[g, w] = k.astype(LOW)
            vt_ref[g, w] = v.T.astype(LOW)
            ka_s[g, w, 0:128, :] = k.T.astype(LOW)
            ka_s[g, w, 128:256, :] = rft_ref[w]
        for e in range(GHEADS):
            at = GHEADS * g + e
            slot = at % P_SLOTS
            mine = lane == e
            if at >= P_SLOTS:
                away(at - P_SLOTS).wait()
            for w in range(2):
                q_wide = jnp.concatenate([jnp.where(mine, q_s[g, w], zero), rf_ref[w]], axis=1)
                s_s[at % 2, w] = product(q_wide, ka_s[g, w])
            for w in range(2):
                for start, count in ROW_CUTS:
                    rows = slice(start, start + count)
                    scores = s_s[at % 2, w, rows, :] + bias_ref[at, rows, :]
                    top = jnp.max(scores, axis=1, keepdims=True)
                    p_s[slot, w, rows, :] = jnp.exp2(scores - top).astype(LOW)
                v_wide = jnp.concatenate(
                    [jnp.where(mine, v_s[g, w], zero), jnp.where(mine, 1.0, 0.0).astype(LOW)], axis=1
                )
                part = product(p_s[slot, w], v_wide)
                acc_s[g, w] = part if e == 0 else acc_s[g, w] + part
            away(at).start()
        for w in range(2):
            inverse = 1.0 / acc_s[g, w, :, 128:256]
            li_ref[g, w] = inverse
            o_ref[g, w] = acc_s[g, w, :, 0:128] * inverse
    for at in range(2 * GHEADS - P_SLOTS, 2 * GHEADS):
        away(at).wait()


def attend(pair, part, a1, weights, qvb, bias, rf, rft, after):
    return run(
        functools.partial(attend_kernel, pair),
        [(part, SCALAR)] + [(a, WHOLE) for a in (a1, *weights, qvb, bias, rf, rft)],
        [
            (pinned(pltpu.HBM, 2 * GHEADS, 2, WIN, WIN, kind=LOW), FAR),
            (pinned(pltpu.HBM, 2, 2, 128, WIN, kind=LOW), WHOLE),
            (pinned(pltpu.HBM, 2, 2, WIN, 128, kind=LOW), WHOLE),
            (pinned(pltpu.HBM, 2, 2, 128, WIN, kind=LOW), WHOLE),
            (shaped(2, 2, WIN, 128), WHOLE),
            (shaped(2, 2, WIN, 128), WHOLE),
        ],
        11, 28,
        scratch=[
            pltpu.VMEM((2, 2, WIN, 128), LOW),
            pltpu.VMEM((2, 2, 256, WIN), LOW),
            pltpu.VMEM((2, 2, WIN, 128), LOW),
            pltpu.VMEM((2, 2, WIN, WIN), F32),
            pltpu.VMEM((2, 2, WIN, 256), F32),
            pltpu.VMEM((P_SLOTS, 2, WIN, WIN), LOW),
            pltpu.SemaphoreType.DMA((P_SLOTS,)),
        ],
        after=after,
    )


def attend_back_kernel(
    at, dop_ref, nd_ref, p_ref, qt_ref, k_ref, vt_ref, a1t_ref, gp_ref,
    dw_ref, wide_ref, low_ref, cs_ref,
    dop_s, nd_s, qt_s, k_s, vt_s, a1t_s, gp_s, p_s, dopt_s, dp_s, ds_s, dq_s, dkt_s, dvt_s, db_s, sems,
):
    lane = lax.broadcasted_iota(jnp.int32, (WIN, 128), 1) // HD
    zero = jnp.zeros((WIN, 128), LOW)
    inside = lax.broadcasted_iota(jnp.int32, (8, 512), 1) < WIN
    names = ("dop", "nd", "vt", "qt", "k", "gp", "a1t")
    sources = (dop_ref.at[at], nd_ref.at[at], vt_ref.at[at], qt_ref.at[at], k_ref.at[at], gp_ref.at[at], a1t_ref)
    targets = (dop_s, nd_s, vt_s, qt_s, k_s, gp_s, a1t_s)
    copies = {
        name: pltpu.make_async_copy(source, target, sems.at[i])
        for i, (name, source, target) in enumerate(zip(names, sources, targets))
    }
    probs = [
        pltpu.make_async_copy(p_ref.at[GHEADS * at + e], p_s.at[e], sems.at[len(names) + e]) for e in range(GHEADS)
    ]
    for name in ("dop", "nd", "vt"):
        copies[name].start()
    probs[0].start()
    copies["qt"].start()
    copies["k"].start()
    for e in range(1, GHEADS):
        probs[e].start()
    copies["a1t"].start()
    copies["gp"].start()
    for name in ("dop", "nd", "vt"):
        copies[name].wait()
    for w in range(2):
        dopt_s[w] = dop_s[w].astype(F32).T.astype(LOW)
    for e in range(GHEADS):
        mine = lane == e
        own = slice(HD * e, HD * e + HD)
        slot = e % 2
        for w in range(2):
            wide = jnp.concatenate([jnp.where(mine, dop_s[w], zero), jnp.where(mine, nd_s[w], zero)], axis=1)
            v_wide = jnp.concatenate([vt_s[w], jnp.ones((128, WIN), LOW)], axis=0)
            dp_s[slot, w] = product(wide, v_wide)
        probs[e].wait()
        for w in range(2):
            dvt_s[w, own, :] = product(dopt_s[w, own, :], p_s[e, w])
        for start, count in ROW_CUTS:
            rows = slice(start, start + count)
            one = p_s[e, 0, rows, :].astype(F32) * dp_s[slot, 0, rows, :]
            two = p_s[e, 1, rows, :].astype(F32) * dp_s[slot, 1, rows, :]
            db_s[slot, rows, 0:WIN] = one + two
            ds_s[slot, 0, rows, :] = one.astype(LOW)
            ds_s[slot, 1, rows, :] = two.astype(LOW)
        if e == 0:
            copies["qt"].wait()
            copies["k"].wait()
        for w in range(2):
            dkt_s[w, own, :] = product(qt_s[w, own, :], ds_s[slot, w])
            part = product(ds_s[slot, w], jnp.where(mine, k_s[w], zero))
            dq_s[w] = part if e == 0 else dq_s[w] + part
        for hi in range(WH):
            own_rows = slice(8 * hi, 8 * hi + 8)
            wide_ref[e, own_rows, :] = jnp.zeros((8, 768), F32)
            for base in (0, 128, 256):
                total = jnp.zeros((8, 512), F32)
                for ti in range(WT):
                    lane_base, by = lanes_of(ti)
                    if lane_base != base:
                        continue
                    first_row = 49 * ti + 7 * hi
                    tile = jnp.where(inside, db_s[slot, first_row : first_row + 8, :], 0.0)
                    total += pltpu.roll(tile, by, 1) if by else tile
                wide_ref[e, own_rows, base : base + 512] += total
    copies["a1t"].wait()
    copies["gp"].wait()
    sum_q = jnp.zeros((1, 128), F32)
    sum_v = jnp.zeros((1, 128), F32)
    grad = jnp.zeros((D, 384), F32)
    for w in range(2):
        dq = dq_s[w] * SCALE
        dk = (dkt_s[w] * (1.0 / LOG2E)).T
        dv = dvt_s[w].T
        sum_q += jnp.sum(dq, axis=0, keepdims=True)
        sum_v += jnp.sum(dv, axis=0, keepdims=True)
        low = jnp.concatenate([dq, dk, dv], axis=1).astype(LOW)
        low_ref[w] = low
        grad += product(a1t_s[w], low)
    dw_ref[:, 0:384] = grad.astype(LOW)
    dw_ref[:, 384:512] = gp_s[...]
    cs_ref[0:1, :] = sum_q
    cs_ref[1:2, :] = sum_v


def attend_back(at, dop, nd, kept, a1t, gproj, after):
    p, qt, k, vt, _, _ = kept
    return run(
        functools.partial(attend_back_kernel, at),
        [(pltpu.with_memory_space_constraint(a, pltpu.HBM), FAR) for a in (dop, nd, p, qt, k, vt, a1t, gproj)],
        [
            (shaped(D, 512, kind=LOW), WHOLE),
            (shaped(GHEADS, 56, 768), WHOLE),
            (shaped(2, WIN, 384, kind=LOW), WHOLE),
            (shaped(2, 128), WHOLE),
        ],
        6, 24,
        scratch=[
            pltpu.VMEM((2, WIN, 128), LOW),
            pltpu.VMEM((2, WIN, 128), LOW),
            pltpu.VMEM((2, 128, WIN), LOW),
            pltpu.VMEM((2, WIN, 128), LOW),
            pltpu.VMEM((2, 128, WIN), LOW),
            pltpu.VMEM((2, D, WIN), LOW),
            pltpu.VMEM((D, 128), LOW),
            pltpu.VMEM((GHEADS, 2, WIN, WIN), LOW),
            pltpu.VMEM((2, 128, WIN), LOW),
            pltpu.VMEM((2, 2, WIN, WIN), F32),
            pltpu.VMEM((2, 2, WIN, WIN), LOW),
            pltpu.VMEM((2, WIN, 128), F32),
            pltpu.VMEM((2, 128, WIN), F32),
            pltpu.VMEM((2, 128, WIN), F32),
            pltpu.VMEM((2, 400, 512), F32),
            pltpu.SemaphoreType.DMA((7 + GHEADS,)),
        ],
        after=after,
    )


def gelu_parts(v):
    size = jnp.abs(v)
    t = 1.0 / (1.0 + (0.3275911 * 0.7071067811865476) * size)
    bell = jnp.exp2(v * v * (-0.5 * LOG2E))
    poly = t * (0.127414796 + t * (-0.142248368 + t * (0.7107068705 + t * (-0.7265760135 + t * 0.5307027145))))
    tail = poly * bell
    phi = jnp.where(v >= 0.0, 1.0 - tail, tail)
    return v * phi, phi + v * bell * 0.3989422804014327


def norm_back(values, dy, gain):
    vhat, rstd = normed(values)
    scaled = dy * gain
    dv = rstd * (
        scaled - jnp.mean(scaled, -1, keepdims=True) - vhat * jnp.mean(scaled * vhat, -1, keepdims=True)
    )
    return dv, jnp.sum(dy * vhat, axis=0, keepdims=True), jnp.sum(dy, axis=0, keepdims=True)


ROWS = 2 * WIN


def before_kernel(
    on_ref, of_ref, x_ref, cot_ref, tb_ref, gain_ref, u0, u1, u2, u3,
    after_ref, a2_ref, a2t_ref, g_ref, gt_ref, mix_ref,
):
    weight = jnp.concatenate([u[:, 0:128] for u in (u0, u1, u2, u3)], axis=1)
    lows = []
    for w in range(2):
        mixed = jnp.concatenate([on_ref[0, w], on_ref[1, w], of_ref[0, w], of_ref[1, w]], axis=1).astype(LOW)
        mix_ref[w] = mixed
        after = x_ref[w] + product(mixed, weight, NT) + tb_ref[1:2, :]
        after_ref[w] = after
        vhat, _ = normed(after)
        lows.append(vhat * gain_ref[1:2, :] + tb_ref[2:3, :])
    a2 = jnp.concatenate(lows, axis=0)
    a2_ref[...] = a2.astype(LOW)
    a2t_ref[...] = a2.T.astype(LOW)
    cot = jnp.concatenate([cot_ref[0], cot_ref[1]], axis=0)
    g_ref[...] = cot.astype(LOW)
    gt_ref[...] = cot.T.astype(LOW)


def before(o_near, o_far, x, cot, biases, gains, ups):
    return run(
        before_kernel,
        [(a, WHOLE) for a in (o_near, o_far, x, cot, biases, gains, *ups)],
        [
            (shaped(2, WIN, D), WHOLE), (shaped(ROWS, D, kind=LOW), WHOLE), (shaped(D, ROWS, kind=LOW), WHOLE),
            (shaped(ROWS, D, kind=LOW), WHOLE), (shaped(D, ROWS, kind=LOW), WHOLE), (shaped(2, WIN, D, kind=LOW), WHOLE),
        ],
        4, 16,
    )


def feed_parts(
    first, part_ref, a2_ref, a2t_ref, g_ref, gt_ref, hb_ref, ups, downs,
    out_ref, da2_ref, gup_ref, gdown_ref, ghb_ref, h_s, d_s, act_s, dh_s,
):
    def rise(p, half):
        cols = slice(256 * half, 256 * half + 256)
        h_s[p, :, cols] = product(a2_ref[...], ups[p][:, 128 + 256 * half : 384 + 256 * half])
        d_s[p, :, cols] = product(g_ref[...], downs[p][:, cols])

    def bend(p, half):
        for cut in range(256 * half, 256 * half + 256, 128):
            cols = slice(cut, cut + 128)
            line = hb_ref[(first + 2 * p) ^ part_ref[0], :, cols]
            sums = jnp.zeros((1, 128), F32)
            for start in range(0, ROWS, 112):
                rows = slice(start, start + 112)
                act, slope = gelu_parts(h_s[p, rows, cols] + line)
                act_s[p, rows, cols] = act.astype(LOW)
                grad = d_s[p, rows, cols] * slope
                sums += jnp.sum(grad, axis=0, keepdims=True)
                dh_s[p, rows, cols] = grad.astype(LOW)
            ghb_ref[p, :, cols] = sums

    def fall(p):
        for half in range(2):
            cols = slice(256 * half, 256 * half + 256)
            gup_ref[p, :, cols] = product(a2t_ref[...], dh_s[p, :, cols]).astype(LOW)
            gdown_ref[p, :, cols] = product(gt_ref[...], act_s[p, :, cols]).astype(LOW)
        out_ref[...] += product(act_s[p], downs[p][...], NT)
        da2_ref[...] += product(dh_s[p], ups[p][:, 128:640], NT)

    rise(0, 0)
    rise(0, 1)
    bend(0, 0)
    rise(1, 0)
    bend(0, 1)
    rise(1, 1)
    bend(1, 0)
    fall(0)
    bend(1, 1)
    fall(1)


def feed_odd_kernel(
    part_ref, a2_ref, a2t_ref, g_ref, gt_ref, hb_ref, ua, ub, wa, wb, after_ref, tb_ref,
    out_ref, da2_ref, gup_ref, gdown_ref, ghb_ref, *work,
):
    for w in range(2):
        out_ref[WIN * w : WIN * w + WIN, :] = after_ref[w] + tb_ref[3:4, :]
    da2_ref[...] = jnp.zeros((ROWS, D), F32)
    feed_parts(
        1, part_ref, a2_ref, a2t_ref, g_ref, gt_ref, hb_ref, (ua, ub), (wa, wb),
        out_ref, da2_ref, gup_ref, gdown_ref, ghb_ref, *work,
    )


def feed_even_kernel(
    part_ref, a2_ref, a2t_ref, g_ref, gt_ref, hb_ref, ua, ub, wa, wb, after_ref,
    out_in, da2_in, on_ref, of_ref, lin_ref, lif_ref, mix_ref, cot_ref, gain_ref, uc, ud,
    out_ref, gup_ref, gdown_ref, ghb_ref, dafter_ref, dn_ref, df_ref, nn_ref, nf_ref, gpn_ref, gpf_ref, sums_ref,
    da2_s, *work,
):
    out_ref[...] = out_in[...]
    da2_s[...] = da2_in[...]
    feed_parts(
        0, part_ref, a2_ref, a2t_ref, g_ref, gt_ref, hb_ref, (ua, ub), (wa, wb),
        out_ref, da2_s, gup_ref, gdown_ref, ghb_ref, *work,
    )
    weight = jnp.concatenate([u[:, 0:128] for u in (ua, uc, ub, ud)], axis=1)
    grad = jnp.zeros((D, D), F32)
    sums = [jnp.zeros((1, D), F32) for _ in range(4)]
    for w in range(2):
        own = slice(WIN * w, WIN * w + WIN)
        dv, dgain, doff = norm_back(after_ref[w], da2_s[own, :], gain_ref[1:2, :])
        cot = cot_ref[w]
        dafter = cot + dv
        dafter_ref[w] = dafter
        turned = dafter.T.astype(LOW)
        dmix = product(dafter.astype(LOW), weight)
        for i in range(PARTS):
            at = i % 2
            d_ref, n_ref, l_ref, m_ref = (
                (dn_ref, nn_ref, lin_ref, on_ref) if i < 2 else (df_ref, nf_ref, lif_ref, of_ref)
            )
            dop = (dmix[:, 128 * i : 128 * i + 128] * l_ref[at, w]).astype(LOW)
            d_ref[at, w] = dop
            n_ref[at, w] = (-(dop.astype(F32) * m_ref[at, w])).astype(LOW)
        grad += product(turned, mix_ref[w])
        parts = (dgain, doff, jnp.sum(dafter, axis=0, keepdims=True), jnp.sum(cot, axis=0, keepdims=True))
        for i, part in enumerate(parts):
            sums[i] += part
    for i, (ref, at) in enumerate(((gpn_ref, 0), (gpn_ref, 1), (gpf_ref, 0), (gpf_ref, 1))):
        ref[at] = grad[:, 128 * i : 128 * i + 128].astype(LOW)
    for i in range(4):
        sums_ref[i : i + 1, :] = sums[i]


FEED_WORK = [
    pltpu.VMEM((2, ROWS, 512), F32), pltpu.VMEM((2, ROWS, 512), F32),
    pltpu.VMEM((2, ROWS, 512), LOW), pltpu.VMEM((2, ROWS, 512), LOW),
]
STEP_OUTS = [(shaped(2, D, 512, kind=LOW), WHOLE), (shaped(2, D, 512, kind=LOW), WHOLE), (shaped(2, 1, 512), WHOLE)]


def feed_odd(part, known, hb, ups, downs, after, biases):
    return run(
        feed_odd_kernel,
        [(part, SCALAR)] + [(a, WHOLE) for a in (*known, hb, *ups, *downs, after, biases)],
        [(shaped(ROWS, D), WHOLE), (shaped(ROWS, D), WHOLE), *STEP_OUTS],
        9, 28,
        scratch=FEED_WORK,
    )


def feed_even(part, known, hb, ups, downs, after, out, da2, o_near, o_far, li_near, li_far, mix, cot, gains, others):
    return run(
        feed_even_kernel,
        [(part, SCALAR)]
        + [
            (a, WHOLE)
            for a in (
                *known, hb, *ups, *downs, after, out, da2, o_near, o_far, li_near, li_far, mix, cot, gains, *others,
            )
        ],
        [
            (shaped(ROWS, D), WHOLE), *STEP_OUTS, (shaped(2, WIN, D), WHOLE),
            *[(pinned(pltpu.HBM, 2, 2, WIN, 128, kind=LOW), WHOLE)] * 4,
            *[(pinned(pltpu.HBM, 2, D, 128, kind=LOW), WHOLE)] * 2,
            (shaped(4, D), WHOLE),
        ],
        13, 32,
        scratch=[pltpu.VMEM((ROWS, D), F32), *FEED_WORK],
    )


def last_kernel(
    part_ref, x_ref, dafter_ref, gain_ref, l0, l1, l2, l3, w0, w1, w2, w3,
    c0, c1, c2, c3, two_ref, odd_ref, even_ref, wide_ref, p0, p1, p2, e1, e2, e3,
    gx_ref, pack_ref, spread_s, pack_s,
):
    sums = [jnp.zeros((1, D), F32) for _ in range(2)]
    for w in range(2):
        da1 = jnp.zeros((WIN, D), F32)
        for low, wt in ((l0, w0), (l1, w1), (l2, w2), (l3, w3)):
            da1 += product(low[w], wt[...], NT)
        dv, dgain, doff = norm_back(x_ref[w], da1, gain_ref[0:1, :])
        gx_ref[w] = dafter_ref[w] + dv
        sums[0] += dgain
        sums[1] += doff
    cols = slice(RELP, PACK)
    pack_s[0:1, cols] = sums[0]
    pack_s[1:2, cols] = sums[1]
    pack_s[2:6, cols] = two_ref[...]
    for group, c in enumerate((c0, c1, c2, c3)):
        own = pl.ds(pl.multiple_of(RELP + (part_ref[0] ^ group) * 128, 128), 128)
        pack_s[6:8, own] = c[...]
    for i in range(PARTS):
        pack_s[pl.ds(8 + (part_ref[0] ^ i), 1), cols] = (odd_ref if i % 2 else even_ref)[i // 2]
    pack_s[12:16, cols] = jnp.zeros((4, D), F32)
    for group, rows in enumerate((e1, e2, e3)):
        for h in range(GHEADS):
            pack_s[pl.ds((part_ref[0] ^ (group + 1)) * GHEADS + h, 1), 0:RELP] = rows[h : h + 1, :]
    shrunk(wide_ref, (p0, p1, p2), spread_s, pack_s, part_ref[0] * GHEADS)
    pack_ref[...] = pack_s[...].astype(LOW)


def swap(values, axis, distance):
    count = lax.axis_size(axis)
    return lax.ppermute(values, axis, [(i, i ^ distance) for i in range(count)])


def bits_of(axis):
    return (lax.axis_size(axis) - 1).bit_length()


def interleaved(own, other, upper):
    place = jnp.arange(2, dtype=jnp.int32).reshape(1, 2, *(1,) * (own.ndim - 1))
    mine = place == upper.astype(jnp.int32)
    return jnp.where(mine, own[:, None], other[:, None]).reshape(-1, *own.shape[1:])


def upper_of(axis, bit):
    return (lax.axis_index(axis) >> bit) % 2 == 1


def gathered(blocks, bits):
    for bit in bits:
        blocks = interleaved(blocks, swap(blocks, "dp", 1 << bit), upper_of("dp", bit))
    return blocks


def flat(blocks):
    return blocks.reshape(-1, blocks.shape[-1])


def half(total, bit, mine):
    pairs = total.reshape(-1, 2, *total.shape[1:])
    return jnp.where(upper_of("dp", bit) == mine, pairs[:, 1], pairs[:, 0])


def halves(total, bit):
    return half(total, bit, False).astype(LOW), half(total, bit, True).astype(F32)


def plus(one, two):
    return one.astype(F32) + two.astype(F32)


def offset_order(rel_index):
    corners = rel_index.reshape(WT, WH, WW, WIN)[::7, ::6, ::6].reshape(2, 2, 2, WT, WH, WW)
    joined = jnp.concatenate([corners[1], corners[0][:, :, 1:]], axis=2)
    joined = jnp.concatenate([joined[1], joined[0][:, :, 1:]], axis=2)
    joined = jnp.concatenate([joined[1], joined[0][:, :, 1:]], axis=2)
    return jnp.pad(joined.reshape(1, REL), ((0, 0), (0, RELP - REL)), constant_values=-1)


def body(
    inputs,
    w_qkv,
    qv_bias,
    w_proj,
    w_fc1,
    fc1_bias,
    w_fc2,
    norm_gains,
    token_biases,
    table,
    shifts,
    rel_index,
    cotangent,
):
    index = lax.axis_index("mp")
    part = index.astype(jnp.int32).reshape(1)
    rows = w_qkv.shape[1]
    x = inputs.reshape(2, WIN, D)
    cot = cotangent.reshape(2, WIN, D)
    high_bits = tuple(reversed(range(1, bits_of("dp"))))
    low_bits = tuple(range(1, bits_of("dp")))

    shard_qkv = w_qkv.transpose(1, 0, 2).reshape(1, rows, 384).astype(LOW)
    (shard_rest,) = run(
        rest_kernel,
        [(a, WHOLE) for a in (w_proj.T, w_fc1, w_fc2.T)],
        [(shaped(rows, 1152, kind=LOW), WHOLE)],
        1, 8,
    )
    shard_rest = shard_rest[None]
    qkv_first = gathered(shard_qkv, high_bits[:1])
    qkv_high = gathered(qkv_first, high_bits[1:])
    own = flat(gathered(qkv_high, (0,)))
    qkv_parts = [own, swap(own, "mp", 1)]
    across = swap(own, "mp", 2)
    rest = gathered(shard_rest, high_bits)
    up_own = gathered(rest[:, :, :640], (0,))
    up_across = swap(up_own, "mp", 2)
    down_across = swap(rest[:, :, 640:], "mp", 2)
    places = jnp.arange(WIN, dtype=jnp.int32)
    places = jnp.stack([places // (WH * WW), places // WW % WH, places % WW])
    order = offset_order(once(rel_index, qkv_first))
    column = jnp.arange(768, dtype=jnp.int32)
    lane_row = jnp.where(
        column < 15 * 49, column // 49 * 169 + column % 49 // 7 * 13 + column % 7, -1
    )
    a1, a1t, rf, rft = run(
        first_norm_kernel,
        [(part, SCALAR), (shifts, SCALAR)] + [(a, WHOLE) for a in (x, norm_gains, token_biases, places)],
        [
            (shaped(2, WIN, D, kind=LOW), WHOLE), (pinned(pltpu.HBM, 2, D, WIN, kind=LOW), WHOLE),
            (shaped(2, WIN, 128, kind=LOW), WHOLE), (shaped(2, 128, WIN, kind=LOW), WHOLE),
        ],
        2, 16,
        after=(qkv_first,),
    )
    row_offsets, *picks = run(
        rows_from_table_kernel,
        [(a, WHOLE) for a in (order, table.T, lane_row.reshape(1, 768), lane_row.reshape(768, 1))],
        [(shaped(HEADS, RELP), WHOLE)]
        + [(shaped(high - low, 256, kind=LOW), WHOLE) for low, high in LANE_CUTS]
        + [(shaped(256, high - low, kind=LOW), WHOLE) for low, high in LANE_CUTS],
        4, 20,
        after=(qkv_high,),
    )
    out_picks, back_picks = picks[:3], picks[3:]
    near_bias = expand_bias(0, part, row_offsets, out_picks, (qkv_high,))
    near = attend(0, part, a1, qkv_parts[:2], qv_bias, near_bias, rf, rft, (rest,))
    across = once(across, near[4])
    qkv_parts += [across, swap(across, "mp", 1)]
    down_pair = jnp.stack([rest[:, :, 640:], once(down_across, near[4])], axis=0)
    down_other = swap(down_pair, "dp", 1)
    down_own, down_across = (
        interleaved(down_pair[i], down_other[i], upper_of("dp", 0)) for i in range(2)
    )
    far_bias = expand_bias(1, part, row_offsets, out_picks, (near[4], up_own, down_pair))
    far = attend(1, part, a1, qkv_parts[2:], qv_bias, far_bias, rf, rft, (up_own,))
    up_parts = [flat(up_own), flat(swap(up_own, "mp", 1)), flat(up_across), flat(swap(once(up_across, far[4]), "mp", 1))]
    down_parts = [
        flat(down_own), flat(swap(down_own, "mp", 1)), flat(down_across), flat(swap(down_across, "mp", 1))
    ]
    hb = fc1_bias.reshape(PARTS, 1, 512)
    after, *known, mix = before(near[4], far[4], x, cot, token_biases, norm_gains, up_parts)
    out, da2, odd_up, odd_down, hb_odd = feed_odd(
        part, known, hb, up_parts[1::2], down_parts[1::2], after, token_biases
    )
    out, even_up, even_down, hb_even, dafter, dop_near, dop_far, nd_near, nd_far, gp_near, gp_far, sums_two = feed_even(
        part, known, hb, up_parts[::2], down_parts[::2], after, out, da2,
        near[4], far[4], near[5], far[5], mix, cot, norm_gains, up_parts[1::2],
    )
    got_up = swap(odd_up, "mp", 1).reshape(2, -1, rows, 512)
    got_down = swap(odd_down, "mp", 1).reshape(2, -1, rows, 512)
    even_up = even_up.reshape(2, -1, rows, 512)
    even_down = even_down.reshape(2, -1, rows, 512)
    up_send = plus(even_up[1], got_up[1]).astype(LOW)
    turned = [a.transpose(1, 0, 2, 3) for a in (even_down, got_down)]
    down_send = plus(*(half(a, 0, False) for a in turned)).astype(LOW)
    three, wide3, low3, col3 = attend_back(1, dop_far, nd_far, far, a1t, gp_far, (up_send, down_send))
    two, wide2, low2, col2 = attend_back(0, dop_far, nd_far, far, a1t, gp_far, (three,))
    up_sum = plus(plus(even_up[0], got_up[0]), swap(up_send, "mp", 2))
    down_sum = plus(plus(*(half(a, 0, True) for a in turned)), swap(down_send, "dp", 1))
    far_sum = plus(two, swap(three, "mp", 1)).astype(LOW)
    up_send, up_keep = halves(up_sum, 0)
    down_send, down_keep = down_sum[:, 1].astype(LOW), down_sum[:, 0]
    one, wide1, low1, col1 = attend_back(
        1, dop_near, nd_near, near, a1t, gp_near, (far_sum, up_send, down_send)
    )
    far_sum = swap(far_sum, "mp", 2)
    up_sum = plus(up_keep, swap(up_send, "dp", 1))
    down_sum = plus(down_keep, swap(down_send, "mp", 2))
    summed = jnp.concatenate([up_sum, down_sum], axis=2)
    mlp_send, mlp_keep = halves(summed, 1)
    zero, wide0, low0, col0 = attend_back(0, dop_near, nd_near, near, a1t, gp_near, (mlp_send, one))
    summed = plus(mlp_keep, swap(mlp_send, "dp", 2))
    total = plus(plus(zero, swap(one, "mp", 1)), far_sum).reshape(-1, rows, 512)
    rows_by = [shrink_bias(w, back_picks, ()) for w in (wide1, wide2, wide3)]
    send, keep = halves(total, 0)
    grad_x, pack = run(
        last_kernel,
        [(part, SCALAR)]
        + [
            (a, WHOLE)
            for a in (
                x, dafter, norm_gains, low0, low1, low2, low3, *qkv_parts, col0, col1, col2, col3,
                sums_two, hb_odd, hb_even, wide0, *back_picks, *rows_by,
            )
        ],
        [(shaped(2, WIN, D), WHOLE), (shaped(HEADS, PACK, kind=LOW), WHOLE)],
        4, 20,
        scratch=[pltpu.VMEM((GHEADS, 56, RELP), F32), pltpu.VMEM((HEADS, PACK), F32)],
        after=(send,),
    )
    total = plus(keep, swap(send, "dp", 1))
    mp_steps = [("mp", 1 << bit) for bit in range(bits_of("mp"))]
    steps = mp_steps + [("dp", 1 << bit) for bit in range(bits_of("dp"))]
    queue = list(low_bits)
    pending = None
    for place, (axis, distance) in enumerate(steps):
        mine = pack.astype(LOW)
        theirs = swap(mine, axis, distance)
        if pending is not None:
            keep, got = pending
            total = plus(keep, once(got, mine))
            pending = None
        if place >= 1 and queue:
            bit = queue.pop(0)
            if bit == 2:
                total = jnp.concatenate([total, summed], axis=2)
            send, keep = halves(once(total, mine), bit)
            theirs = once(theirs, send)
            pending = (keep, swap(send, "dp", 1 << bit))
        pack = plus(mine, theirs)
    if pending is not None:
        total = plus(*pending)
    for bit in queue:
        send, keep = halves(total, bit)
        total = plus(keep, swap(send, "dp", 1 << bit))
    total = total.reshape(rows, 1536)
    own_qkv, own_mlp = total[:, :512], total[:, 512:]
    grad_qkv, grad_proj = run(
        unpack_qkv_kernel,
        [(own_qkv, WHOLE)],
        [(pinned(pltpu.HBM, *dims), held(*dims)) for dims in ((3, rows, 128), (rows, 128))],
        1, 8,
        grid=(1,),
    )
    grad_up, grad_down = run(
        unpack_mlp_kernel,
        [(own_mlp, WHOLE)],
        [(pinned(pltpu.HBM, rows, 512), held(rows, 512))] * 2,
        1, 8,
        grid=(1,),
    )
    grad_table, grad_gains, grad_biases, grad_pair, grad_hidden = run(
        rows_to_table_kernel,
        [(once(order, grad_qkv, grad_proj, grad_up, grad_down), WHOLE), (pack, WHOLE)],
        [(shaped(*dims), WHOLE) for dims in ((HEADS, REL), (2, D), (4, D), (2, D), (4, D))],
        4, 20,
    )
    return (
        out.reshape(inputs.shape),
        grad_x.reshape(inputs.shape),
        grad_qkv,
        grad_pair,
        grad_proj.T,
        grad_up,
        grad_hidden.reshape(FF),
        grad_down.T,
        grad_gains,
        grad_biases,
        grad_table.T,
    )


def solution(mesh):
    placed = (
        P(("dp", "mp"), None),
        P(None, "dp", "mp"),
        P(),
        P("mp", "dp"),
        P("dp", "mp"),
        P(),
        P("mp", "dp"),
        P(),
        P(),
        P(),
        P("dp", None),
        P(),
        P(("dp", "mp"), None),
    )
    return jax.shard_map(
        body,
        mesh=mesh,
        in_specs=placed,
        out_specs=(
            P(("dp", "mp"), None),
            P(("dp", "mp"), None),
            P(None, "dp", "mp"),
            P(),
            P("mp", "dp"),
            P("dp", "mp"),
            P(),
            P("mp", "dp"),
            P(),
            P(),
            P(),
        ),
        check_vma=False,
    )
```

```python
import functools

import jax
import jax.numpy as jnp
from jax import lax
from jax.experimental import pallas as pl
from jax.experimental.pallas import tpu as pltpu
from jax.sharding import PartitionSpec as P

D = 512
HEADS = 16
HD = 32
FF = 2048
WT = 8
WH = 7
WW = 7
GT = 16
GH = 14
GW = 14
WIN = 392
REL = 2535
RELP = 2560
PACK = RELP + D
WINS = 8
PARTS = 4
GHEADS = HEADS // PARTS
LOG2E = 1.4426950408889634
SCALE = HD ** (-0.5)
LOW = jnp.bfloat16
F32 = jnp.float32
NN = (((1,), (0,)), ((), ()))
NT = (((1,), (1,)), ((), ()))
ROW_CUTS = ((0, 64), (64, 64), (128, 64), (192, 64), (256, 64), (320, 72))
LANE_CUTS = ((0, 1024), (768, 1920), (1664, 2560))


def product(left, right, dims=NN):
    return lax.dot_general(left, right, dims, preferred_element_type=F32)


def shaped(*dims, kind=F32):
    return jax.ShapeDtypeStruct(dims, kind)


def cost(micros):
    return pl.CostEstimate(flops=int(micros * 1e9), bytes_accessed=int(micros * 3.6e6), transcendentals=0)


WHOLE = pl.BlockSpec(memory_space=pltpu.VMEM)
ANYWHERE = pl.BlockSpec(memory_space=pl.ANY)
SCALAR = pl.BlockSpec(memory_space=pltpu.SMEM)
FAR = pl.BlockSpec(memory_space=pltpu.HBM)


def run(kernel, ins, outs, micros, mib, grid=(), scratch=(), after=()):
    count = len(ins)

    def inner(*refs):
        kernel(*refs[:count], *refs[count + len(after) :])

    return pl.pallas_call(
        inner,
        grid=grid,
        out_shape=[o[0] for o in outs],
        in_specs=[i[1] for i in ins] + [ANYWHERE] * len(after),
        out_specs=[o[1] for o in outs],
        scratch_shapes=list(scratch),
        cost_estimate=cost(micros),
        compiler_params=pltpu.CompilerParams(vmem_limit_bytes=mib << 20),
    )(*[i[0] for i in ins], *after)


def pinned(space, *dims, kind=F32):
    return space(dims, kind)


def once(value, *others):
    return lax.optimization_barrier((value, *others))[0]


def held(*dims):
    return pl.BlockSpec(dims, lambda e: (0,) * len(dims))


def normed(values):
    centred = values - jnp.mean(values, -1, keepdims=True)
    rstd = lax.rsqrt(jnp.mean(centred * centred, -1, keepdims=True) + 1e-05)
    return centred * rstd, rstd


def first_norm_kernel(part_ref, shift_ref, x_ref, gain_ref, tb_ref, place_ref, a1_ref, a1t_ref, rf_ref, rft_ref):
    codes = lax.broadcasted_iota(jnp.int32, (128, WIN), 0)
    for w in range(2):
        window = (2 * part_ref[0] + w) % WINS
        region = jnp.zeros((1, WIN), jnp.int32)
        for axis, (length, size, along) in enumerate(
            ((WT, GT, window // 4), (WH, GH, window // 2 % 2), (WW, GW, window % 2))
        ):
            cell = place_ref[axis : axis + 1, :] + along * length
            halves_in = (cell >= size - length).astype(jnp.int32)
            shifted = (cell >= size - shift_ref[0, axis]).astype(jnp.int32)
            region = region * 3 + halves_in + shifted
        vhat, _ = normed(x_ref[w])
        a1 = vhat * gain_ref[0:1, :] + tb_ref[0:1, :]
        a1_ref[w] = a1.astype(LOW)
        a1t_ref[w] = a1.T.astype(LOW)
        differs = jnp.where(codes == region, 0.0, 1.0)
        rft_ref[w] = differs.astype(LOW)
        rf_ref[w] = ((1.0 - differs.T) * -1e30).astype(LOW)


def rest_kernel(proj_ref, up_ref, down_ref, out_ref):
    out_ref[...] = jnp.concatenate([proj_ref[...], up_ref[...], down_ref[...]], axis=1).astype(LOW)


def split3(values):
    high = values.astype(LOW)
    rest = values - high.astype(F32)
    mid = rest.astype(LOW)
    return high, mid, (rest - mid.astype(F32)).astype(LOW)


def rows_from_table_kernel(order_ref, table_ref, lane_ref, column_ref, out_ref, *picks):
    table = jnp.concatenate(split3(table_ref[...]), axis=0)
    rows = lax.broadcasted_iota(jnp.int32, (REL, 256), 0)
    for block in range(RELP // 256):
        cols = slice(block * 256, block * 256 + 256)
        picked = jnp.where(rows == order_ref[:, cols], 1.0, 0.0).astype(LOW)
        got = product(table, picked)
        out_ref[:, cols] = (got[:HEADS] + got[HEADS : 2 * HEADS] + got[2 * HEADS :]) * LOG2E
    for block in range(3):
        low, high = LANE_CUTS[block]
        cols = slice(block * 256, block * 256 + 256)
        down = lax.broadcasted_iota(jnp.int32, (high - low, 256), 0) + low
        picks[block][...] = jnp.where(down == lane_ref[:, cols], 1.0, 0.0).astype(LOW)
        across = lax.broadcasted_iota(jnp.int32, (256, high - low), 1) + low
        picks[3 + block][...] = jnp.where(across == column_ref[cols, :], 1.0, 0.0).astype(LOW)


def rows_to_table_kernel(order_ref, pack_ref, out_ref, gains_ref, biases_ref, pair_ref, hidden_ref):
    rows = jnp.concatenate(split3(pack_ref[:, 0:RELP]), axis=0)
    ids = lax.broadcasted_iota(jnp.int32, (256, RELP), 0)
    for start in range(0, REL, 256):
        count = min(256, REL - start)
        picked = jnp.where(ids + start == order_ref[...], 1.0, 0.0).astype(LOW)
        got = product(rows, picked, NT)
        got = got[:HEADS] + got[HEADS : 2 * HEADS] + got[2 * HEADS :]
        out_ref[:, start : start + count] = got[:, :count]
    cols = slice(RELP, PACK)
    for i, at in enumerate((0, 2)):
        gains_ref[i : i + 1, :] = pack_ref[at : at + 1, cols]
    for i, at in enumerate((1, 4, 3, 5)):
        biases_ref[i : i + 1, :] = pack_ref[at : at + 1, cols]
    pair_ref[...] = pack_ref[6:8, cols]
    hidden_ref[...] = pack_ref[8:12, cols]


def unpack_qkv_kernel(qkv_ref, out_ref, proj_ref):
    for i in range(3):
        out_ref[i] = qkv_ref[:, 128 * i : 128 * i + 128]
    proj_ref[...] = qkv_ref[:, 384:512]


def unpack_mlp_kernel(mlp_ref, up_ref, down_ref):
    up_ref[...] = mlp_ref[0]
    down_ref[...] = mlp_ref[1]


def lanes_of(ti):
    off = 49 * (7 - ti)
    base = off // 128 * 128
    return base, off - base


def expand_kernel(pair, part_ref, rows_ref, p0, p1, p2, bias_ref, left_s, wide_s):
    group = 2 * pair + pl.program_id(0)
    base_row = (part_ref[0] ^ group) * GHEADS
    back = 7 - lax.broadcasted_iota(jnp.int32, (8, RELP), 0)
    for h in range(GHEADS):
        row = jnp.broadcast_to(rows_ref[pl.ds(base_row + h, 1), :], (8, RELP))
        for bit in range(3):
            row = jnp.where(((back >> bit) & 1) == 1, pltpu.roll(row, RELP - (1 << bit), 1), row)
        for hi in range(WH):
            rolled = pltpu.roll(row, (1 - (6 - hi) * 13) % RELP, 1)
            at = 56 * h + 8 * hi
            left_s[at : at + 8, :] = rolled
    for block, pick in enumerate((p0, p1, p2)):
        low, high = LANE_CUTS[block]
        got = product(left_s[:, low:high].astype(LOW), pick[...])
        for h in range(GHEADS):
            wide_s[h, :, block * 256 : block * 256 + 256] = got[56 * h : 56 * h + 56]
    for h in range(GHEADS):
        for ti in range(WT):
            base, by = lanes_of(ti)
            for hi in range(WH):
                tile = wide_s[h, 8 * hi : 8 * hi + 8, base : base + 512]
                if by:
                    tile = pltpu.roll(tile, 512 - by, 1)
                at = 49 * ti + 7 * hi
                bias_ref[h, at : at + 7, :] = tile[:7, :WIN]


def expand_bias(pair, part, rows, picks, after):
    return run(
        functools.partial(expand_kernel, pair),
        [(part, SCALAR), (rows, WHOLE)] + [(p, WHOLE) for p in picks],
        [(shaped(2 * GHEADS, WIN, WIN), pl.BlockSpec((GHEADS, WIN, WIN), lambda g: (g, 0, 0)))],
        5, 14,
        grid=(2,),
        scratch=[pltpu.VMEM((56 * GHEADS, RELP), F32), pltpu.VMEM((GHEADS, 56, 768), F32)],
        after=after,
    )[0]


def shrunk(wide_refs, picks, spread_s, out_ref, at):
    heads = wide_refs.shape[0]
    used = (lax.broadcasted_iota(jnp.int32, (56, 256), 0) & 7) < 7
    spread_s[...] = jnp.zeros(spread_s.shape, F32)
    for block, pick in enumerate(picks):
        low, high = LANE_CUTS[block]
        parts = []
        for h in range(heads):
            wide = jnp.where(used, wide_refs[h, :, block * 256 : block * 256 + 256], 0.0)
            near = wide.astype(LOW).astype(F32)
            parts += [near, wide - near]
        got = product(jnp.concatenate(parts, axis=0).astype(LOW), pick[...])
        for h in range(heads):
            spread_s[h, :, low:high] += got[112 * h : 112 * h + 56] + got[112 * h + 56 : 112 * h + 112]
    left = 7 - lax.broadcasted_iota(jnp.int32, (8, RELP), 0)
    for h in range(heads):
        total = jnp.zeros((8, RELP), F32)
        for hi in range(WH):
            total += pltpu.roll(spread_s[h, 8 * hi : 8 * hi + 8, :], ((6 - hi) * 13 - 1) % RELP, 1)
        for bit in range(3):
            total = jnp.where(((left >> bit) & 1) == 1, pltpu.roll(total, 1 << bit, 1), total)
        out_ref[pl.ds(at + h, 1), 0:RELP] = jnp.sum(total, axis=0, keepdims=True)


def shrink_kernel(wide_ref, p0, p1, p2, out_ref, spread_s):
    shrunk(wide_ref, (p0, p1, p2), spread_s, out_ref, 0)


def shrink_bias(wide, picks, after):
    return run(
        shrink_kernel,
        [(wide, WHOLE)] + [(p, WHOLE) for p in picks],
        [(shaped(GHEADS, RELP), WHOLE)],
        1.4, 12,
        scratch=[pltpu.VMEM((GHEADS, 56, RELP), F32)],
        after=after,
    )[0]


P_SLOTS = 3


def attend_kernel(
    pair, part_ref, a1_ref, wa_ref, wb_ref, qvb_ref, bias_ref, rf_ref, rft_ref,
    p_ref, qt_ref, k_ref, vt_ref, o_ref, li_ref,
    q_s, ka_s, v_s, s_s, acc_s, p_s, p_sem,
):
    lane = lax.broadcasted_iota(jnp.int32, (WIN, 128), 1) // HD
    zero = jnp.zeros((WIN, 128), LOW)

    def away(at):
        slot = at % P_SLOTS
        return pltpu.make_async_copy(p_s.at[slot], p_ref.at[at], p_sem.at[slot])

    for g, w_ref in enumerate((wa_ref, wb_ref)):
        cols = pl.ds(pl.multiple_of((part_ref[0] ^ (2 * pair + g)) * 128, 128), 128)
        for w in range(2):
            qkv = product(a1_ref[w], w_ref[:, 0:384] if w_ref.shape[1] > 384 else w_ref[...])
            q = (qkv[:, :128] + qvb_ref[0:1, cols]) * (SCALE * LOG2E)
            k = qkv[:, 128:256]
            v = qkv[:, 256:384] + qvb_ref[1:2, cols]
            q_s[g, w] = q.astype(LOW)
            v_s[g, w] = v.astype(LOW)
            qt_ref[g, w] = q.T.astype(LOW)
            k_ref[g, w] = k.astype(LOW)
            vt_ref[g, w] = v.T.astype(LOW)
            ka_s[g, w, 0:128, :] = k.T.astype(LOW)
            ka_s[g, w, 128:256, :] = rft_ref[w]
        for e in range(GHEADS):
            at = GHEADS * g + e
            slot = at % P_SLOTS
            mine = lane == e
            if at >= P_SLOTS:
                away(at - P_SLOTS).wait()
            for w in range(2):
                q_wide = jnp.concatenate([jnp.where(mine, q_s[g, w], zero), rf_ref[w]], axis=1)
                s_s[at % 2, w] = product(q_wide, ka_s[g, w])
            for w in range(2):
                for start, count in ROW_CUTS:
                    rows = slice(start, start + count)
                    scores = s_s[at % 2, w, rows, :] + bias_ref[at, rows, :]
                    top = jnp.max(scores, axis=1, keepdims=True)
                    p_s[slot, w, rows, :] = jnp.exp2(scores - top).astype(LOW)
                v_wide = jnp.concatenate(
                    [jnp.where(mine, v_s[g, w], zero), jnp.where(mine, 1.0, 0.0).astype(LOW)], axis=1
                )
                part = product(p_s[slot, w], v_wide)
                acc_s[g, w] = part if e == 0 else acc_s[g, w] + part
            away(at).start()
        for w in range(2):
            inverse = 1.0 / acc_s[g, w, :, 128:256]
            li_ref[g, w] = inverse
            o_ref[g, w] = (acc_s[g, w, :, 0:128] * inverse).astype(LOW)
    for at in range(2 * GHEADS - P_SLOTS, 2 * GHEADS):
        away(at).wait()


def attend(pair, part, a1, weights, qvb, bias, rf, rft, after):
    return run(
        functools.partial(attend_kernel, pair),
        [(part, SCALAR)] + [(a, WHOLE) for a in (a1, *weights, qvb, bias, rf, rft)],
        [
            (pinned(pltpu.HBM, 2 * GHEADS, 2, WIN, WIN, kind=LOW), FAR),
            (pinned(pltpu.HBM, 2, 2, 128, WIN, kind=LOW), WHOLE),
            (pinned(pltpu.HBM, 2, 2, WIN, 128, kind=LOW), WHOLE),
            (pinned(pltpu.HBM, 2, 2, 128, WIN, kind=LOW), WHOLE),
            (shaped(2, 2, WIN, 128, kind=LOW), WHOLE),
            (pinned(pltpu.HBM, 2, 2, WIN, 128), WHOLE),
        ],
        2, 28,
        scratch=[
            pltpu.VMEM((2, 2, WIN, 128), LOW),
            pltpu.VMEM((2, 2, 256, WIN), LOW),
            pltpu.VMEM((2, 2, WIN, 128), LOW),
            pltpu.VMEM((2, 2, WIN, WIN), F32),
            pltpu.VMEM((2, 2, WIN, 256), F32),
            pltpu.VMEM((P_SLOTS, 2, WIN, WIN), LOW),
            pltpu.SemaphoreType.DMA((P_SLOTS,)),
        ],
        after=after,
    )


def attend_back_kernel(
    at, dop_ref, nd_ref, p_ref, qt_ref, k_ref, vt_ref, a1t_ref, gp_ref,
    dw_ref, wide_ref, low_ref, cs_ref,
    dop_s, nd_s, qt_s, k_s, vt_s, a1t_s, gp_s, p_s, dopt_s, dp_s, ds_s, dq_s, dkt_s, dvt_s, db_s, sems,
):
    lane = lax.broadcasted_iota(jnp.int32, (WIN, 128), 1) // HD
    zero = jnp.zeros((WIN, 128), LOW)
    inside = lax.broadcasted_iota(jnp.int32, (8, 512), 1) < WIN
    names = ("dop", "nd", "vt", "qt", "k", "gp", "a1t")
    sources = (dop_ref.at[at], nd_ref.at[at], vt_ref.at[at], qt_ref.at[at], k_ref.at[at], gp_ref.at[at], a1t_ref)
    targets = (dop_s, nd_s, vt_s, qt_s, k_s, gp_s, a1t_s)
    copies = {
        name: pltpu.make_async_copy(source, target, sems.at[i])
        for i, (name, source, target) in enumerate(zip(names, sources, targets))
    }
    probs = [
        pltpu.make_async_copy(p_ref.at[GHEADS * at + e], p_s.at[e], sems.at[len(names) + e]) for e in range(GHEADS)
    ]
    for name in ("dop", "nd", "vt"):
        copies[name].start()
    probs[0].start()
    copies["qt"].start()
    copies["k"].start()
    for e in range(1, GHEADS):
        probs[e].start()
    copies["a1t"].start()
    copies["gp"].start()
    for name in ("dop", "nd", "vt"):
        copies[name].wait()
    for w in range(2):
        dopt_s[w] = dop_s[w].astype(F32).T.astype(LOW)
    for e in range(GHEADS):
        mine = lane == e
        own = slice(HD * e, HD * e + HD)
        slot = e % 2
        for w in range(2):
            wide = jnp.concatenate([jnp.where(mine, dop_s[w], zero), jnp.where(mine, nd_s[w], zero)], axis=1)
            v_wide = jnp.concatenate([vt_s[w], jnp.ones((128, WIN), LOW)], axis=0)
            dp_s[slot, w] = product(wide, v_wide)
        probs[e].wait()
        for w in range(2):
            dvt_s[w, own, :] = product(dopt_s[w, own, :], p_s[e, w])
        for start, count in ROW_CUTS:
            rows = slice(start, start + count)
            one = p_s[e, 0, rows, :].astype(F32) * dp_s[slot, 0, rows, :]
            two = p_s[e, 1, rows, :].astype(F32) * dp_s[slot, 1, rows, :]
            db_s[slot, rows, 0:WIN] = one + two
            ds_s[slot, 0, rows, :] = one.astype(LOW)
            ds_s[slot, 1, rows, :] = two.astype(LOW)
        if e == 0:
            copies["qt"].wait()
            copies["k"].wait()
        for w in range(2):
            dkt_s[w, own, :] = product(qt_s[w, own, :], ds_s[slot, w])
            part = product(ds_s[slot, w], jnp.where(mine, k_s[w], zero))
            dq_s[w] = part if e == 0 else dq_s[w] + part
        for hi in range(WH):
            own_rows = slice(8 * hi, 8 * hi + 8)
            wide_ref[e, own_rows, :] = jnp.zeros((8, 768), F32)
            for base in (0, 128, 256):
                total = jnp.zeros((8, 512), F32)
                for ti in range(WT):
                    lane_base, by = lanes_of(ti)
                    if lane_base != base:
                        continue
                    first_row = 49 * ti + 7 * hi
                    tile = jnp.where(inside, db_s[slot, first_row : first_row + 8, :], 0.0)
                    total += pltpu.roll(tile, by, 1) if by else tile
                wide_ref[e, own_rows, base : base + 512] += total
    copies["a1t"].wait()
    copies["gp"].wait()
    sum_q = jnp.zeros((1, 128), F32)
    sum_v = jnp.zeros((1, 128), F32)
    grad = jnp.zeros((D, 384), F32)
    for w in range(2):
        dq = dq_s[w] * SCALE
        dk = (dkt_s[w] * (1.0 / LOG2E)).T
        dv = dvt_s[w].T
        sum_q += jnp.sum(dq, axis=0, keepdims=True)
        sum_v += jnp.sum(dv, axis=0, keepdims=True)
        low = jnp.concatenate([dq, dk, dv], axis=1).astype(LOW)
        low_ref[w] = low
        grad += product(a1t_s[w], low)
    dw_ref[:, 0:384] = grad.astype(LOW)
    dw_ref[:, 384:512] = gp_s[...]
    cs_ref[0:1, :] = sum_q
    cs_ref[1:2, :] = sum_v


def attend_back(at, dop, nd, kept, a1t, gproj, after):
    p, qt, k, vt, _, _ = kept
    return run(
        functools.partial(attend_back_kernel, at),
        [(pltpu.with_memory_space_constraint(a, pltpu.HBM), FAR) for a in (dop, nd, p, qt, k, vt, a1t, gproj)],
        [
            (shaped(D, 512, kind=LOW), WHOLE),
            (shaped(GHEADS, 56, 768), WHOLE),
            (shaped(2, WIN, 384, kind=LOW), WHOLE),
            (shaped(2, 128), WHOLE),
        ],
        6, 24,
        scratch=[
            pltpu.VMEM((2, WIN, 128), LOW),
            pltpu.VMEM((2, WIN, 128), LOW),
            pltpu.VMEM((2, 128, WIN), LOW),
            pltpu.VMEM((2, WIN, 128), LOW),
            pltpu.VMEM((2, 128, WIN), LOW),
            pltpu.VMEM((2, D, WIN), LOW),
            pltpu.VMEM((D, 128), LOW),
            pltpu.VMEM((GHEADS, 2, WIN, WIN), LOW),
            pltpu.VMEM((2, 128, WIN), LOW),
            pltpu.VMEM((2, 2, WIN, WIN), F32),
            pltpu.VMEM((2, 2, WIN, WIN), LOW),
            pltpu.VMEM((2, WIN, 128), F32),
            pltpu.VMEM((2, 128, WIN), F32),
            pltpu.VMEM((2, 128, WIN), F32),
            pltpu.VMEM((2, 400, 512), F32),
            pltpu.SemaphoreType.DMA((7 + GHEADS,)),
        ],
        after=after,
    )


def gelu_parts(v):
    size = jnp.abs(v)
    t = 1.0 / (1.0 + (0.3275911 * 0.7071067811865476) * size)
    bell = jnp.exp2(v * v * (-0.5 * LOG2E))
    poly = t * (0.127414796 + t * (-0.142248368 + t * (0.7107068705 + t * (-0.7265760135 + t * 0.5307027145))))
    tail = poly * bell
    phi = jnp.where(v >= 0.0, 1.0 - tail, tail)
    return v * phi, phi + v * bell * 0.3989422804014327


def norm_back(values, dy, gain):
    vhat, rstd = normed(values)
    scaled = dy * gain
    dv = rstd * (
        scaled - jnp.mean(scaled, -1, keepdims=True) - vhat * jnp.mean(scaled * vhat, -1, keepdims=True)
    )
    return dv, jnp.sum(dy * vhat, axis=0, keepdims=True), jnp.sum(dy, axis=0, keepdims=True)


ROWS = 2 * WIN


def before_kernel(
    on_ref, of_ref, x_ref, cot_ref, tb_ref, gain_ref, u0, u1, u2, u3,
    after_ref, a2_ref, a2t_ref, g_ref, gt_ref,
):
    weight = jnp.concatenate([u[:, 0:128] for u in (u0, u1, u2, u3)], axis=1)
    lows = []
    for w in range(2):
        mixed = jnp.concatenate([on_ref[0, w], on_ref[1, w], of_ref[0, w], of_ref[1, w]], axis=1)
        after = x_ref[w] + product(mixed, weight, NT) + tb_ref[1:2, :]
        after_ref[w] = after
        vhat, _ = normed(after)
        lows.append(vhat * gain_ref[1:2, :] + tb_ref[2:3, :])
    a2 = jnp.concatenate(lows, axis=0)
    a2_ref[...] = a2.astype(LOW)
    a2t_ref[...] = a2.T.astype(LOW)
    cot = jnp.concatenate([cot_ref[0], cot_ref[1]], axis=0)
    g_ref[...] = cot.astype(LOW)
    gt_ref[...] = cot.T.astype(LOW)


def before(o_near, o_far, x, cot, biases, gains, ups):
    return run(
        before_kernel,
        [(o_near, WHOLE), (o_far, WHOLE)]
        + [(pltpu.with_memory_space_constraint(a, pltpu.HBM), held(2, WIN, D)) for a in (x, cot)]
        + [(a, WHOLE) for a in (biases, gains, *ups)],
        [
            (shaped(2, WIN, D), WHOLE), (shaped(ROWS, D, kind=LOW), WHOLE), (shaped(D, ROWS, kind=LOW), WHOLE),
            (shaped(ROWS, D, kind=LOW), WHOLE), (shaped(D, ROWS, kind=LOW), WHOLE),
        ],
        4, 20,
        grid=(1,),
    )


def feed_parts(
    first, part_ref, a2_ref, a2t_ref, g_ref, gt_ref, hb_ref, ups, own_ref, other_ref,
    out_ref, da2_ref, gup_ref, gdown_ref, ghb_ref, down_s, h_s, d_s, act_s, dh_s,
):
    count, block = own_ref.shape[1:3]
    for p in range(2):
        for z in range(count):
            for ref, place in ((own_ref, part_ref[1]), (other_ref, 1 - part_ref[1])):
                at = pl.multiple_of((2 * z + place) * block, block)
                down_s[p, pl.ds(at, block), :] = ref[p, z]
    downs = (down_s.at[0], down_s.at[1])

    def rise(p, half):
        cols = slice(256 * half, 256 * half + 256)
        h_s[p, :, cols] = product(a2_ref[...], ups[p][:, 128 + 256 * half : 384 + 256 * half])
        d_s[p, :, cols] = product(g_ref[...], downs[p][:, cols])

    def bend(p, half):
        for cut in range(256 * half, 256 * half + 256, 128):
            cols = slice(cut, cut + 128)
            line = hb_ref[(first + 2 * p) ^ part_ref[0], :, cols]
            sums = jnp.zeros((1, 128), F32)
            for start in range(0, ROWS, 112):
                rows = slice(start, start + 112)
                act, slope = gelu_parts(h_s[p, rows, cols] + line)
                act_s[p, rows, cols] = act.astype(LOW)
                grad = d_s[p, rows, cols] * slope
                sums += jnp.sum(grad, axis=0, keepdims=True)
                dh_s[p, rows, cols] = grad.astype(LOW)
            ghb_ref[p, :, cols] = sums

    def fall(p):
        for half in range(2):
            cols = slice(256 * half, 256 * half + 256)
            gup_ref[p, :, cols] = product(a2t_ref[...], dh_s[p, :, cols]).astype(LOW)
            gdown_ref[p, :, cols] = product(gt_ref[...], act_s[p, :, cols]).astype(LOW)
        out_ref[...] += product(act_s[p], downs[p][...], NT)
        da2_ref[...] += product(dh_s[p], ups[p][:, 128:640], NT)

    rise(0, 0)
    rise(0, 1)
    bend(0, 0)
    rise(1, 0)
    bend(0, 1)
    rise(1, 1)
    bend(1, 0)
    fall(0)
    bend(1, 1)
    fall(1)


def feed_odd_kernel(
    part_ref, a2_ref, a2t_ref, g_ref, gt_ref, hb_ref, ua, ub, own_ref, other_ref, after_ref, tb_ref,
    out_ref, da2_ref, gup_ref, gdown_ref, ghb_ref, *work,
):
    for w in range(2):
        out_ref[WIN * w : WIN * w + WIN, :] = after_ref[w] + tb_ref[3:4, :]
    da2_ref[...] = jnp.zeros((ROWS, D), F32)
    feed_parts(
        1, part_ref, a2_ref, a2t_ref, g_ref, gt_ref, hb_ref, (ua, ub), own_ref, other_ref,
        out_ref, da2_ref, gup_ref, gdown_ref, ghb_ref, *work,
    )


def feed_even_kernel(
    part_ref, a2_ref, a2t_ref, g_ref, gt_ref, hb_ref, ua, ub, own_ref, other_ref, after_ref,
    out_in, da2_in, on_ref, of_ref, lin_ref, lif_ref, cot_ref, gain_ref, uc, ud,
    out_ref, gup_ref, gdown_ref, ghb_ref, dafter_ref, dn_ref, df_ref, nn_ref, nf_ref, gpn_ref, gpf_ref, sums_ref,
    da2_s, *work,
):
    out_ref[...] = out_in[...]
    da2_s[...] = da2_in[...]
    feed_parts(
        0, part_ref, a2_ref, a2t_ref, g_ref, gt_ref, hb_ref, (ua, ub), own_ref, other_ref,
        out_ref, da2_s, gup_ref, gdown_ref, ghb_ref, *work,
    )
    weight = jnp.concatenate([u[:, 0:128] for u in (ua, uc, ub, ud)], axis=1)
    grad = jnp.zeros((D, D), F32)
    sums = [jnp.zeros((1, D), F32) for _ in range(4)]
    for w in range(2):
        own = slice(WIN * w, WIN * w + WIN)
        dv, dgain, doff = norm_back(after_ref[w], da2_s[own, :], gain_ref[1:2, :])
        cot = cot_ref[w]
        dafter = cot + dv
        dafter_ref[w] = dafter
        turned = dafter.T.astype(LOW)
        dmix = product(dafter.astype(LOW), weight)
        for i in range(PARTS):
            at = i % 2
            d_ref, n_ref, l_ref, m_ref = (
                (dn_ref, nn_ref, lin_ref, on_ref) if i < 2 else (df_ref, nf_ref, lif_ref, of_ref)
            )
            dop = (dmix[:, 128 * i : 128 * i + 128] * l_ref[at, w]).astype(LOW)
            d_ref[at, w] = dop
            n_ref[at, w] = (-(dop.astype(F32) * m_ref[at, w].astype(F32))).astype(LOW)
        grad += product(turned, jnp.concatenate([on_ref[0, w], on_ref[1, w], of_ref[0, w], of_ref[1, w]], axis=1))
        parts = (dgain, doff, jnp.sum(dafter, axis=0, keepdims=True), jnp.sum(cot, axis=0, keepdims=True))
        for i, part in enumerate(parts):
            sums[i] += part
    for i, (ref, at) in enumerate(((gpn_ref, 0), (gpn_ref, 1), (gpf_ref, 0), (gpf_ref, 1))):
        ref[at] = grad[:, 128 * i : 128 * i + 128].astype(LOW)
    for i in range(4):
        sums_ref[i : i + 1, :] = sums[i]


FEED_WORK = [
    pltpu.VMEM((2, 512, 512), LOW),
    pltpu.VMEM((2, ROWS, 512), F32), pltpu.VMEM((2, ROWS, 512), F32),
    pltpu.VMEM((2, ROWS, 512), LOW), pltpu.VMEM((2, ROWS, 512), LOW),
]
STEP_OUTS = [(shaped(2, D, 512, kind=LOW), WHOLE), (shaped(2, D, 512, kind=LOW), WHOLE), (shaped(2, 1, 512), WHOLE)]


def feed_odd(part, known, hb, ups, downs, after, biases):
    return run(
        feed_odd_kernel,
        [(part, SCALAR)] + [(a, WHOLE) for a in (*known, hb, *ups, *downs, after, biases)],
        [(shaped(ROWS, D), WHOLE), (shaped(ROWS, D), WHOLE), *STEP_OUTS],
        9, 28,
        scratch=FEED_WORK,
    )


def feed_even(part, known, hb, ups, downs, after, out, da2, o_near, o_far, li_near, li_far, cot, gains, others):
    return run(
        feed_even_kernel,
        [(part, SCALAR)]
        + [
            (a, WHOLE)
            for a in (
                *known, hb, *ups, *downs, after, out, da2, o_near, o_far, li_near, li_far, cot, gains, *others,
            )
        ],
        [
            (shaped(ROWS, D), WHOLE), *STEP_OUTS, (shaped(2, WIN, D), WHOLE),
            *[(pinned(pltpu.HBM, 2, 2, WIN, 128, kind=LOW), WHOLE)] * 4,
            *[(pinned(pltpu.HBM, 2, D, 128, kind=LOW), WHOLE)] * 2,
            (shaped(4, D), WHOLE),
        ],
        13, 32,
        scratch=[pltpu.VMEM((ROWS, D), F32), *FEED_WORK],
    )


def last_kernel(
    part_ref, x_ref, dafter_ref, gain_ref, l0, l1, l2, l3, w0, w1, w2, w3,
    c0, c1, c2, c3, two_ref, odd_ref, even_ref, wide_ref, p0, p1, p2, e1, e2, e3,
    gx_ref, pack_ref, spread_s, pack_s,
):
    sums = [jnp.zeros((1, D), F32) for _ in range(2)]
    for w in range(2):
        da1 = jnp.zeros((WIN, D), F32)
        for low, wt in ((l0, w0), (l1, w1), (l2, w2), (l3, w3)):
            da1 += product(low[w], wt[...], NT)
        dv, dgain, doff = norm_back(x_ref[w], da1, gain_ref[0:1, :])
        gx_ref[w] = dafter_ref[w] + dv
        sums[0] += dgain
        sums[1] += doff
    cols = slice(RELP, PACK)
    pack_s[0:1, cols] = sums[0]
    pack_s[1:2, cols] = sums[1]
    pack_s[2:6, cols] = two_ref[...]
    for group, c in enumerate((c0, c1, c2, c3)):
        own = pl.ds(pl.multiple_of(RELP + (part_ref[0] ^ group) * 128, 128), 128)
        pack_s[6:8, own] = c[...]
    for i in range(PARTS):
        pack_s[pl.ds(8 + (part_ref[0] ^ i), 1), cols] = (odd_ref if i % 2 else even_ref)[i // 2]
    pack_s[12:16, cols] = jnp.zeros((4, D), F32)
    for group, rows in enumerate((e1, e2, e3)):
        for h in range(GHEADS):
            pack_s[pl.ds((part_ref[0] ^ (group + 1)) * GHEADS + h, 1), 0:RELP] = rows[h : h + 1, :]
    shrunk(wide_ref, (p0, p1, p2), spread_s, pack_s, part_ref[0] * GHEADS)
    pack_ref[...] = pack_s[...].astype(LOW)


def swap(values, axis, distance):
    count = lax.axis_size(axis)
    return lax.ppermute(values, axis, [(i, i ^ distance) for i in range(count)])


def bits_of(axis):
    return (lax.axis_size(axis) - 1).bit_length()


def interleaved(own, other, upper):
    place = jnp.arange(2, dtype=jnp.int32).reshape(1, 2, *(1,) * (own.ndim - 1))
    mine = place == upper.astype(jnp.int32)
    return jnp.where(mine, own[:, None], other[:, None]).reshape(-1, *own.shape[1:])


def upper_of(axis, bit):
    return (lax.axis_index(axis) >> bit) % 2 == 1


def gathered(blocks, bits):
    for bit in bits:
        blocks = interleaved(blocks, swap(blocks, "dp", 1 << bit), upper_of("dp", bit))
    return blocks


def flat(blocks):
    return blocks.reshape(-1, blocks.shape[-1])


def half(total, bit, mine):
    pairs = total.reshape(-1, 2, *total.shape[1:])
    return jnp.where(upper_of("dp", bit) == mine, pairs[:, 1], pairs[:, 0])


def halves(total, bit):
    return half(total, bit, False).astype(LOW), half(total, bit, True).astype(F32)


def plus(one, two):
    return one.astype(F32) + two.astype(F32)


def offset_order(rel_index):
    corners = rel_index.reshape(WT, WH, WW, WIN)[::7, ::6, ::6].reshape(2, 2, 2, WT, WH, WW)
    joined = jnp.concatenate([corners[1], corners[0][:, :, 1:]], axis=2)
    joined = jnp.concatenate([joined[1], joined[0][:, :, 1:]], axis=2)
    joined = jnp.concatenate([joined[1], joined[0][:, :, 1:]], axis=2)
    return jnp.pad(joined.reshape(1, REL), ((0, 0), (0, RELP - REL)), constant_values=-1)


def body(
    inputs,
    w_qkv,
    qv_bias,
    w_proj,
    w_fc1,
    fc1_bias,
    w_fc2,
    norm_gains,
    token_biases,
    table,
    shifts,
    rel_index,
    cotangent,
):
    index = lax.axis_index("mp")
    part = index.astype(jnp.int32).reshape(1)
    rows = w_qkv.shape[1]
    x = inputs.reshape(2, WIN, D)
    cot = cotangent.reshape(2, WIN, D)
    high_bits = tuple(reversed(range(1, bits_of("dp"))))
    low_bits = tuple(range(1, bits_of("dp")))

    shard_qkv = w_qkv.transpose(1, 0, 2).reshape(1, rows, 384).astype(LOW)
    (shard_rest,) = run(
        rest_kernel,
        [(a, WHOLE) for a in (w_proj.T, w_fc1, w_fc2.T)],
        [(shaped(rows, 1152, kind=LOW), WHOLE)],
        1, 8,
    )
    shard_rest = shard_rest[None]
    qkv_first = gathered(shard_qkv, high_bits[:1])
    qkv_high = gathered(qkv_first, high_bits[1:])
    own = flat(gathered(qkv_high, (0,)))
    qkv_parts = [own, swap(own, "mp", 1)]
    across = swap(own, "mp", 2)
    rest = gathered(shard_rest, high_bits)
    up_own = gathered(rest[:, :, :640], (0,))
    up_across = swap(up_own, "mp", 2)
    down_across = swap(rest[:, :, 640:], "mp", 2)
    places = jnp.arange(WIN, dtype=jnp.int32)
    places = jnp.stack([places // (WH * WW), places // WW % WH, places % WW])
    order = offset_order(once(rel_index, qkv_first))
    column = jnp.arange(768, dtype=jnp.int32)
    lane_row = jnp.where(
        column < 15 * 49, column // 49 * 169 + column % 49 // 7 * 13 + column % 7, -1
    )
    a1, a1t, rf, rft = run(
        first_norm_kernel,
        [(part, SCALAR), (shifts, SCALAR)] + [(a, WHOLE) for a in (x, norm_gains, token_biases, places)],
        [
            (shaped(2, WIN, D, kind=LOW), WHOLE), (pinned(pltpu.HBM, 2, D, WIN, kind=LOW), WHOLE),
            (shaped(2, WIN, 128, kind=LOW), WHOLE), (shaped(2, 128, WIN, kind=LOW), WHOLE),
        ],
        2, 16,
        after=(qkv_first,),
    )
    row_offsets, *picks = run(
        rows_from_table_kernel,
        [(a, WHOLE) for a in (order, table.T, lane_row.reshape(1, 768), lane_row.reshape(768, 1))],
        [(shaped(HEADS, RELP), WHOLE)]
        + [(shaped(high - low, 256, kind=LOW), WHOLE) for low, high in LANE_CUTS]
        + [(shaped(256, high - low, kind=LOW), WHOLE) for low, high in LANE_CUTS],
        4, 20,
        after=(qkv_high,),
    )
    out_picks, back_picks = picks[:3], picks[3:]
    near_bias = expand_bias(0, part, row_offsets, out_picks, (qkv_high,))
    near = attend(0, part, a1, qkv_parts[:2], qv_bias, near_bias, rf, rft, (rest,))
    across = once(across, near[4])
    qkv_parts += [across, swap(across, "mp", 1)]
    far_bias = expand_bias(1, part, row_offsets, out_picks, (near[4], up_own))
    down_pair = jnp.stack([rest[:, :, 640:], once(down_across, far_bias)], axis=0)
    down_other = swap(down_pair, "dp", 1)
    far = attend(1, part, a1, qkv_parts[2:], qv_bias, far_bias, rf, rft, (up_own, down_pair))
    up_parts = [flat(up_own), flat(swap(up_own, "mp", 1)), flat(up_across), flat(swap(once(up_across, far[4]), "mp", 1))]
    hb = fc1_bias.reshape(PARTS, 1, 512)
    after, *known = before(near[4], far[4], x, cot, token_biases, norm_gains, up_parts)
    down_other = once(down_other, far[4])
    upper = upper_of("dp", 0).astype(jnp.int32).reshape(1)
    if rows % 16:
        joined = jnp.stack([flat(interleaved(down_pair[i], down_other[i], upper_of("dp", 0))) for i in range(2)])
        joined = joined.reshape(2, 2, 1, D // 2, 512)
        down_pair, down_other, upper = joined[:, 0], joined[:, 1], jnp.zeros((1,), jnp.int32)
    places_of = jnp.concatenate([part, upper])
    down_even = (down_pair, down_other)
    down_odd = [swap(a, "mp", 1) for a in down_even]
    out, da2, odd_up, odd_down, hb_odd = feed_odd(
        places_of, known, hb, up_parts[1::2], down_odd, after, token_biases
    )
    out, even_up, even_down, hb_even, dafter, dop_near, dop_far, nd_near, nd_far, gp_near, gp_far, sums_two = feed_even(
        places_of, known, hb, up_parts[::2], down_even, after, out, da2,
        near[4], far[4], near[5], far[5], cot, norm_gains, up_parts[1::2],
    )
    got_up = swap(odd_up, "mp", 1).reshape(2, -1, rows, 512)
    got_down = swap(odd_down, "mp", 1).reshape(2, -1, rows, 512)
    even_up = even_up.reshape(2, -1, rows, 512)
    even_down = even_down.reshape(2, -1, rows, 512)
    up_send = plus(even_up[1], got_up[1]).astype(LOW)
    turned = [a.transpose(1, 0, 2, 3) for a in (even_down, got_down)]
    down_send = plus(*(half(a, 0, False) for a in turned)).astype(LOW)
    three, wide3, low3, col3 = attend_back(1, dop_far, nd_far, far, a1t, gp_far, (up_send, down_send))
    two, wide2, low2, col2 = attend_back(0, dop_far, nd_far, far, a1t, gp_far, (three,))
    up_sum = plus(plus(even_up[0], got_up[0]), swap(up_send, "mp", 2))
    down_sum = plus(plus(*(half(a, 0, True) for a in turned)), swap(down_send, "dp", 1))
    far_sum = plus(two, swap(three, "mp", 1)).astype(LOW)
    up_send, up_keep = halves(up_sum, 0)
    down_send, down_keep = down_sum[:, 1].astype(LOW), down_sum[:, 0]
    one, wide1, low1, col1 = attend_back(
        1, dop_near, nd_near, near, a1t, gp_near, (far_sum, up_send, down_send)
    )
    far_sum = swap(far_sum, "mp", 2)
    up_sum = plus(up_keep, swap(up_send, "dp", 1))
    down_sum = plus(down_keep, swap(down_send, "mp", 2))
    summed = jnp.stack([up_sum, down_sum], axis=1)
    top = bits_of("dp") - 1
    is_top = upper_of("dp", top)
    ends = summed.reshape(2, -1, 2, rows, 512)
    mlp_send = jnp.where(is_top, ends[0], ends[1]).astype(LOW)
    mlp_keep = jnp.where(is_top, ends[1], ends[0])
    zero, wide0, low0, col0 = attend_back(0, dop_near, nd_near, near, a1t, gp_near, (mlp_send, one))
    summed = plus(mlp_keep, swap(mlp_send, "dp", 1 << top))
    total = plus(plus(zero, swap(one, "mp", 1)), far_sum).reshape(-1, rows, 512)
    rows_by = [shrink_bias(w, back_picks, ()) for w in (wide1, wide2, wide3)]
    send, keep = halves(total, 0)
    grad_x, pack = run(
        last_kernel,
        [(part, SCALAR)]
        + [
            (a, WHOLE)
            for a in (
                x, dafter, norm_gains, low0, low1, low2, low3, *qkv_parts, col0, col1, col2, col3,
                sums_two, hb_odd, hb_even, wide0, *back_picks, *rows_by,
            )
        ],
        [(shaped(2, WIN, D), WHOLE), (shaped(HEADS, PACK, kind=LOW), WHOLE)],
        4, 20,
        scratch=[pltpu.VMEM((GHEADS, 56, RELP), F32), pltpu.VMEM((HEADS, PACK), F32)],
        after=(send,),
    )
    total = plus(keep, swap(send, "dp", 1))
    mp_steps = [("mp", 1 << bit) for bit in range(bits_of("mp"))]
    steps = mp_steps + [("dp", 1 << bit) for bit in range(bits_of("dp"))]
    queue = list(low_bits)
    pending = None

    def settled(bit, keep, got):
        if bit == top:
            return plus(keep[0], got), keep[1]
        count = keep[0].shape[0]
        mlp_got = got[count:].reshape(keep[1].shape)
        return plus(keep[0], got[:count]), plus(keep[1], mlp_got)

    def parted(bit, total, summed):
        send, keep = halves(total, bit)
        if bit == top:
            return send, (keep, summed)
        mlp_send, mlp_keep = halves(summed, bit)
        return jnp.concatenate([send, mlp_send.reshape(-1, rows, 512)], axis=0), (keep, mlp_keep)

    for place, (axis, distance) in enumerate(steps):
        mine = pack.astype(LOW)
        theirs = swap(mine, axis, distance)
        if pending is not None:
            bit, keep, got = pending
            total, summed = settled(bit, keep, once(got, mine))
            pending = None
        if place >= 1 and queue:
            bit = queue.pop(0)
            send, keep = parted(bit, once(total, mine), summed)
            theirs = once(theirs, send)
            pending = (bit, keep, swap(send, "dp", 1 << bit))
        pack = plus(mine, theirs)
    if pending is not None:
        total, summed = settled(*pending)
    for bit in queue:
        send, keep = parted(bit, total, summed)
        total, summed = settled(bit, keep, swap(send, "dp", 1 << bit))
    own_qkv, own_mlp = total.reshape(rows, 512), summed.reshape(2, rows, 512)
    grad_qkv, grad_proj = run(
        unpack_qkv_kernel,
        [(own_qkv, WHOLE)],
        [(pinned(pltpu.HBM, *dims), held(*dims)) for dims in ((3, rows, 128), (rows, 128))],
        1, 8,
        grid=(1,),
    )
    grad_up, grad_down = run(
        unpack_mlp_kernel,
        [(own_mlp, WHOLE)],
        [(pinned(pltpu.HBM, rows, 512), held(rows, 512))] * 2,
        1, 8,
        grid=(1,),
    )
    grad_table, grad_gains, grad_biases, grad_pair, grad_hidden = run(
        rows_to_table_kernel,
        [(once(order, grad_qkv, grad_proj, grad_up, grad_down), WHOLE), (pack, WHOLE)],
        [(shaped(*dims), WHOLE) for dims in ((HEADS, REL), (2, D), (4, D), (2, D), (4, D))],
        4, 20,
    )
    return (
        out.reshape(inputs.shape),
        grad_x.reshape(inputs.shape),
        grad_qkv,
        grad_pair,
        grad_proj.T,
        grad_up,
        grad_hidden.reshape(FF),
        grad_down.T,
        grad_gains,
        grad_biases,
        grad_table.T,
    )


def solution(mesh):
    placed = (
        P(("dp", "mp"), None),
        P(None, "dp", "mp"),
        P(),
        P("mp", "dp"),
        P("dp", "mp"),
        P(),
        P("mp", "dp"),
        P(),
        P(),
        P(),
        P("dp", None),
        P(),
        P(("dp", "mp"), None),
    )
    return jax.shard_map(
        body,
        mesh=mesh,
        in_specs=placed,
        out_specs=(
            P(("dp", "mp"), None),
            P(("dp", "mp"), None),
            P(None, "dp", "mp"),
            P(),
            P("mp", "dp"),
            P("dp", "mp"),
            P(),
            P("mp", "dp"),
            P(),
            P(),
            P(),
        ),
        check_vma=False,
    )
```

```python
import functools

import jax
import jax.numpy as jnp
from jax import lax
from jax.experimental import pallas as pl
from jax.experimental.pallas import tpu as pltpu
from jax.sharding import PartitionSpec as P

D = 512
HEADS = 16
HD = 32
FF = 2048
WT = 8
WH = 7
WW = 7
GT = 16
GH = 14
GW = 14
WIN = 392
REL = 2535
RELP = 2560
PACK = RELP + D
WINS = 8
PARTS = 4
GHEADS = HEADS // PARTS
LOG2E = 1.4426950408889634
SCALE = HD ** (-0.5)
LOW = jnp.bfloat16
F32 = jnp.float32
NN = (((1,), (0,)), ((), ()))
NT = (((1,), (1,)), ((), ()))
ROW_CUTS = ((0, 64), (64, 64), (128, 64), (192, 64), (256, 64), (320, 72))
LANE_CUTS = ((0, 1024), (768, 1920), (1664, 2560))


def product(left, right, dims=NN):
    return lax.dot_general(left, right, dims, preferred_element_type=F32)


def shaped(*dims, kind=F32):
    return jax.ShapeDtypeStruct(dims, kind)


def cost(micros):
    return pl.CostEstimate(flops=int(micros * 1e9), bytes_accessed=int(micros * 3.6e6), transcendentals=0)


WHOLE = pl.BlockSpec(memory_space=pltpu.VMEM)
ANYWHERE = pl.BlockSpec(memory_space=pl.ANY)
SCALAR = pl.BlockSpec(memory_space=pltpu.SMEM)
FAR = pl.BlockSpec(memory_space=pltpu.HBM)


def run(kernel, ins, outs, micros, mib, grid=(), scratch=(), after=()):
    count = len(ins)

    def inner(*refs):
        kernel(*refs[:count], *refs[count + len(after) :])

    return pl.pallas_call(
        inner,
        grid=grid,
        out_shape=[o[0] for o in outs],
        in_specs=[i[1] for i in ins] + [ANYWHERE] * len(after),
        out_specs=[o[1] for o in outs],
        scratch_shapes=list(scratch),
        cost_estimate=cost(micros),
        compiler_params=pltpu.CompilerParams(vmem_limit_bytes=mib << 20),
    )(*[i[0] for i in ins], *after)


def pinned(space, *dims, kind=F32):
    return space(dims, kind)


def once(value, *others):
    return lax.optimization_barrier((value, *others))[0]


def held(*dims):
    return pl.BlockSpec(dims, lambda e: (0,) * len(dims))


def normed(values):
    centred = values - jnp.mean(values, -1, keepdims=True)
    rstd = lax.rsqrt(jnp.mean(centred * centred, -1, keepdims=True) + 1e-05)
    return centred * rstd, rstd


def first_norm_kernel(part_ref, shift_ref, x_ref, gain_ref, tb_ref, place_ref, a1_ref, a1t_ref, rf_ref, rft_ref):
    codes = lax.broadcasted_iota(jnp.int32, (128, WIN), 0)
    for w in range(2):
        window = (2 * part_ref[0] + w) % WINS
        region = jnp.zeros((1, WIN), jnp.int32)
        for axis, (length, size, along) in enumerate(
            ((WT, GT, window // 4), (WH, GH, window // 2 % 2), (WW, GW, window % 2))
        ):
            cell = place_ref[axis : axis + 1, :] + along * length
            halves_in = (cell >= size - length).astype(jnp.int32)
            shifted = (cell >= size - shift_ref[0, axis]).astype(jnp.int32)
            region = region * 3 + halves_in + shifted
        vhat, _ = normed(x_ref[w])
        a1 = vhat * gain_ref[0:1, :] + tb_ref[0:1, :]
        a1_ref[w] = a1.astype(LOW)
        a1t_ref[w] = a1.T.astype(LOW)
        differs = jnp.where(codes == region, 0.0, 1.0)
        rft_ref[w] = differs.astype(LOW)
        rf_ref[w] = ((1.0 - differs.T) * -1e30).astype(LOW)


def rest_kernel(proj_ref, up_ref, down_ref, out_ref):
    out_ref[...] = jnp.concatenate([proj_ref[...], up_ref[...], down_ref[...]], axis=1).astype(LOW)


def split3(values):
    high = values.astype(LOW)
    rest = values - high.astype(F32)
    mid = rest.astype(LOW)
    return high, mid, (rest - mid.astype(F32)).astype(LOW)


def rows_from_table_kernel(order_ref, table_ref, lane_ref, column_ref, out_ref, *picks):
    table = jnp.concatenate(split3(table_ref[...]), axis=0)
    rows = lax.broadcasted_iota(jnp.int32, (REL, 256), 0)
    for block in range(RELP // 256):
        cols = slice(block * 256, block * 256 + 256)
        picked = jnp.where(rows == order_ref[:, cols], 1.0, 0.0).astype(LOW)
        got = product(table, picked)
        out_ref[:, cols] = (got[:HEADS] + got[HEADS : 2 * HEADS] + got[2 * HEADS :]) * LOG2E
    for block in range(3):
        low, high = LANE_CUTS[block]
        cols = slice(block * 256, block * 256 + 256)
        down = lax.broadcasted_iota(jnp.int32, (high - low, 256), 0) + low
        picks[block][...] = jnp.where(down == lane_ref[:, cols], 1.0, 0.0).astype(LOW)
        across = lax.broadcasted_iota(jnp.int32, (256, high - low), 1) + low
        picks[3 + block][...] = jnp.where(across == column_ref[cols, :], 1.0, 0.0).astype(LOW)


def rows_to_table_kernel(order_ref, pack_ref, out_ref, gains_ref, biases_ref, pair_ref, hidden_ref):
    rows = jnp.concatenate(split3(pack_ref[:, 0:RELP]), axis=0)
    ids = lax.broadcasted_iota(jnp.int32, (256, RELP), 0)
    for start in range(0, REL, 256):
        count = min(256, REL - start)
        picked = jnp.where(ids + start == order_ref[...], 1.0, 0.0).astype(LOW)
        got = product(rows, picked, NT)
        got = got[:HEADS] + got[HEADS : 2 * HEADS] + got[2 * HEADS :]
        out_ref[:, start : start + count] = got[:, :count]
    cols = slice(RELP, PACK)
    for i, at in enumerate((0, 2)):
        gains_ref[i : i + 1, :] = pack_ref[at : at + 1, cols]
    for i, at in enumerate((1, 4, 3, 5)):
        biases_ref[i : i + 1, :] = pack_ref[at : at + 1, cols]
    pair_ref[...] = pack_ref[6:8, cols]
    hidden_ref[...] = pack_ref[8:12, cols]


def unpack_qkv_kernel(qkv_ref, out_ref, proj_ref):
    for i in range(3):
        out_ref[i] = qkv_ref[:, 128 * i : 128 * i + 128]
    proj_ref[...] = qkv_ref[:, 384:512]


def unpack_mlp_kernel(mlp_ref, up_ref, down_ref):
    up_ref[...] = mlp_ref[0]
    down_ref[...] = mlp_ref[1]


def lanes_of(ti):
    off = 49 * (7 - ti)
    base = off // 128 * 128
    return base, off - base


def expand_kernel(pair, part_ref, rows_ref, p0, p1, p2, bias_ref, left_s, wide_s):
    back = 7 - lax.broadcasted_iota(jnp.int32, (8, RELP), 0)
    for g in range(2):
        base_row = (part_ref[0] ^ (2 * pair + g)) * GHEADS
        for h in range(GHEADS):
            row = jnp.broadcast_to(rows_ref[pl.ds(base_row + h, 1), :], (8, RELP))
            for bit in range(3):
                row = jnp.where(((back >> bit) & 1) == 1, pltpu.roll(row, RELP - (1 << bit), 1), row)
            for hi in range(WH):
                rolled = pltpu.roll(row, (1 - (6 - hi) * 13) % RELP, 1)
                at = 56 * h + 8 * hi
                left_s[g, at : at + 8, :] = rolled
        for block, pick in enumerate((p0, p1, p2)):
            low, high = LANE_CUTS[block]
            got = product(left_s[g, :, low:high].astype(LOW), pick[...])
            for h in range(GHEADS):
                wide_s[g, h, :, block * 256 : block * 256 + 256] = got[56 * h : 56 * h + 56]
        for h in range(GHEADS):
            for ti in range(WT):
                base, by = lanes_of(ti)
                for hi in range(WH):
                    tile = wide_s[g, h, 8 * hi : 8 * hi + 8, base : base + 512]
                    if by:
                        tile = pltpu.roll(tile, 512 - by, 1)
                    at = 49 * ti + 7 * hi
                    bias_ref[GHEADS * g + h, at : at + 7, :] = tile[:7, :WIN]


def expand_bias(pair, part, rows, picks, after):
    return run(
        functools.partial(expand_kernel, pair),
        [(part, SCALAR), (rows, WHOLE)] + [(p, WHOLE) for p in picks],
        [(shaped(2 * GHEADS, WIN, WIN), WHOLE)],
        5, 16,
        scratch=[pltpu.VMEM((2, 56 * GHEADS, RELP), F32), pltpu.VMEM((2, GHEADS, 56, 768), F32)],
        after=after,
    )[0]


def shrunk(wide_refs, picks, spread_s, out_ref, at):
    heads = wide_refs.shape[0]
    used = (lax.broadcasted_iota(jnp.int32, (56, 256), 0) & 7) < 7
    spread_s[...] = jnp.zeros(spread_s.shape, F32)
    for block, pick in enumerate(picks):
        low, high = LANE_CUTS[block]
        parts = []
        for h in range(heads):
            wide = jnp.where(used, wide_refs[h, :, block * 256 : block * 256 + 256], 0.0)
            near = wide.astype(LOW).astype(F32)
            parts += [near, wide - near]
        got = product(jnp.concatenate(parts, axis=0).astype(LOW), pick[...])
        for h in range(heads):
            spread_s[h, :, low:high] += got[112 * h : 112 * h + 56] + got[112 * h + 56 : 112 * h + 112]
    left = 7 - lax.broadcasted_iota(jnp.int32, (8, RELP), 0)
    for h in range(heads):
        total = jnp.zeros((8, RELP), F32)
        for hi in range(WH):
            total += pltpu.roll(spread_s[h, 8 * hi : 8 * hi + 8, :], ((6 - hi) * 13 - 1) % RELP, 1)
        for bit in range(3):
            total = jnp.where(((left >> bit) & 1) == 1, pltpu.roll(total, 1 << bit, 1), total)
        out_ref[pl.ds(at + h, 1), 0:RELP] = jnp.sum(total, axis=0, keepdims=True)


def shrink_kernel(wide_ref, p0, p1, p2, out_ref, spread_s):
    shrunk(wide_ref, (p0, p1, p2), spread_s, out_ref, 0)


def shrink_bias(wide, picks, after):
    return run(
        shrink_kernel,
        [(wide, WHOLE)] + [(p, WHOLE) for p in picks],
        [(shaped(GHEADS, RELP), WHOLE)],
        1.4, 12,
        scratch=[pltpu.VMEM((GHEADS, 56, RELP), F32)],
        after=after,
    )[0]


P_SLOTS = 3


def attend_kernel(
    pair, part_ref, a1_ref, wa_ref, wb_ref, qvb_ref, bias_ref, rf_ref, rft_ref,
    p_ref, qt_ref, k_ref, vt_ref, o_ref, li_ref,
    q_s, ka_s, v_s, s_s, acc_s, p_s, p_sem, qt_s, k_s, vt_s, li_s, side_sem,
):
    lane = lax.broadcasted_iota(jnp.int32, (WIN, 128), 1) // HD
    zero = jnp.zeros((WIN, 128), LOW)

    def away(at):
        slot = at % P_SLOTS
        return pltpu.make_async_copy(p_s.at[slot], p_ref.at[at], p_sem.at[slot])

    def side(i, g):
        source, target = ((qt_s, qt_ref), (k_s, k_ref), (vt_s, vt_ref), (li_s, li_ref))[i]
        return pltpu.make_async_copy(source.at[g], target.at[g], side_sem.at[i, g])

    for g, w_ref in enumerate((wa_ref, wb_ref)):
        cols = pl.ds(pl.multiple_of((part_ref[0] ^ (2 * pair + g)) * 128, 128), 128)
        for w in range(2):
            qkv = product(a1_ref[w], w_ref[:, 0:384] if w_ref.shape[1] > 384 else w_ref[...])
            q = (qkv[:, :128] + qvb_ref[0:1, cols]) * (SCALE * LOG2E)
            k = qkv[:, 128:256]
            v = qkv[:, 256:384] + qvb_ref[1:2, cols]
            q_s[g, w] = q.astype(LOW)
            v_s[g, w] = v.astype(LOW)
            qt_s[g, w] = q.T.astype(LOW)
            k_s[g, w] = k.astype(LOW)
            vt_s[g, w] = v.T.astype(LOW)
            ka_s[g, w, 0:128, :] = k.T.astype(LOW)
            ka_s[g, w, 128:256, :] = rft_ref[w]
        for i in range(3):
            side(i, g).start()
        for e in range(GHEADS):
            at = GHEADS * g + e
            slot = at % P_SLOTS
            mine = lane == e
            if at >= P_SLOTS:
                away(at - P_SLOTS).wait()
            for w in range(2):
                q_wide = jnp.concatenate([jnp.where(mine, q_s[g, w], zero), rf_ref[w]], axis=1)
                s_s[at % 2, w] = product(q_wide, ka_s[g, w])
            for w in range(2):
                for start, count in ROW_CUTS:
                    rows = slice(start, start + count)
                    scores = s_s[at % 2, w, rows, :] + bias_ref[at, rows, :]
                    top = jnp.max(scores, axis=1, keepdims=True)
                    p_s[slot, w, rows, :] = jnp.exp2(scores - top).astype(LOW)
                v_wide = jnp.concatenate(
                    [jnp.where(mine, v_s[g, w], zero), jnp.where(mine, 1.0, 0.0).astype(LOW)], axis=1
                )
                part = product(p_s[slot, w], v_wide)
                acc_s[g, w] = part if e == 0 else acc_s[g, w] + part
            away(at).start()
        for w in range(2):
            inverse = 1.0 / acc_s[g, w, :, 128:256]
            li_s[g, w] = inverse
            o_ref[g, w] = (acc_s[g, w, :, 0:128] * inverse).astype(LOW)
        side(3, g).start()
    for at in range(2 * GHEADS - P_SLOTS, 2 * GHEADS):
        away(at).wait()
    for g in range(2):
        for i in range(4):
            side(i, g).wait()


def attend(pair, part, a1, weights, qvb, bias, rf, rft, after):
    return run(
        functools.partial(attend_kernel, pair),
        [(part, SCALAR)] + [(a, WHOLE) for a in (a1, *weights, qvb, bias, rf, rft)],
        [
            (pinned(pltpu.HBM, 2 * GHEADS, 2, WIN, WIN, kind=LOW), FAR),
            (pinned(pltpu.HBM, 2, 2, 128, WIN, kind=LOW), FAR),
            (pinned(pltpu.HBM, 2, 2, WIN, 128, kind=LOW), FAR),
            (pinned(pltpu.HBM, 2, 2, 128, WIN, kind=LOW), FAR),
            (shaped(2, 2, WIN, 128, kind=LOW), WHOLE),
            (pinned(pltpu.HBM, 2, 2, WIN, 128), FAR),
        ],
        2, 28,
        scratch=[
            pltpu.VMEM((2, 2, WIN, 128), LOW),
            pltpu.VMEM((2, 2, 256, WIN), LOW),
            pltpu.VMEM((2, 2, WIN, 128), LOW),
            pltpu.VMEM((2, 2, WIN, WIN), F32),
            pltpu.VMEM((2, 2, WIN, 256), F32),
            pltpu.VMEM((P_SLOTS, 2, WIN, WIN), LOW),
            pltpu.SemaphoreType.DMA((P_SLOTS,)),
            pltpu.VMEM((2, 2, 128, WIN), LOW),
            pltpu.VMEM((2, 2, WIN, 128), LOW),
            pltpu.VMEM((2, 2, 128, WIN), LOW),
            pltpu.VMEM((2, 2, WIN, 128), F32),
            pltpu.SemaphoreType.DMA((4, 2)),
        ],
        after=after,
    )


def attend_back_kernel(
    at, dop_ref, nd_ref, p_ref, qt_ref, k_ref, vt_ref, a1t_ref, gp_ref,
    dw_ref, wide_ref, low_ref, cs_ref,
    dop_s, nd_s, qt_s, k_s, vt_s, a1t_s, gp_s, p_s, dopt_s, dp_s, ds_s, dq_s, dkt_s, dvt_s, db_s, sems,
):
    lane = lax.broadcasted_iota(jnp.int32, (WIN, 128), 1) // HD
    zero = jnp.zeros((WIN, 128), LOW)
    inside = lax.broadcasted_iota(jnp.int32, (8, 512), 1) < WIN
    names = ("dop", "nd", "vt", "qt", "k", "gp", "a1t")
    sources = (dop_ref.at[at], nd_ref.at[at], vt_ref.at[at], qt_ref.at[at], k_ref.at[at], gp_ref.at[at], a1t_ref)
    targets = (dop_s, nd_s, vt_s, qt_s, k_s, gp_s, a1t_s)
    copies = {
        name: pltpu.make_async_copy(source, target, sems.at[i])
        for i, (name, source, target) in enumerate(zip(names, sources, targets))
    }
    probs = [
        pltpu.make_async_copy(p_ref.at[GHEADS * at + e], p_s.at[e], sems.at[len(names) + e]) for e in range(GHEADS)
    ]
    for name in ("dop", "nd", "vt"):
        copies[name].start()
    probs[0].start()
    copies["qt"].start()
    copies["k"].start()
    for e in range(1, GHEADS):
        probs[e].start()
    copies["a1t"].start()
    copies["gp"].start()
    for name in ("dop", "nd", "vt"):
        copies[name].wait()
    for w in range(2):
        dopt_s[w] = dop_s[w].astype(F32).T.astype(LOW)
    for e in range(GHEADS):
        mine = lane == e
        own = slice(HD * e, HD * e + HD)
        slot = e % 2
        for w in range(2):
            wide = jnp.concatenate([jnp.where(mine, dop_s[w], zero), jnp.where(mine, nd_s[w], zero)], axis=1)
            v_wide = jnp.concatenate([vt_s[w], jnp.ones((128, WIN), LOW)], axis=0)
            dp_s[slot, w] = product(wide, v_wide)
        probs[e].wait()
        for w in range(2):
            dvt_s[w, own, :] = product(dopt_s[w, own, :], p_s[e, w])
        for start, count in ROW_CUTS:
            rows = slice(start, start + count)
            one = p_s[e, 0, rows, :].astype(F32) * dp_s[slot, 0, rows, :]
            two = p_s[e, 1, rows, :].astype(F32) * dp_s[slot, 1, rows, :]
            db_s[slot, rows, 0:WIN] = one + two
            ds_s[slot, 0, rows, :] = one.astype(LOW)
            ds_s[slot, 1, rows, :] = two.astype(LOW)
        if e == 0:
            copies["qt"].wait()
            copies["k"].wait()
        for w in range(2):
            dkt_s[w, own, :] = product(qt_s[w, own, :], ds_s[slot, w])
            part = product(ds_s[slot, w], jnp.where(mine, k_s[w], zero))
            dq_s[w] = part if e == 0 else dq_s[w] + part
        for hi in range(WH):
            own_rows = slice(8 * hi, 8 * hi + 8)
            wide_ref[e, own_rows, :] = jnp.zeros((8, 768), F32)
            for base in (0, 128, 256):
                total = jnp.zeros((8, 512), F32)
                for ti in range(WT):
                    lane_base, by = lanes_of(ti)
                    if lane_base != base:
                        continue
                    first_row = 49 * ti + 7 * hi
                    tile = jnp.where(inside, db_s[slot, first_row : first_row + 8, :], 0.0)
                    total += pltpu.roll(tile, by, 1) if by else tile
                wide_ref[e, own_rows, base : base + 512] += total
    copies["a1t"].wait()
    copies["gp"].wait()
    sum_q = jnp.zeros((1, 128), F32)
    sum_v = jnp.zeros((1, 128), F32)
    grad = jnp.zeros((D, 384), F32)
    for w in range(2):
        dq = dq_s[w] * SCALE
        dk = (dkt_s[w] * (1.0 / LOG2E)).T
        dv = dvt_s[w].T
        sum_q += jnp.sum(dq, axis=0, keepdims=True)
        sum_v += jnp.sum(dv, axis=0, keepdims=True)
        low = jnp.concatenate([dq, dk, dv], axis=1).astype(LOW)
        low_ref[w] = low
        grad += product(a1t_s[w], low)
    dw_ref[:, 0:384] = grad.astype(LOW)
    dw_ref[:, 384:512] = gp_s[...]
    cs_ref[0:1, :] = sum_q
    cs_ref[1:2, :] = sum_v


def attend_back(at, dop, nd, kept, a1t, gproj, after):
    p, qt, k, vt, _, _ = kept
    return run(
        functools.partial(attend_back_kernel, at),
        [(pltpu.with_memory_space_constraint(a, pltpu.HBM), FAR) for a in (dop, nd, p, qt, k, vt, a1t, gproj)],
        [
            (shaped(D, 512, kind=LOW), WHOLE),
            (shaped(GHEADS, 56, 768), WHOLE),
            (shaped(2, WIN, 384, kind=LOW), WHOLE),
            (shaped(2, 128), WHOLE),
        ],
        6, 24,
        scratch=[
            pltpu.VMEM((2, WIN, 128), LOW),
            pltpu.VMEM((2, WIN, 128), LOW),
            pltpu.VMEM((2, 128, WIN), LOW),
            pltpu.VMEM((2, WIN, 128), LOW),
            pltpu.VMEM((2, 128, WIN), LOW),
            pltpu.VMEM((2, D, WIN), LOW),
            pltpu.VMEM((D, 128), LOW),
            pltpu.VMEM((GHEADS, 2, WIN, WIN), LOW),
            pltpu.VMEM((2, 128, WIN), LOW),
            pltpu.VMEM((2, 2, WIN, WIN), F32),
            pltpu.VMEM((2, 2, WIN, WIN), LOW),
            pltpu.VMEM((2, WIN, 128), F32),
            pltpu.VMEM((2, 128, WIN), F32),
            pltpu.VMEM((2, 128, WIN), F32),
            pltpu.VMEM((2, 400, 512), F32),
            pltpu.SemaphoreType.DMA((7 + GHEADS,)),
        ],
        after=after,
    )


def gelu_parts(v):
    size = jnp.abs(v)
    t = 1.0 / (1.0 + (0.3275911 * 0.7071067811865476) * size)
    bell = jnp.exp2(v * v * (-0.5 * LOG2E))
    poly = t * (0.127414796 + t * (-0.142248368 + t * (0.7107068705 + t * (-0.7265760135 + t * 0.5307027145))))
    tail = poly * bell
    phi = jnp.where(v >= 0.0, 1.0 - tail, tail)
    return v * phi, phi + v * bell * 0.3989422804014327


def norm_back(values, dy, gain):
    vhat, rstd = normed(values)
    scaled = dy * gain
    dv = rstd * (
        scaled - jnp.mean(scaled, -1, keepdims=True) - vhat * jnp.mean(scaled * vhat, -1, keepdims=True)
    )
    return dv, jnp.sum(dy * vhat, axis=0, keepdims=True), jnp.sum(dy, axis=0, keepdims=True)


ROWS = 2 * WIN


def before_kernel(
    on_ref, of_ref, x_ref, cot_ref, tb_ref, gain_ref, u0, u1, u2, u3,
    after_ref, a2_ref, a2t_ref, g_ref, gt_ref,
):
    weight = jnp.concatenate([u[:, 0:128] for u in (u0, u1, u2, u3)], axis=1)
    lows = []
    for w in range(2):
        mixed = jnp.concatenate([on_ref[0, w], on_ref[1, w], of_ref[0, w], of_ref[1, w]], axis=1)
        after = x_ref[w] + product(mixed, weight, NT) + tb_ref[1:2, :]
        after_ref[w] = after
        vhat, _ = normed(after)
        lows.append(vhat * gain_ref[1:2, :] + tb_ref[2:3, :])
    a2 = jnp.concatenate(lows, axis=0)
    a2_ref[...] = a2.astype(LOW)
    a2t_ref[...] = a2.T.astype(LOW)
    cot = jnp.concatenate([cot_ref[0], cot_ref[1]], axis=0)
    g_ref[...] = cot.astype(LOW)
    gt_ref[...] = cot.T.astype(LOW)


def before(o_near, o_far, x, cot, biases, gains, ups):
    return run(
        before_kernel,
        [(o_near, WHOLE), (o_far, WHOLE)]
        + [(pltpu.with_memory_space_constraint(a, pltpu.HBM), held(2, WIN, D)) for a in (x, cot)]
        + [(a, WHOLE) for a in (biases, gains, *ups)],
        [
            (shaped(2, WIN, D), WHOLE), (shaped(ROWS, D, kind=LOW), WHOLE), (shaped(D, ROWS, kind=LOW), WHOLE),
            (shaped(ROWS, D, kind=LOW), WHOLE), (shaped(D, ROWS, kind=LOW), WHOLE),
        ],
        4, 20,
        grid=(1,),
    )


def feed_parts(
    first, part_ref, a2_ref, a2t_ref, g_ref, gt_ref, hb_ref, ups, own_ref, other_ref,
    out_ref, da2_ref, gup_ref, gdown_ref, ghb_ref, down_s, h_s, d_s, act_s, dh_s,
):
    count, block = own_ref.shape[1:3]
    for p in range(2):
        for z in range(count):
            for ref, place in ((own_ref, part_ref[1]), (other_ref, 1 - part_ref[1])):
                at = pl.multiple_of((2 * z + place) * block, block)
                down_s[p, pl.ds(at, block), :] = ref[p, z]
    downs = (down_s.at[0], down_s.at[1])

    def rise(p, half):
        cols = slice(256 * half, 256 * half + 256)
        h_s[p, :, cols] = product(a2_ref[...], ups[p][:, 128 + 256 * half : 384 + 256 * half])
        d_s[p, :, cols] = product(g_ref[...], downs[p][:, cols])

    def bend(p, half):
        for cut in range(256 * half, 256 * half + 256, 128):
            cols = slice(cut, cut + 128)
            line = hb_ref[(first + 2 * p) ^ part_ref[0], :, cols]
            sums = jnp.zeros((1, 128), F32)
            for start in range(0, ROWS, 112):
                rows = slice(start, start + 112)
                act, slope = gelu_parts(h_s[p, rows, cols] + line)
                act_s[p, rows, cols] = act.astype(LOW)
                grad = d_s[p, rows, cols] * slope
                sums += jnp.sum(grad, axis=0, keepdims=True)
                dh_s[p, rows, cols] = grad.astype(LOW)
            ghb_ref[p, :, cols] = sums

    def fall(p):
        for half in range(2):
            cols = slice(256 * half, 256 * half + 256)
            gup_ref[p, :, cols] = product(a2t_ref[...], dh_s[p, :, cols]).astype(LOW)
            gdown_ref[p, :, cols] = product(gt_ref[...], act_s[p, :, cols]).astype(LOW)
        out_ref[...] += product(act_s[p], downs[p][...], NT)
        da2_ref[...] += product(dh_s[p], ups[p][:, 128:640], NT)

    rise(0, 0)
    rise(0, 1)
    bend(0, 0)
    rise(1, 0)
    bend(0, 1)
    rise(1, 1)
    bend(1, 0)
    fall(0)
    bend(1, 1)
    fall(1)


def feed_odd_kernel(
    part_ref, a2_ref, a2t_ref, g_ref, gt_ref, hb_ref, ua, ub, own_ref, other_ref, after_ref, tb_ref,
    out_ref, da2_ref, gup_ref, gdown_ref, ghb_ref, *work,
):
    for w in range(2):
        out_ref[WIN * w : WIN * w + WIN, :] = after_ref[w] + tb_ref[3:4, :]
    da2_ref[...] = jnp.zeros((ROWS, D), F32)
    feed_parts(
        1, part_ref, a2_ref, a2t_ref, g_ref, gt_ref, hb_ref, (ua, ub), own_ref, other_ref,
        out_ref, da2_ref, gup_ref, gdown_ref, ghb_ref, *work,
    )


def feed_even_kernel(
    part_ref, a2_ref, a2t_ref, g_ref, gt_ref, hb_ref, ua, ub, own_ref, other_ref, after_ref,
    out_in, da2_in, on_ref, of_ref, lin_ref, lif_ref, cot_ref, gain_ref, uc, ud,
    out_ref, gup_ref, gdown_ref, ghb_ref, dafter_ref, dn_ref, df_ref, nn_ref, nf_ref, gpn_ref, gpf_ref, sums_ref,
    da2_s, *work,
):
    out_ref[...] = out_in[...]
    da2_s[...] = da2_in[...]
    feed_parts(
        0, part_ref, a2_ref, a2t_ref, g_ref, gt_ref, hb_ref, (ua, ub), own_ref, other_ref,
        out_ref, da2_s, gup_ref, gdown_ref, ghb_ref, *work,
    )
    weight = jnp.concatenate([u[:, 0:128] for u in (ua, uc, ub, ud)], axis=1)
    grad = jnp.zeros((D, D), F32)
    sums = [jnp.zeros((1, D), F32) for _ in range(4)]
    for w in range(2):
        own = slice(WIN * w, WIN * w + WIN)
        dv, dgain, doff = norm_back(after_ref[w], da2_s[own, :], gain_ref[1:2, :])
        cot = cot_ref[w]
        dafter = cot + dv
        dafter_ref[w] = dafter
        turned = dafter.T.astype(LOW)
        dmix = product(dafter.astype(LOW), weight)
        for i in range(PARTS):
            at = i % 2
            d_ref, n_ref, l_ref, m_ref = (
                (dn_ref, nn_ref, lin_ref, on_ref) if i < 2 else (df_ref, nf_ref, lif_ref, of_ref)
            )
            dop = (dmix[:, 128 * i : 128 * i + 128] * l_ref[at, w]).astype(LOW)
            d_ref[at, w] = dop
            n_ref[at, w] = (-(dop.astype(F32) * m_ref[at, w].astype(F32))).astype(LOW)
        grad += product(turned, jnp.concatenate([on_ref[0, w], on_ref[1, w], of_ref[0, w], of_ref[1, w]], axis=1))
        parts = (dgain, doff, jnp.sum(dafter, axis=0, keepdims=True), jnp.sum(cot, axis=0, keepdims=True))
        for i, part in enumerate(parts):
            sums[i] += part
    for i, (ref, at) in enumerate(((gpn_ref, 0), (gpn_ref, 1), (gpf_ref, 0), (gpf_ref, 1))):
        ref[at] = grad[:, 128 * i : 128 * i + 128].astype(LOW)
    for i in range(4):
        sums_ref[i : i + 1, :] = sums[i]


FEED_WORK = [
    pltpu.VMEM((2, 512, 512), LOW),
    pltpu.VMEM((2, ROWS, 512), F32), pltpu.VMEM((2, ROWS, 512), F32),
    pltpu.VMEM((2, ROWS, 512), LOW), pltpu.VMEM((2, ROWS, 512), LOW),
]
STEP_OUTS = [(shaped(2, D, 512, kind=LOW), WHOLE), (shaped(2, D, 512, kind=LOW), WHOLE), (shaped(2, 1, 512), WHOLE)]


def feed_odd(part, known, hb, ups, downs, after, biases):
    return run(
        feed_odd_kernel,
        [(part, SCALAR)] + [(a, WHOLE) for a in (*known, hb, *ups, *downs, after, biases)],
        [(shaped(ROWS, D), WHOLE), (shaped(ROWS, D), WHOLE), *STEP_OUTS],
        9, 28,
        scratch=FEED_WORK,
    )


def feed_even(part, known, hb, ups, downs, after, out, da2, o_near, o_far, li_near, li_far, cot, gains, others):
    return run(
        feed_even_kernel,
        [(part, SCALAR)]
        + [
            (a, WHOLE)
            for a in (
                *known, hb, *ups, *downs, after, out, da2, o_near, o_far, li_near, li_far, cot, gains, *others,
            )
        ],
        [
            (shaped(ROWS, D), WHOLE), *STEP_OUTS, (shaped(2, WIN, D), WHOLE),
            *[(pinned(pltpu.HBM, 2, 2, WIN, 128, kind=LOW), WHOLE)] * 4,
            *[(pinned(pltpu.HBM, 2, D, 128, kind=LOW), WHOLE)] * 2,
            (shaped(4, D), WHOLE),
        ],
        13, 32,
        scratch=[pltpu.VMEM((ROWS, D), F32), *FEED_WORK],
    )


def last_kernel(
    part_ref, x_ref, dafter_ref, gain_ref, l0, l1, l2, l3, w0, w1, w2, w3,
    c0, c1, c2, c3, two_ref, odd_ref, even_ref, wide_ref, p0, p1, p2, e1, e2, e3,
    gx_ref, pack_ref, spread_s, pack_s,
):
    sums = [jnp.zeros((1, D), F32) for _ in range(2)]
    for w in range(2):
        da1 = jnp.zeros((WIN, D), F32)
        for low, wt in ((l0, w0), (l1, w1), (l2, w2), (l3, w3)):
            da1 += product(low[w], wt[...], NT)
        dv, dgain, doff = norm_back(x_ref[w], da1, gain_ref[0:1, :])
        gx_ref[w] = dafter_ref[w] + dv
        sums[0] += dgain
        sums[1] += doff
    cols = slice(RELP, PACK)
    pack_s[0:1, cols] = sums[0]
    pack_s[1:2, cols] = sums[1]
    pack_s[2:6, cols] = two_ref[...]
    for group, c in enumerate((c0, c1, c2, c3)):
        own = pl.ds(pl.multiple_of(RELP + (part_ref[0] ^ group) * 128, 128), 128)
        pack_s[6:8, own] = c[...]
    for i in range(PARTS):
        pack_s[pl.ds(8 + (part_ref[0] ^ i), 1), cols] = (odd_ref if i % 2 else even_ref)[i // 2]
    pack_s[12:16, cols] = jnp.zeros((4, D), F32)
    for group, rows in enumerate((e1, e2, e3)):
        for h in range(GHEADS):
            pack_s[pl.ds((part_ref[0] ^ (group + 1)) * GHEADS + h, 1), 0:RELP] = rows[h : h + 1, :]
    shrunk(wide_ref, (p0, p1, p2), spread_s, pack_s, part_ref[0] * GHEADS)
    pack_ref[...] = pack_s[...].astype(LOW)


def swap(values, axis, distance):
    count = lax.axis_size(axis)
    return lax.ppermute(values, axis, [(i, i ^ distance) for i in range(count)])


def bits_of(axis):
    return (lax.axis_size(axis) - 1).bit_length()


def interleaved(own, other, upper):
    place = jnp.arange(2, dtype=jnp.int32).reshape(1, 2, *(1,) * (own.ndim - 1))
    mine = place == upper.astype(jnp.int32)
    return jnp.where(mine, own[:, None], other[:, None]).reshape(-1, *own.shape[1:])


def upper_of(axis, bit):
    return (lax.axis_index(axis) >> bit) % 2 == 1


def gathered(blocks, bits):
    for bit in bits:
        blocks = interleaved(blocks, swap(blocks, "dp", 1 << bit), upper_of("dp", bit))
    return blocks


def flat(blocks):
    return blocks.reshape(-1, blocks.shape[-1])


def half(total, bit, mine):
    pairs = total.reshape(-1, 2, *total.shape[1:])
    return jnp.where(upper_of("dp", bit) == mine, pairs[:, 1], pairs[:, 0])


def halves(total, bit):
    return half(total, bit, False).astype(LOW), half(total, bit, True).astype(F32)


def plus(one, two):
    return one.astype(F32) + two.astype(F32)


def offset_order(rel_index):
    corners = rel_index.reshape(WT, WH, WW, WIN)[::7, ::6, ::6].reshape(2, 2, 2, WT, WH, WW)
    joined = jnp.concatenate([corners[1], corners[0][:, :, 1:]], axis=2)
    joined = jnp.concatenate([joined[1], joined[0][:, :, 1:]], axis=2)
    joined = jnp.concatenate([joined[1], joined[0][:, :, 1:]], axis=2)
    return jnp.pad(joined.reshape(1, REL), ((0, 0), (0, RELP - REL)), constant_values=-1)


def body(
    inputs,
    w_qkv,
    qv_bias,
    w_proj,
    w_fc1,
    fc1_bias,
    w_fc2,
    norm_gains,
    token_biases,
    table,
    shifts,
    rel_index,
    cotangent,
):
    index = lax.axis_index("mp")
    part = index.astype(jnp.int32).reshape(1)
    rows = w_qkv.shape[1]
    x = inputs.reshape(2, WIN, D)
    cot = cotangent.reshape(2, WIN, D)
    high_bits = tuple(reversed(range(1, bits_of("dp"))))
    low_bits = tuple(range(1, bits_of("dp")))

    shard_qkv = w_qkv.transpose(1, 0, 2).reshape(1, rows, 384).astype(LOW)
    (shard_rest,) = run(
        rest_kernel,
        [(a, WHOLE) for a in (w_proj.T, w_fc1, w_fc2.T)],
        [(shaped(rows, 1152, kind=LOW), WHOLE)],
        1, 8,
    )
    shard_rest = shard_rest[None]
    qkv_first = gathered(shard_qkv, high_bits[:1])
    qkv_high = gathered(qkv_first, high_bits[1:])
    own = flat(gathered(qkv_high, (0,)))
    qkv_parts = [own, swap(own, "mp", 1)]
    across = swap(own, "mp", 2)
    rest = gathered(shard_rest, high_bits)
    (up_own,) = lax.optimization_barrier((gathered(rest[:, :, :640], (0,)),))
    up_across = swap(up_own, "mp", 2)
    down_across = swap(rest[:, :, 640:], "mp", 2)
    places = jnp.arange(WIN, dtype=jnp.int32)
    places = jnp.stack([places // (WH * WW), places // WW % WH, places % WW])
    order = offset_order(once(rel_index, qkv_first))
    column = jnp.arange(768, dtype=jnp.int32)
    lane_row = jnp.where(
        column < 15 * 49, column // 49 * 169 + column % 49 // 7 * 13 + column % 7, -1
    )
    a1, a1t, rf, rft = run(
        first_norm_kernel,
        [(part, SCALAR), (shifts, SCALAR)] + [(a, WHOLE) for a in (x, norm_gains, token_biases, places)],
        [
            (shaped(2, WIN, D, kind=LOW), WHOLE), (pinned(pltpu.HBM, 2, D, WIN, kind=LOW), WHOLE),
            (shaped(2, WIN, 128, kind=LOW), WHOLE), (shaped(2, 128, WIN, kind=LOW), WHOLE),
        ],
        2, 16,
        after=(qkv_first,),
    )
    row_offsets, *picks = run(
        rows_from_table_kernel,
        [(a, WHOLE) for a in (order, table.T, lane_row.reshape(1, 768), lane_row.reshape(768, 1))],
        [(shaped(HEADS, RELP), WHOLE)]
        + [(shaped(high - low, 256, kind=LOW), WHOLE) for low, high in LANE_CUTS]
        + [(shaped(256, high - low, kind=LOW), WHOLE) for low, high in LANE_CUTS],
        4, 20,
        after=(qkv_high,),
    )
    out_picks, back_picks = picks[:3], picks[3:]
    near_bias = expand_bias(0, part, row_offsets, out_picks, (qkv_high,))
    near = attend(0, part, a1, qkv_parts[:2], qv_bias, near_bias, rf, rft, (rest,))
    across = once(across, near[4])
    qkv_parts += [across, swap(across, "mp", 1)]
    far_bias = expand_bias(1, part, row_offsets, out_picks, (near[4], up_own))
    down_pair = jnp.stack([rest[:, :, 640:], once(down_across, far_bias)], axis=0)
    down_other = swap(down_pair, "dp", 1)
    far = attend(1, part, a1, qkv_parts[2:], qv_bias, far_bias, rf, rft, (up_own, down_pair))
    up_parts = [flat(up_own), flat(swap(up_own, "mp", 1)), flat(up_across), flat(swap(once(up_across, far[4]), "mp", 1))]
    hb = fc1_bias.reshape(PARTS, 1, 512)
    after, *known = before(near[4], far[4], x, cot, token_biases, norm_gains, up_parts)
    down_other = once(down_other, far[4])
    upper = upper_of("dp", 0).astype(jnp.int32).reshape(1)
    if rows % 16:
        joined = jnp.stack([flat(interleaved(down_pair[i], down_other[i], upper_of("dp", 0))) for i in range(2)])
        joined = joined.reshape(2, 2, 1, D // 2, 512)
        down_pair, down_other, upper = joined[:, 0], joined[:, 1], jnp.zeros((1,), jnp.int32)
    places_of = jnp.concatenate([part, upper])
    down_even = (down_pair, down_other)
    down_odd = [swap(a, "mp", 1) for a in down_even]
    out, da2, odd_up, odd_down, hb_odd = feed_odd(
        places_of, known, hb, up_parts[1::2], down_odd, after, token_biases
    )
    out, even_up, even_down, hb_even, dafter, dop_near, dop_far, nd_near, nd_far, gp_near, gp_far, sums_two = feed_even(
        places_of, known, hb, up_parts[::2], down_even, after, out, da2,
        near[4], far[4], near[5], far[5], cot, norm_gains, up_parts[1::2],
    )
    got_up = swap(odd_up, "mp", 1).reshape(2, -1, rows, 512)
    got_down = swap(odd_down, "mp", 1).reshape(2, -1, rows, 512)
    even_up = even_up.reshape(2, -1, rows, 512)
    even_down = even_down.reshape(2, -1, rows, 512)
    up_send = plus(even_up[1], got_up[1]).astype(LOW)
    turned = [a.transpose(1, 0, 2, 3) for a in (even_down, got_down)]
    down_send = plus(*(half(a, 0, False) for a in turned)).astype(LOW)
    three, wide3, low3, col3 = attend_back(1, dop_far, nd_far, far, a1t, gp_far, (up_send, down_send))
    two, wide2, low2, col2 = attend_back(0, dop_far, nd_far, far, a1t, gp_far, (three,))
    up_sum = plus(plus(even_up[0], got_up[0]), swap(up_send, "mp", 2))
    down_sum = plus(plus(*(half(a, 0, True) for a in turned)), swap(down_send, "dp", 1))
    far_sum = plus(two, swap(three, "mp", 1)).astype(LOW)
    up_send, up_keep = halves(up_sum, 0)
    down_send, down_keep = down_sum[:, 1].astype(LOW), down_sum[:, 0]
    one, wide1, low1, col1 = attend_back(
        1, dop_near, nd_near, near, a1t, gp_near, (far_sum, up_send, down_send)
    )
    far_sum = swap(far_sum, "mp", 2)
    up_sum = plus(up_keep, swap(up_send, "dp", 1))
    down_sum = plus(down_keep, swap(down_send, "mp", 2))
    summed = jnp.stack([up_sum, down_sum], axis=1)
    top = bits_of("dp") - 1
    is_top = upper_of("dp", top)
    ends = summed.reshape(2, -1, 2, rows, 512)
    mlp_send = jnp.where(is_top, ends[0], ends[1]).astype(LOW)
    mlp_keep = jnp.where(is_top, ends[1], ends[0])
    zero, wide0, low0, col0 = attend_back(0, dop_near, nd_near, near, a1t, gp_near, (mlp_send, one))
    summed = plus(mlp_keep, swap(mlp_send, "dp", 1 << top))
    total = plus(plus(zero, swap(one, "mp", 1)), far_sum).reshape(-1, rows, 512)
    rows_by = [shrink_bias(w, back_picks, ()) for w in (wide1, wide2, wide3)]
    send, keep = halves(total, 0)
    grad_x, pack = run(
        last_kernel,
        [(part, SCALAR)]
        + [
            (a, WHOLE)
            for a in (
                x, dafter, norm_gains, low0, low1, low2, low3, *qkv_parts, col0, col1, col2, col3,
                sums_two, hb_odd, hb_even, wide0, *back_picks, *rows_by,
            )
        ],
        [(shaped(2, WIN, D), WHOLE), (shaped(HEADS, PACK, kind=LOW), WHOLE)],
        4, 20,
        scratch=[pltpu.VMEM((GHEADS, 56, RELP), F32), pltpu.VMEM((HEADS, PACK), F32)],
        after=(send,),
    )
    total = plus(keep, swap(send, "dp", 1))
    mp_steps = [("mp", 1 << bit) for bit in range(bits_of("mp"))]
    steps = mp_steps + [("dp", 1 << bit) for bit in range(bits_of("dp"))]
    queue = list(low_bits)
    pending = None

    def settled(bit, keep, got):
        if bit == top:
            return plus(keep[0], got), keep[1]
        count = keep[0].shape[0]
        mlp_got = got[count:].reshape(keep[1].shape)
        return plus(keep[0], got[:count]), plus(keep[1], mlp_got)

    def parted(bit, total, summed):
        send, keep = halves(total, bit)
        if bit == top:
            return send, (keep, summed)
        mlp_send, mlp_keep = halves(summed, bit)
        return jnp.concatenate([send, mlp_send.reshape(-1, rows, 512)], axis=0), (keep, mlp_keep)

    for place, (axis, distance) in enumerate(steps):
        mine = pack.astype(LOW)
        theirs = swap(mine, axis, distance)
        if pending is not None:
            bit, keep, got = pending
            total, summed = settled(bit, keep, once(got, mine))
            pending = None
        if place >= 1 and queue:
            bit = queue.pop(0)
            send, keep = parted(bit, once(total, mine), summed)
            theirs = once(theirs, send)
            pending = (bit, keep, swap(send, "dp", 1 << bit))
        pack = plus(mine, theirs)
    if pending is not None:
        total, summed = settled(*pending)
    for bit in queue:
        send, keep = parted(bit, total, summed)
        total, summed = settled(bit, keep, swap(send, "dp", 1 << bit))
    own_qkv, own_mlp = total.reshape(rows, 512), summed.reshape(2, rows, 512)
    grad_qkv, grad_proj = run(
        unpack_qkv_kernel,
        [(own_qkv, WHOLE)],
        [(pinned(pltpu.HBM, *dims), held(*dims)) for dims in ((3, rows, 128), (rows, 128))],
        1, 8,
        grid=(1,),
    )
    grad_up, grad_down = run(
        unpack_mlp_kernel,
        [(own_mlp, WHOLE)],
        [(pinned(pltpu.HBM, rows, 512), held(rows, 512))] * 2,
        1, 8,
        grid=(1,),
    )
    grad_table, grad_gains, grad_biases, grad_pair, grad_hidden = run(
        rows_to_table_kernel,
        [(once(order, grad_qkv, grad_proj, grad_up, grad_down), WHOLE), (pack, WHOLE)],
        [(shaped(*dims), WHOLE) for dims in ((HEADS, REL), (2, D), (4, D), (2, D), (4, D))],
        4, 20,
    )
    return (
        out.reshape(inputs.shape),
        grad_x.reshape(inputs.shape),
        grad_qkv,
        grad_pair,
        grad_proj.T,
        grad_up,
        grad_hidden.reshape(FF),
        grad_down.T,
        grad_gains,
        grad_biases,
        grad_table.T,
    )


def solution(mesh):
    placed = (
        P(("dp", "mp"), None),
        P(None, "dp", "mp"),
        P(),
        P("mp", "dp"),
        P("dp", "mp"),
        P(),
        P("mp", "dp"),
        P(),
        P(),
        P(),
        P("dp", None),
        P(),
        P(("dp", "mp"), None),
    )
    return jax.shard_map(
        body,
        mesh=mesh,
        in_specs=placed,
        out_specs=(
            P(("dp", "mp"), None),
            P(("dp", "mp"), None),
            P(None, "dp", "mp"),
            P(),
            P("mp", "dp"),
            P("dp", "mp"),
            P(),
            P("mp", "dp"),
            P(),
            P(),
            P(),
        ),
        check_vma=False,
    )
```

```python
import functools

import jax
import jax.numpy as jnp
from jax import lax
from jax.experimental import pallas as pl
from jax.experimental.pallas import tpu as pltpu
from jax.sharding import PartitionSpec as P

D = 512
HEADS = 16
HD = 32
FF = 2048
WT = 8
WH = 7
WW = 7
GT = 16
GH = 14
GW = 14
WIN = 392
REL = 2535
RELP = 2560
PACK = RELP + D
WINS = 8
PARTS = 4
GHEADS = HEADS // PARTS
LOG2E = 1.4426950408889634
SCALE = HD ** (-0.5)
LOW = jnp.bfloat16
F32 = jnp.float32
NN = (((1,), (0,)), ((), ()))
NT = (((1,), (1,)), ((), ()))
ROW_CUTS = ((0, 64), (64, 64), (128, 64), (192, 64), (256, 64), (320, 72))
LANE_CUTS = ((0, 1024), (768, 1920), (1664, 2560))


def product(left, right, dims=NN):
    return lax.dot_general(left, right, dims, preferred_element_type=F32)


def shaped(*dims, kind=F32):
    return jax.ShapeDtypeStruct(dims, kind)


def cost(micros):
    return pl.CostEstimate(flops=int(micros * 1e9), bytes_accessed=int(micros * 3.6e6), transcendentals=0)


WHOLE = pl.BlockSpec(memory_space=pltpu.VMEM)
ANYWHERE = pl.BlockSpec(memory_space=pl.ANY)
SCALAR = pl.BlockSpec(memory_space=pltpu.SMEM)
FAR = pl.BlockSpec(memory_space=pltpu.HBM)


def run(kernel, ins, outs, micros, mib, grid=(), scratch=(), after=()):
    count = len(ins)

    def inner(*refs):
        kernel(*refs[:count], *refs[count + len(after) :])

    return pl.pallas_call(
        inner,
        grid=grid,
        out_shape=[o[0] for o in outs],
        in_specs=[i[1] for i in ins] + [ANYWHERE] * len(after),
        out_specs=[o[1] for o in outs],
        scratch_shapes=list(scratch),
        cost_estimate=cost(micros),
        compiler_params=pltpu.CompilerParams(vmem_limit_bytes=mib << 20),
    )(*[i[0] for i in ins], *after)


def pinned(space, *dims, kind=F32):
    return space(dims, kind)


def once(value, *others):
    return lax.optimization_barrier((value, *others))[0]


def held(*dims):
    return pl.BlockSpec(dims, lambda e: (0,) * len(dims))


def normed(values):
    centred = values - jnp.mean(values, -1, keepdims=True)
    rstd = lax.rsqrt(jnp.mean(centred * centred, -1, keepdims=True) + 1e-05)
    return centred * rstd, rstd


def first_norm_kernel(part_ref, shift_ref, x_ref, gain_ref, tb_ref, place_ref, a1_ref, a1t_ref, rf_ref, rft_ref):
    codes = lax.broadcasted_iota(jnp.int32, (128, WIN), 0)
    for w in range(2):
        window = (2 * part_ref[0] + w) % WINS
        region = jnp.zeros((1, WIN), jnp.int32)
        for axis, (length, size, along) in enumerate(
            ((WT, GT, window // 4), (WH, GH, window // 2 % 2), (WW, GW, window % 2))
        ):
            cell = place_ref[axis : axis + 1, :] + along * length
            halves_in = (cell >= size - length).astype(jnp.int32)
            shifted = (cell >= size - shift_ref[0, axis]).astype(jnp.int32)
            region = region * 3 + halves_in + shifted
        vhat, _ = normed(x_ref[w])
        a1 = vhat * gain_ref[0:1, :] + tb_ref[0:1, :]
        a1_ref[w] = a1.astype(LOW)
        a1t_ref[w] = a1.T.astype(LOW)
        differs = jnp.where(codes == region, 0.0, 1.0)
        rft_ref[w] = differs.astype(LOW)
        rf_ref[w] = ((1.0 - differs.T) * -1e30).astype(LOW)


def rest_kernel(proj_ref, up_ref, down_ref, out_ref):
    out_ref[...] = jnp.concatenate([proj_ref[...], up_ref[...], down_ref[...]], axis=1).astype(LOW)


BLOCKS = RELP // 128


def ones_of(order):
    place = lax.broadcasted_iota(jnp.int32, (128, RELP), 0)
    return jnp.where(place == (order & 127), 1.0, 0.0).astype(LOW), order >> 7


def split3(values):
    high = values.astype(LOW)
    rest = values - high.astype(F32)
    mid = rest.astype(LOW)
    return high, mid, (rest - mid.astype(F32)).astype(LOW)


def rows_from_table_kernel(order_ref, table_ref, lane_ref, column_ref, out_ref, *picks):
    table = jnp.concatenate(split3(table_ref[...]), axis=0)
    rows = lax.broadcasted_iota(jnp.int32, (REL, 256), 0)
    for block in range(RELP // 256):
        cols = slice(block * 256, block * 256 + 256)
        picked = jnp.where(rows == order_ref[:, cols], 1.0, 0.0).astype(LOW)
        got = product(table, picked)
        out_ref[:, cols] = (got[:HEADS] + got[HEADS : 2 * HEADS] + got[2 * HEADS :]) * LOG2E
    for block in range(3):
        low, high = LANE_CUTS[block]
        cols = slice(block * 256, block * 256 + 256)
        down = lax.broadcasted_iota(jnp.int32, (high - low, 256), 0) + low
        picks[block][...] = jnp.where(down == lane_ref[:, cols], 1.0, 0.0).astype(LOW)
        across = lax.broadcasted_iota(jnp.int32, (256, high - low), 1) + low
        picks[3 + block][...] = jnp.where(across == column_ref[cols, :], 1.0, 0.0).astype(LOW)


def rows_to_table_kernel(order_ref, pack_ref, out_ref, gains_ref, biases_ref, pair_ref, hidden_ref):
    ones, block_of = ones_of(order_ref[...])
    values = pack_ref[:, 0:RELP]
    high = values.astype(LOW).astype(F32)
    both = jnp.concatenate([high, values - high], axis=0)
    mine = [jnp.where(block_of == i, both, 0.0).astype(LOW) for i in range(BLOCKS)]
    got = product(jnp.concatenate(mine, axis=0), ones, NT)
    for i in range(BLOCKS):
        count = min(128, REL - 128 * i)
        at = 2 * HEADS * i
        total = got[at : at + HEADS] + got[at + HEADS : at + 2 * HEADS]
        out_ref[:, 128 * i : 128 * i + count] = total[:, :count]
    cols = slice(RELP, PACK)
    for i, at in enumerate((0, 2)):
        gains_ref[i : i + 1, :] = pack_ref[at : at + 1, cols]
    for i, at in enumerate((1, 4, 3, 5)):
        biases_ref[i : i + 1, :] = pack_ref[at : at + 1, cols]
    pair_ref[...] = pack_ref[6:8, cols]
    hidden_ref[...] = pack_ref[8:12, cols]


def unpack_qkv_kernel(qkv_ref, out_ref, proj_ref):
    for i in range(3):
        out_ref[i] = qkv_ref[:, 128 * i : 128 * i + 128]
    proj_ref[...] = qkv_ref[:, 384:512]


def unpack_mlp_kernel(mlp_ref, up_ref, down_ref):
    up_ref[...] = mlp_ref[0]
    down_ref[...] = mlp_ref[1]


def lanes_of(ti):
    off = 49 * (7 - ti)
    base = off // 128 * 128
    return base, off - base


def expand_kernel(pair, part_ref, rows_ref, p0, p1, p2, bias_ref, left_s, wide_s):
    back = 7 - lax.broadcasted_iota(jnp.int32, (8, RELP), 0)
    for g in range(2):
        base_row = (part_ref[0] ^ (2 * pair + g)) * GHEADS
        for h in range(GHEADS):
            row = jnp.broadcast_to(rows_ref[pl.ds(base_row + h, 1), :], (8, RELP))
            for bit in range(3):
                row = jnp.where(((back >> bit) & 1) == 1, pltpu.roll(row, RELP - (1 << bit), 1), row)
            for hi in range(WH):
                rolled = pltpu.roll(row, (1 - (6 - hi) * 13) % RELP, 1)
                at = 56 * h + 8 * hi
                left_s[g, at : at + 8, :] = rolled
        for block, pick in enumerate((p0, p1, p2)):
            low, high = LANE_CUTS[block]
            got = product(left_s[g, :, low:high].astype(LOW), pick[...])
            for h in range(GHEADS):
                wide_s[g, h, :, block * 256 : block * 256 + 256] = got[56 * h : 56 * h + 56]
        for h in range(GHEADS):
            for ti in range(WT):
                base, by = lanes_of(ti)
                for hi in range(WH):
                    tile = wide_s[g, h, 8 * hi : 8 * hi + 8, base : base + 512]
                    if by:
                        tile = pltpu.roll(tile, 512 - by, 1)
                    at = 49 * ti + 7 * hi
                    bias_ref[GHEADS * g + h, at : at + 7, :] = tile[:7, :WIN]


def expand_bias(pair, part, rows, picks, after):
    return run(
        functools.partial(expand_kernel, pair),
        [(part, SCALAR), (rows, WHOLE)] + [(p, WHOLE) for p in picks],
        [(shaped(2 * GHEADS, WIN, WIN), WHOLE)],
        5, 16,
        scratch=[pltpu.VMEM((2, 56 * GHEADS, RELP), F32), pltpu.VMEM((2, GHEADS, 56, 768), F32)],
        after=after,
    )[0]


def shrunk(wide_refs, picks, spread_s, out_ref, at):
    heads = wide_refs.shape[0]
    used = (lax.broadcasted_iota(jnp.int32, (56, 256), 0) & 7) < 7
    spread_s[...] = jnp.zeros(spread_s.shape, F32)
    for block, pick in enumerate(picks):
        low, high = LANE_CUTS[block]
        parts = []
        for h in range(heads):
            wide = jnp.where(used, wide_refs[h, :, block * 256 : block * 256 + 256], 0.0)
            near = wide.astype(LOW).astype(F32)
            parts += [near, wide - near]
        got = product(jnp.concatenate(parts, axis=0).astype(LOW), pick[...])
        for h in range(heads):
            spread_s[h, :, low:high] += got[112 * h : 112 * h + 56] + got[112 * h + 56 : 112 * h + 112]
    left = 7 - lax.broadcasted_iota(jnp.int32, (8, RELP), 0)
    for h in range(heads):
        total = jnp.zeros((8, RELP), F32)
        for hi in range(WH):
            total += pltpu.roll(spread_s[h, 8 * hi : 8 * hi + 8, :], ((6 - hi) * 13 - 1) % RELP, 1)
        for bit in range(3):
            total = jnp.where(((left >> bit) & 1) == 1, pltpu.roll(total, 1 << bit, 1), total)
        out_ref[pl.ds(at + h, 1), 0:RELP] = jnp.sum(total, axis=0, keepdims=True)


def shrink_kernel(wide_ref, p0, p1, p2, out_ref, spread_s):
    shrunk(wide_ref, (p0, p1, p2), spread_s, out_ref, 0)


def shrink_bias(wide, picks, after):
    return run(
        shrink_kernel,
        [(wide, WHOLE)] + [(p, WHOLE) for p in picks],
        [(shaped(GHEADS, RELP), WHOLE)],
        1.4, 12,
        scratch=[pltpu.VMEM((GHEADS, 56, RELP), F32)],
        after=after,
    )[0]


P_SLOTS = 3


def attend_kernel(
    pair, part_ref, a1_ref, wa_ref, wb_ref, qvb_ref, bias_ref, rf_ref, rft_ref,
    p_ref, qt_ref, k_ref, vt_ref, o_ref, li_ref,
    q_s, ka_s, v_s, s_s, acc_s, p_s, p_sem, qt_s, k_s, vt_s, li_s, side_sem,
):
    lane = lax.broadcasted_iota(jnp.int32, (WIN, 128), 1) // HD
    zero = jnp.zeros((WIN, 128), LOW)

    def away(at):
        slot = at % P_SLOTS
        return pltpu.make_async_copy(p_s.at[slot], p_ref.at[at], p_sem.at[slot])

    def side(i, g):
        source, target = ((qt_s, qt_ref), (k_s, k_ref), (vt_s, vt_ref), (li_s, li_ref))[i]
        return pltpu.make_async_copy(source.at[g], target.at[g], side_sem.at[i, g])

    for g, w_ref in enumerate((wa_ref, wb_ref)):
        cols = pl.ds(pl.multiple_of((part_ref[0] ^ (2 * pair + g)) * 128, 128), 128)
        for w in range(2):
            qkv = product(a1_ref[w], w_ref[:, 0:384] if w_ref.shape[1] > 384 else w_ref[...])
            q = (qkv[:, :128] + qvb_ref[0:1, cols]) * (SCALE * LOG2E)
            k = qkv[:, 128:256]
            v = qkv[:, 256:384] + qvb_ref[1:2, cols]
            q_s[g, w] = q.astype(LOW)
            v_s[g, w] = v.astype(LOW)
            qt_s[g, w] = q.T.astype(LOW)
            k_s[g, w] = k.astype(LOW)
            vt_s[g, w] = v.T.astype(LOW)
            ka_s[g, w, 0:128, :] = k.T.astype(LOW)
            ka_s[g, w, 128:256, :] = rft_ref[w]
        for i in range(3):
            side(i, g).start()
        for e in range(GHEADS):
            at = GHEADS * g + e
            slot = at % P_SLOTS
            mine = lane == e
            if at >= P_SLOTS:
                away(at - P_SLOTS).wait()
            for w in range(2):
                q_wide = jnp.concatenate([jnp.where(mine, q_s[g, w], zero), rf_ref[w]], axis=1)
                s_s[at % 2, w] = product(q_wide, ka_s[g, w])
            for w in range(2):
                for start, count in ROW_CUTS:
                    rows = slice(start, start + count)
                    scores = s_s[at % 2, w, rows, :] + bias_ref[at, rows, :]
                    top = jnp.max(scores, axis=1, keepdims=True)
                    p_s[slot, w, rows, :] = jnp.exp2(scores - top).astype(LOW)
                v_wide = jnp.concatenate(
                    [jnp.where(mine, v_s[g, w], zero), jnp.where(mine, 1.0, 0.0).astype(LOW)], axis=1
                )
                part = product(p_s[slot, w], v_wide)
                acc_s[g, w] = part if e == 0 else acc_s[g, w] + part
            away(at).start()
        for w in range(2):
            inverse = 1.0 / acc_s[g, w, :, 128:256]
            li_s[g, w] = inverse
            o_ref[g, w] = (acc_s[g, w, :, 0:128] * inverse).astype(LOW)
        side(3, g).start()
    for at in range(2 * GHEADS - P_SLOTS, 2 * GHEADS):
        away(at).wait()
    for g in range(2):
        for i in range(4):
            side(i, g).wait()


def attend(pair, part, a1, weights, qvb, bias, rf, rft, after):
    return run(
        functools.partial(attend_kernel, pair),
        [(part, SCALAR)] + [(a, WHOLE) for a in (a1, *weights, qvb, bias, rf, rft)],
        [
            (pinned(pltpu.HBM, 2 * GHEADS, 2, WIN, WIN, kind=LOW), FAR),
            (pinned(pltpu.HBM, 2, 2, 128, WIN, kind=LOW), FAR),
            (pinned(pltpu.HBM, 2, 2, WIN, 128, kind=LOW), FAR),
            (pinned(pltpu.HBM, 2, 2, 128, WIN, kind=LOW), FAR),
            (shaped(2, 2, WIN, 128, kind=LOW), WHOLE),
            (pinned(pltpu.HBM, 2, 2, WIN, 128), FAR),
        ],
        2, 28,
        scratch=[
            pltpu.VMEM((2, 2, WIN, 128), LOW),
            pltpu.VMEM((2, 2, 256, WIN), LOW),
            pltpu.VMEM((2, 2, WIN, 128), LOW),
            pltpu.VMEM((2, 2, WIN, WIN), F32),
            pltpu.VMEM((2, 2, WIN, 256), F32),
            pltpu.VMEM((P_SLOTS, 2, WIN, WIN), LOW),
            pltpu.SemaphoreType.DMA((P_SLOTS,)),
            pltpu.VMEM((2, 2, 128, WIN), LOW),
            pltpu.VMEM((2, 2, WIN, 128), LOW),
            pltpu.VMEM((2, 2, 128, WIN), LOW),
            pltpu.VMEM((2, 2, WIN, 128), F32),
            pltpu.SemaphoreType.DMA((4, 2)),
        ],
        after=after,
    )


def attend_back_kernel(
    at, dop_ref, nd_ref, p_ref, qt_ref, k_ref, vt_ref, a1t_ref, gp_ref,
    dw_ref, wide_ref, low_ref, cs_ref,
    dop_s, nd_s, qt_s, k_s, vt_s, a1t_s, gp_s, p_s, dopt_s, dp_s, ds_s, dq_s, dkt_s, dvt_s, db_s, sems,
):
    lane = lax.broadcasted_iota(jnp.int32, (WIN, 128), 1) // HD
    zero = jnp.zeros((WIN, 128), LOW)
    inside = lax.broadcasted_iota(jnp.int32, (8, 512), 1) < WIN
    names = ("dop", "nd", "vt", "qt", "k", "gp", "a1t")
    sources = (dop_ref.at[at], nd_ref.at[at], vt_ref.at[at], qt_ref.at[at], k_ref.at[at], gp_ref.at[at], a1t_ref)
    targets = (dop_s, nd_s, vt_s, qt_s, k_s, gp_s, a1t_s)
    copies = {
        name: pltpu.make_async_copy(source, target, sems.at[i])
        for i, (name, source, target) in enumerate(zip(names, sources, targets))
    }
    probs = [
        pltpu.make_async_copy(p_ref.at[GHEADS * at + e], p_s.at[e], sems.at[len(names) + e]) for e in range(GHEADS)
    ]
    for name in ("dop", "nd", "vt"):
        copies[name].start()
    probs[0].start()
    copies["qt"].start()
    copies["k"].start()
    for e in range(1, GHEADS):
        probs[e].start()
    copies["a1t"].start()
    copies["gp"].start()
    for name in ("dop", "nd", "vt"):
        copies[name].wait()
    for w in range(2):
        dopt_s[w] = dop_s[w].astype(F32).T.astype(LOW)
    for e in range(GHEADS):
        mine = lane == e
        own = slice(HD * e, HD * e + HD)
        slot = e % 2
        for w in range(2):
            wide = jnp.concatenate([jnp.where(mine, dop_s[w], zero), jnp.where(mine, nd_s[w], zero)], axis=1)
            v_wide = jnp.concatenate([vt_s[w], jnp.ones((128, WIN), LOW)], axis=0)
            dp_s[slot, w] = product(wide, v_wide)
        probs[e].wait()
        for w in range(2):
            dvt_s[w, own, :] = product(dopt_s[w, own, :], p_s[e, w])
        for start, count in ROW_CUTS:
            rows = slice(start, start + count)
            one = p_s[e, 0, rows, :].astype(F32) * dp_s[slot, 0, rows, :]
            two = p_s[e, 1, rows, :].astype(F32) * dp_s[slot, 1, rows, :]
            db_s[slot, rows, 0:WIN] = one + two
            ds_s[slot, 0, rows, :] = one.astype(LOW)
            ds_s[slot, 1, rows, :] = two.astype(LOW)
        if e == 0:
            copies["qt"].wait()
            copies["k"].wait()
        for w in range(2):
            dkt_s[w, own, :] = product(qt_s[w, own, :], ds_s[slot, w])
            part = product(ds_s[slot, w], jnp.where(mine, k_s[w], zero))
            dq_s[w] = part if e == 0 else dq_s[w] + part
        for hi in range(WH):
            own_rows = slice(8 * hi, 8 * hi + 8)
            wide_ref[e, own_rows, :] = jnp.zeros((8, 768), F32)
            for base in (0, 128, 256):
                total = jnp.zeros((8, 512), F32)
                for ti in range(WT):
                    lane_base, by = lanes_of(ti)
                    if lane_base != base:
                        continue
                    first_row = 49 * ti + 7 * hi
                    tile = jnp.where(inside, db_s[slot, first_row : first_row + 8, :], 0.0)
                    total += pltpu.roll(tile, by, 1) if by else tile
                wide_ref[e, own_rows, base : base + 512] += total
    copies["a1t"].wait()
    copies["gp"].wait()
    sum_q = jnp.zeros((1, 128), F32)
    sum_v = jnp.zeros((1, 128), F32)
    grad = jnp.zeros((D, 384), F32)
    for w in range(2):
        dq = dq_s[w] * SCALE
        dk = (dkt_s[w] * (1.0 / LOG2E)).T
        dv = dvt_s[w].T
        sum_q += jnp.sum(dq, axis=0, keepdims=True)
        sum_v += jnp.sum(dv, axis=0, keepdims=True)
        low = jnp.concatenate([dq, dk, dv], axis=1).astype(LOW)
        low_ref[w] = low
        grad += product(a1t_s[w], low)
    dw_ref[:, 0:384] = grad.astype(LOW)
    dw_ref[:, 384:512] = gp_s[...]
    cs_ref[0:1, :] = sum_q
    cs_ref[1:2, :] = sum_v


def attend_back(at, dop, nd, kept, a1t, gproj, after):
    p, qt, k, vt, _, _ = kept
    return run(
        functools.partial(attend_back_kernel, at),
        [(pltpu.with_memory_space_constraint(a, pltpu.HBM), FAR) for a in (dop, nd, p, qt, k, vt, a1t, gproj)],
        [
            (shaped(D, 512, kind=LOW), WHOLE),
            (shaped(GHEADS, 56, 768), WHOLE),
            (shaped(2, WIN, 384, kind=LOW), WHOLE),
            (shaped(2, 128), WHOLE),
        ],
        6, 24,
        scratch=[
            pltpu.VMEM((2, WIN, 128), LOW),
            pltpu.VMEM((2, WIN, 128), LOW),
            pltpu.VMEM((2, 128, WIN), LOW),
            pltpu.VMEM((2, WIN, 128), LOW),
            pltpu.VMEM((2, 128, WIN), LOW),
            pltpu.VMEM((2, D, WIN), LOW),
            pltpu.VMEM((D, 128), LOW),
            pltpu.VMEM((GHEADS, 2, WIN, WIN), LOW),
            pltpu.VMEM((2, 128, WIN), LOW),
            pltpu.VMEM((2, 2, WIN, WIN), F32),
            pltpu.VMEM((2, 2, WIN, WIN), LOW),
            pltpu.VMEM((2, WIN, 128), F32),
            pltpu.VMEM((2, 128, WIN), F32),
            pltpu.VMEM((2, 128, WIN), F32),
            pltpu.VMEM((2, 400, 512), F32),
            pltpu.SemaphoreType.DMA((7 + GHEADS,)),
        ],
        after=after,
    )


def gelu_parts(v):
    size = jnp.abs(v)
    t = 1.0 / (1.0 + (0.3275911 * 0.7071067811865476) * size)
    bell = jnp.exp2(v * v * (-0.5 * LOG2E))
    poly = t * (0.127414796 + t * (-0.142248368 + t * (0.7107068705 + t * (-0.7265760135 + t * 0.5307027145))))
    tail = poly * bell
    phi = jnp.where(v >= 0.0, 1.0 - tail, tail)
    return v * phi, phi + v * bell * 0.3989422804014327


def norm_back(values, dy, gain):
    vhat, rstd = normed(values)
    scaled = dy * gain
    dv = rstd * (
        scaled - jnp.mean(scaled, -1, keepdims=True) - vhat * jnp.mean(scaled * vhat, -1, keepdims=True)
    )
    return dv, jnp.sum(dy * vhat, axis=0, keepdims=True), jnp.sum(dy, axis=0, keepdims=True)


ROWS = 2 * WIN


def before_kernel(
    on_ref, of_ref, x_ref, cot_ref, tb_ref, gain_ref, u0, u1, u2, u3,
    after_ref, a2_ref, a2t_ref, g_ref, gt_ref,
):
    weight = jnp.concatenate([u[:, 0:128] for u in (u0, u1, u2, u3)], axis=1)
    lows = []
    for w in range(2):
        mixed = jnp.concatenate([on_ref[0, w], on_ref[1, w], of_ref[0, w], of_ref[1, w]], axis=1)
        after = x_ref[w] + product(mixed, weight, NT) + tb_ref[1:2, :]
        after_ref[w] = after
        vhat, _ = normed(after)
        lows.append(vhat * gain_ref[1:2, :] + tb_ref[2:3, :])
    a2 = jnp.concatenate(lows, axis=0)
    a2_ref[...] = a2.astype(LOW)
    a2t_ref[...] = a2.T.astype(LOW)
    cot = jnp.concatenate([cot_ref[0], cot_ref[1]], axis=0)
    g_ref[...] = cot.astype(LOW)
    gt_ref[...] = cot.T.astype(LOW)


def before(o_near, o_far, x, cot, biases, gains, ups):
    return run(
        before_kernel,
        [(o_near, WHOLE), (o_far, WHOLE)]
        + [(pltpu.with_memory_space_constraint(a, pltpu.HBM), held(2, WIN, D)) for a in (x, cot)]
        + [(a, WHOLE) for a in (biases, gains, *ups)],
        [
            (shaped(2, WIN, D), WHOLE), (shaped(ROWS, D, kind=LOW), WHOLE), (shaped(D, ROWS, kind=LOW), WHOLE),
            (shaped(ROWS, D, kind=LOW), WHOLE), (shaped(D, ROWS, kind=LOW), WHOLE),
        ],
        4, 20,
        grid=(1,),
    )


def feed_parts(
    first, part_ref, a2_ref, a2t_ref, g_ref, gt_ref, hb_ref, ups, own_ref, other_ref,
    out_ref, da2_ref, gup_ref, gdown_ref, ghb_ref, down_s, h_s, d_s, act_s, dh_s,
):
    count, block = own_ref.shape[1:3]
    for p in range(2):
        for z in range(count):
            for ref, place in ((own_ref, part_ref[1]), (other_ref, 1 - part_ref[1])):
                at = pl.multiple_of((2 * z + place) * block, block)
                down_s[p, pl.ds(at, block), :] = ref[p, z]
    downs = (down_s.at[0], down_s.at[1])

    def rise(p, half):
        cols = slice(256 * half, 256 * half + 256)
        h_s[p, :, cols] = product(a2_ref[...], ups[p][:, 128 + 256 * half : 384 + 256 * half])
        d_s[p, :, cols] = product(g_ref[...], downs[p][:, cols])

    def bend(p, half):
        for cut in range(256 * half, 256 * half + 256, 128):
            cols = slice(cut, cut + 128)
            line = hb_ref[(first + 2 * p) ^ part_ref[0], :, cols]
            sums = jnp.zeros((1, 128), F32)
            for start in range(0, ROWS, 112):
                rows = slice(start, start + 112)
                act, slope = gelu_parts(h_s[p, rows, cols] + line)
                act_s[p, rows, cols] = act.astype(LOW)
                grad = d_s[p, rows, cols] * slope
                sums += jnp.sum(grad, axis=0, keepdims=True)
                dh_s[p, rows, cols] = grad.astype(LOW)
            ghb_ref[p, :, cols] = sums

    def fall(p):
        for half in range(2):
            cols = slice(256 * half, 256 * half + 256)
            gup_ref[p, :, cols] = product(a2t_ref[...], dh_s[p, :, cols]).astype(LOW)
            gdown_ref[p, :, cols] = product(gt_ref[...], act_s[p, :, cols]).astype(LOW)
        out_ref[...] += product(act_s[p], downs[p][...], NT)
        da2_ref[...] += product(dh_s[p], ups[p][:, 128:640], NT)

    rise(0, 0)
    rise(0, 1)
    bend(0, 0)
    rise(1, 0)
    bend(0, 1)
    rise(1, 1)
    bend(1, 0)
    fall(0)
    bend(1, 1)
    fall(1)


def feed_odd_kernel(
    part_ref, a2_ref, a2t_ref, g_ref, gt_ref, hb_ref, ua, ub, own_ref, other_ref, after_ref, tb_ref,
    out_ref, da2_ref, gup_ref, gdown_ref, ghb_ref, *work,
):
    for w in range(2):
        out_ref[WIN * w : WIN * w + WIN, :] = after_ref[w] + tb_ref[3:4, :]
    da2_ref[...] = jnp.zeros((ROWS, D), F32)
    feed_parts(
        1, part_ref, a2_ref, a2t_ref, g_ref, gt_ref, hb_ref, (ua, ub), own_ref, other_ref,
        out_ref, da2_ref, gup_ref, gdown_ref, ghb_ref, *work,
    )


def feed_even_kernel(
    part_ref, a2_ref, a2t_ref, g_ref, gt_ref, hb_ref, ua, ub, own_ref, other_ref, after_ref,
    out_in, da2_in, on_ref, of_ref, lin_ref, lif_ref, cot_ref, gain_ref, uc, ud,
    out_ref, gup_ref, gdown_ref, ghb_ref, dafter_ref, dn_ref, df_ref, nn_ref, nf_ref, gpn_ref, gpf_ref, sums_ref,
    da2_s, *work,
):
    out_ref[...] = out_in[...]
    da2_s[...] = da2_in[...]
    feed_parts(
        0, part_ref, a2_ref, a2t_ref, g_ref, gt_ref, hb_ref, (ua, ub), own_ref, other_ref,
        out_ref, da2_s, gup_ref, gdown_ref, ghb_ref, *work,
    )
    weight = jnp.concatenate([u[:, 0:128] for u in (ua, uc, ub, ud)], axis=1)
    grad = jnp.zeros((D, D), F32)
    sums = [jnp.zeros((1, D), F32) for _ in range(4)]
    for w in range(2):
        own = slice(WIN * w, WIN * w + WIN)
        dv, dgain, doff = norm_back(after_ref[w], da2_s[own, :], gain_ref[1:2, :])
        cot = cot_ref[w]
        dafter = cot + dv
        dafter_ref[w] = dafter
        turned = dafter.T.astype(LOW)
        dmix = product(dafter.astype(LOW), weight)
        for i in range(PARTS):
            at = i % 2
            d_ref, n_ref, l_ref, m_ref = (
                (dn_ref, nn_ref, lin_ref, on_ref) if i < 2 else (df_ref, nf_ref, lif_ref, of_ref)
            )
            dop = (dmix[:, 128 * i : 128 * i + 128] * l_ref[at, w]).astype(LOW)
            d_ref[at, w] = dop
            n_ref[at, w] = (-(dop.astype(F32) * m_ref[at, w].astype(F32))).astype(LOW)
        grad += product(turned, jnp.concatenate([on_ref[0, w], on_ref[1, w], of_ref[0, w], of_ref[1, w]], axis=1))
        parts = (dgain, doff, jnp.sum(dafter, axis=0, keepdims=True), jnp.sum(cot, axis=0, keepdims=True))
        for i, part in enumerate(parts):
            sums[i] += part
    for i, (ref, at) in enumerate(((gpn_ref, 0), (gpn_ref, 1), (gpf_ref, 0), (gpf_ref, 1))):
        ref[at] = grad[:, 128 * i : 128 * i + 128].astype(LOW)
    for i in range(4):
        sums_ref[i : i + 1, :] = sums[i]


FEED_WORK = [
    pltpu.VMEM((2, 512, 512), LOW),
    pltpu.VMEM((2, ROWS, 512), F32), pltpu.VMEM((2, ROWS, 512), F32),
    pltpu.VMEM((2, ROWS, 512), LOW), pltpu.VMEM((2, ROWS, 512), LOW),
]
STEP_OUTS = [(shaped(2, D, 512, kind=LOW), WHOLE), (shaped(2, D, 512, kind=LOW), WHOLE), (shaped(2, 1, 512), WHOLE)]


def feed_odd(part, known, hb, ups, downs, after, biases):
    return run(
        feed_odd_kernel,
        [(part, SCALAR)] + [(a, WHOLE) for a in (*known, hb, *ups, *downs, after, biases)],
        [(shaped(ROWS, D), WHOLE), (shaped(ROWS, D), WHOLE), *STEP_OUTS],
        9, 28,
        scratch=FEED_WORK,
    )


def feed_even(part, known, hb, ups, downs, after, out, da2, o_near, o_far, li_near, li_far, cot, gains, others):
    return run(
        feed_even_kernel,
        [(part, SCALAR)]
        + [
            (a, WHOLE)
            for a in (
                *known, hb, *ups, *downs, after, out, da2, o_near, o_far, li_near, li_far, cot, gains, *others,
            )
        ],
        [
            (shaped(ROWS, D), WHOLE), *STEP_OUTS, (shaped(2, WIN, D), WHOLE),
            *[(pinned(pltpu.HBM, 2, 2, WIN, 128, kind=LOW), WHOLE)] * 4,
            *[(pinned(pltpu.HBM, 2, D, 128, kind=LOW), WHOLE)] * 2,
            (shaped(4, D), WHOLE),
        ],
        13, 32,
        scratch=[pltpu.VMEM((ROWS, D), F32), *FEED_WORK],
    )


def last_kernel(
    part_ref, x_ref, dafter_ref, gain_ref, l0, l1, l2, l3, w0, w1, w2, w3,
    c0, c1, c2, c3, two_ref, odd_ref, even_ref, wide_ref, p0, p1, p2, e1, e2, e3,
    gx_ref, pack_ref, spread_s, pack_s,
):
    sums = [jnp.zeros((1, D), F32) for _ in range(2)]
    for w in range(2):
        da1 = jnp.zeros((WIN, D), F32)
        for low, wt in ((l0, w0), (l1, w1), (l2, w2), (l3, w3)):
            da1 += product(low[w], wt[...], NT)
        dv, dgain, doff = norm_back(x_ref[w], da1, gain_ref[0:1, :])
        gx_ref[w] = dafter_ref[w] + dv
        sums[0] += dgain
        sums[1] += doff
    cols = slice(RELP, PACK)
    pack_s[0:1, cols] = sums[0]
    pack_s[1:2, cols] = sums[1]
    pack_s[2:6, cols] = two_ref[...]
    for group, c in enumerate((c0, c1, c2, c3)):
        own = pl.ds(pl.multiple_of(RELP + (part_ref[0] ^ group) * 128, 128), 128)
        pack_s[6:8, own] = c[...]
    for i in range(PARTS):
        pack_s[pl.ds(8 + (part_ref[0] ^ i), 1), cols] = (odd_ref if i % 2 else even_ref)[i // 2]
    pack_s[12:16, cols] = jnp.zeros((4, D), F32)
    for group, rows in enumerate((e1, e2, e3)):
        for h in range(GHEADS):
            pack_s[pl.ds((part_ref[0] ^ (group + 1)) * GHEADS + h, 1), 0:RELP] = rows[h : h + 1, :]
    shrunk(wide_ref, (p0, p1, p2), spread_s, pack_s, part_ref[0] * GHEADS)
    pack_ref[...] = pack_s[...].astype(LOW)


def swap(values, axis, distance):
    count = lax.axis_size(axis)
    return lax.ppermute(values, axis, [(i, i ^ distance) for i in range(count)])


def bits_of(axis):
    return (lax.axis_size(axis) - 1).bit_length()


def interleaved(own, other, upper):
    place = jnp.arange(2, dtype=jnp.int32).reshape(1, 2, *(1,) * (own.ndim - 1))
    mine = place == upper.astype(jnp.int32)
    return jnp.where(mine, own[:, None], other[:, None]).reshape(-1, *own.shape[1:])


def upper_of(axis, bit):
    return (lax.axis_index(axis) >> bit) % 2 == 1


def gathered(blocks, bits):
    for bit in bits:
        blocks = interleaved(blocks, swap(blocks, "dp", 1 << bit), upper_of("dp", bit))
    return blocks


def flat(blocks):
    return blocks.reshape(-1, blocks.shape[-1])


def half(total, bit, mine):
    pairs = total.reshape(-1, 2, *total.shape[1:])
    return jnp.where(upper_of("dp", bit) == mine, pairs[:, 1], pairs[:, 0])


def halves(total, bit):
    return half(total, bit, False).astype(LOW), half(total, bit, True).astype(F32)


def plus(one, two):
    return one.astype(F32) + two.astype(F32)


def offset_order(rel_index):
    corners = rel_index.reshape(WT, WH, WW, WIN)[::7, ::6, ::6].reshape(2, 2, 2, WT, WH, WW)
    joined = jnp.concatenate([corners[1], corners[0][:, :, 1:]], axis=2)
    joined = jnp.concatenate([joined[1], joined[0][:, :, 1:]], axis=2)
    joined = jnp.concatenate([joined[1], joined[0][:, :, 1:]], axis=2)
    return jnp.pad(joined.reshape(1, REL), ((0, 0), (0, RELP - REL)), constant_values=-1)


def body(
    inputs,
    w_qkv,
    qv_bias,
    w_proj,
    w_fc1,
    fc1_bias,
    w_fc2,
    norm_gains,
    token_biases,
    table,
    shifts,
    rel_index,
    cotangent,
):
    index = lax.axis_index("mp")
    part = index.astype(jnp.int32).reshape(1)
    rows = w_qkv.shape[1]
    x = inputs.reshape(2, WIN, D)
    cot = cotangent.reshape(2, WIN, D)
    high_bits = tuple(reversed(range(1, bits_of("dp"))))
    low_bits = tuple(range(1, bits_of("dp")))

    shard_qkv = w_qkv.transpose(1, 0, 2).reshape(1, rows, 384).astype(LOW)
    (shard_rest,) = run(
        rest_kernel,
        [(a, WHOLE) for a in (w_proj.T, w_fc1, w_fc2.T)],
        [(shaped(rows, 1152, kind=LOW), WHOLE)],
        1, 8,
    )
    shard_rest = shard_rest[None]
    qkv_first = gathered(shard_qkv, high_bits[:1])
    qkv_high = gathered(qkv_first, high_bits[1:])
    own = flat(gathered(qkv_high, (0,)))
    qkv_parts = [own, swap(own, "mp", 1)]
    across = swap(own, "mp", 2)
    rest = gathered(shard_rest, high_bits)
    (up_own,) = lax.optimization_barrier((gathered(rest[:, :, :640], (0,)),))
    up_across = swap(up_own, "mp", 2)
    down_across = swap(rest[:, :, 640:], "mp", 2)
    places = jnp.arange(WIN, dtype=jnp.int32)
    places = jnp.stack([places // (WH * WW), places // WW % WH, places % WW])
    order = offset_order(once(rel_index, qkv_first))
    column = jnp.arange(768, dtype=jnp.int32)
    lane_row = jnp.where(
        column < 15 * 49, column // 49 * 169 + column % 49 // 7 * 13 + column % 7, -1
    )
    a1, a1t, rf, rft = run(
        first_norm_kernel,
        [(part, SCALAR), (shifts, SCALAR)] + [(a, WHOLE) for a in (x, norm_gains, token_biases, places)],
        [
            (shaped(2, WIN, D, kind=LOW), WHOLE), (pinned(pltpu.HBM, 2, D, WIN, kind=LOW), WHOLE),
            (shaped(2, WIN, 128, kind=LOW), WHOLE), (shaped(2, 128, WIN, kind=LOW), WHOLE),
        ],
        2, 16,
        after=(qkv_first,),
    )
    row_offsets, *picks = run(
        rows_from_table_kernel,
        [(a, WHOLE) for a in (order, table.T, lane_row.reshape(1, 768), lane_row.reshape(768, 1))],
        [(shaped(HEADS, RELP), WHOLE)]
        + [(shaped(high - low, 256, kind=LOW), WHOLE) for low, high in LANE_CUTS]
        + [(shaped(256, high - low, kind=LOW), WHOLE) for low, high in LANE_CUTS],
        4, 20,
        after=(qkv_high,),
    )
    out_picks, back_picks = picks[:3], picks[3:]
    near_bias = expand_bias(0, part, row_offsets, out_picks, (qkv_high,))
    near = attend(0, part, a1, qkv_parts[:2], qv_bias, near_bias, rf, rft, (rest,))
    across = once(across, near[4])
    qkv_parts += [across, swap(across, "mp", 1)]
    far_bias = expand_bias(1, part, row_offsets, out_picks, (near[4], up_own))
    down_pair = jnp.stack([rest[:, :, 640:], once(down_across, far_bias)], axis=0)
    down_other = swap(down_pair, "dp", 1)
    far = attend(1, part, a1, qkv_parts[2:], qv_bias, far_bias, rf, rft, (up_own, down_pair))
    up_parts = [flat(up_own), flat(swap(up_own, "mp", 1)), flat(up_across), flat(swap(once(up_across, far[4]), "mp", 1))]
    hb = fc1_bias.reshape(PARTS, 1, 512)
    after, *known = before(near[4], far[4], x, cot, token_biases, norm_gains, up_parts)
    down_other = once(down_other, far[4])
    upper = upper_of("dp", 0).astype(jnp.int32).reshape(1)
    if rows % 16:
        joined = jnp.stack([flat(interleaved(down_pair[i], down_other[i], upper_of("dp", 0))) for i in range(2)])
        joined = joined.reshape(2, 2, 1, D // 2, 512)
        down_pair, down_other, upper = joined[:, 0], joined[:, 1], jnp.zeros((1,), jnp.int32)
    places_of = jnp.concatenate([part, upper])
    down_even = (down_pair, down_other)
    down_odd = [swap(a, "mp", 1) for a in down_even]
    out, da2, odd_up, odd_down, hb_odd = feed_odd(
        places_of, known, hb, up_parts[1::2], down_odd, after, token_biases
    )
    out, even_up, even_down, hb_even, dafter, dop_near, dop_far, nd_near, nd_far, gp_near, gp_far, sums_two = feed_even(
        places_of, known, hb, up_parts[::2], down_even, after, out, da2,
        near[4], far[4], near[5], far[5], cot, norm_gains, up_parts[1::2],
    )
    got_up = swap(odd_up, "mp", 1).reshape(2, -1, rows, 512)
    got_down = swap(odd_down, "mp", 1).reshape(2, -1, rows, 512)
    even_up = even_up.reshape(2, -1, rows, 512)
    even_down = even_down.reshape(2, -1, rows, 512)
    up_send = plus(even_up[1], got_up[1]).astype(LOW)
    turned = [a.transpose(1, 0, 2, 3) for a in (even_down, got_down)]
    down_send = plus(*(half(a, 0, False) for a in turned)).astype(LOW)
    three, wide3, low3, col3 = attend_back(1, dop_far, nd_far, far, a1t, gp_far, (up_send, down_send))
    two, wide2, low2, col2 = attend_back(0, dop_far, nd_far, far, a1t, gp_far, (three,))
    up_sum = plus(plus(even_up[0], got_up[0]), swap(up_send, "mp", 2))
    down_sum = plus(plus(*(half(a, 0, True) for a in turned)), swap(down_send, "dp", 1))
    far_sum = plus(two, swap(three, "mp", 1)).astype(LOW)
    up_send, up_keep = halves(up_sum, 0)
    down_send, down_keep = down_sum[:, 1].astype(LOW), down_sum[:, 0]
    one, wide1, low1, col1 = attend_back(
        1, dop_near, nd_near, near, a1t, gp_near, (far_sum, up_send, down_send)
    )
    far_sum = swap(far_sum, "mp", 2)
    up_sum = plus(up_keep, swap(up_send, "dp", 1))
    down_sum = plus(down_keep, swap(down_send, "mp", 2))
    summed = jnp.stack([up_sum, down_sum], axis=1)
    top = bits_of("dp") - 1
    is_top = upper_of("dp", top)
    ends = summed.reshape(2, -1, 2, rows, 512)
    mlp_send = jnp.where(is_top, ends[0], ends[1]).astype(LOW)
    mlp_keep = jnp.where(is_top, ends[1], ends[0])
    zero, wide0, low0, col0 = attend_back(0, dop_near, nd_near, near, a1t, gp_near, (mlp_send, one))
    summed = plus(mlp_keep, swap(mlp_send, "dp", 1 << top))
    total = plus(plus(zero, swap(one, "mp", 1)), far_sum).reshape(-1, rows, 512)
    rows_by = [shrink_bias(w, back_picks, ()) for w in (wide1, wide2, wide3)]
    send, keep = halves(total, 0)
    grad_x, pack = run(
        last_kernel,
        [(part, SCALAR)]
        + [
            (a, WHOLE)
            for a in (
                x, dafter, norm_gains, low0, low1, low2, low3, *qkv_parts, col0, col1, col2, col3,
                sums_two, hb_odd, hb_even, wide0, *back_picks, *rows_by,
            )
        ],
        [(shaped(2, WIN, D), WHOLE), (shaped(HEADS, PACK, kind=LOW), WHOLE)],
        4, 20,
        scratch=[pltpu.VMEM((GHEADS, 56, RELP), F32), pltpu.VMEM((HEADS, PACK), F32)],
        after=(send,),
    )
    total = plus(keep, swap(send, "dp", 1))
    mp_steps = [("mp", 1 << bit) for bit in range(bits_of("mp"))]
    steps = mp_steps + [("dp", 1 << bit) for bit in range(bits_of("dp"))]
    queue = list(low_bits)
    pending = None

    def settled(bit, keep, got):
        if bit == top:
            return plus(keep[0], got), keep[1]
        count = keep[0].shape[0]
        mlp_got = got[count:].reshape(keep[1].shape)
        return plus(keep[0], got[:count]), plus(keep[1], mlp_got)

    def parted(bit, total, summed):
        send, keep = halves(total, bit)
        if bit == top:
            return send, (keep, summed)
        mlp_send, mlp_keep = halves(summed, bit)
        return jnp.concatenate([send, mlp_send.reshape(-1, rows, 512)], axis=0), (keep, mlp_keep)

    for place, (axis, distance) in enumerate(steps):
        mine = pack.astype(LOW)
        theirs = swap(mine, axis, distance)
        if pending is not None:
            bit, keep, got = pending
            total, summed = settled(bit, keep, once(got, mine))
            pending = None
        if place >= 1 and queue:
            bit = queue.pop(0)
            send, keep = parted(bit, once(total, mine), summed)
            theirs = once(theirs, send)
            pending = (bit, keep, swap(send, "dp", 1 << bit))
        pack = plus(mine, theirs)
    if pending is not None:
        total, summed = settled(*pending)
    for bit in queue:
        send, keep = parted(bit, total, summed)
        total, summed = settled(bit, keep, swap(send, "dp", 1 << bit))
    own_qkv, own_mlp = total.reshape(rows, 512), summed.reshape(2, rows, 512)
    grad_qkv, grad_proj = run(
        unpack_qkv_kernel,
        [(own_qkv, WHOLE)],
        [(pinned(pltpu.HBM, *dims), held(*dims)) for dims in ((3, rows, 128), (rows, 128))],
        1, 8,
        grid=(1,),
    )
    grad_up, grad_down = run(
        unpack_mlp_kernel,
        [(own_mlp, WHOLE)],
        [(pinned(pltpu.HBM, rows, 512), held(rows, 512))] * 2,
        1, 8,
        grid=(1,),
    )
    grad_table, grad_gains, grad_biases, grad_pair, grad_hidden = run(
        rows_to_table_kernel,
        [(once(order, grad_qkv, grad_proj, grad_up, grad_down), WHOLE), (pack, WHOLE)],
        [(shaped(*dims), WHOLE) for dims in ((HEADS, REL), (2, D), (4, D), (2, D), (4, D))],
        4, 20,
    )
    return (
        out.reshape(inputs.shape),
        grad_x.reshape(inputs.shape),
        grad_qkv,
        grad_pair,
        grad_proj.T,
        grad_up,
        grad_hidden.reshape(FF),
        grad_down.T,
        grad_gains,
        grad_biases,
        grad_table.T,
    )


def solution(mesh):
    placed = (
        P(("dp", "mp"), None),
        P(None, "dp", "mp"),
        P(),
        P("mp", "dp"),
        P("dp", "mp"),
        P(),
        P("mp", "dp"),
        P(),
        P(),
        P(),
        P("dp", None),
        P(),
        P(("dp", "mp"), None),
    )
    return jax.shard_map(
        body,
        mesh=mesh,
        in_specs=placed,
        out_specs=(
            P(("dp", "mp"), None),
            P(("dp", "mp"), None),
            P(None, "dp", "mp"),
            P(),
            P("mp", "dp"),
            P("dp", "mp"),
            P(),
            P("mp", "dp"),
            P(),
            P(),
            P(),
        ),
        check_vma=False,
    )
```
